32 devices in a mesh: section: 2 (over x), seq: 4 (over y, core), tp: 4 (over z).
Axes of the slice: x: 2, y: 2, z: 4, core: 2. Of those that a mesh axis runs over, the one named last changes fastest.
Arguments:
- inputs: bfloat16 [4, 1024, 2048], P(None, ('seq', 'tp')), may hold values from -6 to 6
- cotangent: bfloat16 [4, 1024, 2048], P(None, 'seq'), may hold values from -6 to 6
- doc_start: int32 [4, 1024], P(None, 'seq'), may hold values from 0 to 4095, as said below
- norm_in: float32 [2, 2048], P('section'), may hold values from 0.5 to 1.5
- query_weight: bfloat16 [2, 2048, 1024], P('section', None, 'tp'), may hold values from -0.125 to 0.125
- key_weight: bfloat16 [2, 2048, 1024], P('section', None, 'tp'), may hold values from -0.125 to 0.125
- value_weight: bfloat16 [2, 2048, 2048], P('section', None, 'tp'), may hold values from -0.125 to 0.125
- outgate_weight: bfloat16 [2, 2048, 2048], P('section', None, 'tp'), may hold values from -0.125 to 0.125
- decay_weight: bfloat16 [2, 2048, 8], P('section', None, 'tp'), may hold values from -0.125 to 0.125
- beta_weight: bfloat16 [2, 2048, 8], P('section', None, 'tp'), may hold values from -0.125 to 0.125
- conv_query: float32 [2, 4, 1024], P('section', None, 'tp'), may hold values from -0.6 to 0.6
- conv_key: float32 [2, 4, 1024], P('section', None, 'tp'), may hold values from -0.6 to 0.6
- conv_value: float32 [2, 4, 2048], P('section', None, 'tp'), may hold values from -0.6 to 0.6
- decay_log: float32 [2, 8], P('section', 'tp'), may hold values from -7 to -3
- decay_bias: float32 [2, 8], P('section', 'tp'), may hold values from -2 to 1
- head_norm: float32 [2, 256], P('section'), may hold values from 0.5 to 1.5
- out_weight: bfloat16 [2, 2048, 2048], P('section', 'tp'), may hold values from -0.125 to 0.125
- norm_feed: float32 [2, 2048], P('section'), may hold values from 0.5 to 1.5
- gate_weight: bfloat16 [2, 2048, 5632], P('section', None, 'tp'), may hold values from -0.125 to 0.125
- up_weight: bfloat16 [2, 2048, 5632], P('section', None, 'tp'), may hold values from -0.125 to 0.125
- down_weight: bfloat16 [2, 5632, 2048], P('section', 'tp'), may hold values from -0.078125 to 0.078125
Outputs:
- section_out: float32 [2, 4, 1024, 2048], P('section', None, ('seq', 'tp'))
- section_in_grad: float32 [2, 4, 1024, 2048], P('section', None, ('seq', 'tp'))
- grad_norm_in: float32 [2, 2048], P('section')
- grad_query: float32 [2, 2048, 1024], P('section', 'seq', 'tp')
- grad_key: float32 [2, 2048, 1024], P('section', 'seq', 'tp')
- grad_value: float32 [2, 2048, 2048], P('section', 'seq', 'tp')
- grad_outgate: float32 [2, 2048, 2048], P('section', 'seq', 'tp')
- grad_decay: float32 [2, 2048, 8], P('section', 'seq', 'tp')
- grad_beta: float32 [2, 2048, 8], P('section', 'seq', 'tp')
- grad_conv_query: float32 [2, 4, 1024], P('section', None, 'tp')
- grad_conv_key: float32 [2, 4, 1024], P('section', None, 'tp')
- grad_conv_value: float32 [2, 4, 2048], P('section', None, 'tp')
- grad_decay_log: float32 [2, 8], P('section', 'tp')
- grad_decay_bias: float32 [2, 8], P('section', 'tp')
- grad_head_norm: float32 [2, 256], P('section')
- grad_out: float32 [2, 2048, 2048], P('section', 'tp', 'seq')
- grad_norm_feed: float32 [2, 2048], P('section')
- grad_gate: float32 [2, 2048, 5632], P('section', 'seq', 'tp')
- grad_up: float32 [2, 2048, 5632], P('section', 'seq', 'tp')
- grad_down: float32 [2, 5632, 2048], P('section', 'tp', 'seq')
The draws below stay inside these ranges and needn't reach their ends.
Inputs may be any that keep to these rules, and one draw needn't show every extreme that they name: `doc_start`: each entry is the position where its token's document starts: entries never fall along the positions, none exceeds its own position, an entry equals its own position wherever it differs from the entry before it; position 0 and the last position each start a document.
All inputs are finite; a program needn't handle non-finite values.
Results may differ from the reference program's by a relative error of at most 0.039.
Values sent between devices are 32-bit elements; how exact they have to be, the bound alone decides.
No kernel may reach another device: no remote copies, remote signals or barrier semaphores. Data moves between devices by JAX's collectives and lax.ppermute only.
A program may use at most 384 MiB of HBM per device.

```python
import jax
import jax.numpy as jnp
from jax import lax

D = 2048
HEADS = 8
DK = 128
DV = 256
FF = 5632
CONV = 4
BLOCK = 64
MICRO = 4
MB = 1024


def draw_doc_start(key, part):
    key = jax.random.fold_in(key, 11)
    flag_key, pick_key = jax.random.split(key)
    total_rows = MICRO * MB
    places = jnp.arange(total_rows, dtype=jnp.int32)
    starting = jax.random.randint(flag_key, (total_rows,), 0, max(MB // 2, 2)) == 0
    chosen = jax.random.randint(pick_key, (), 0, MICRO)
    begin = chosen * MB
    inside = (places > begin) & (places < begin + MB)
    starting = starting & jnp.logical_not(inside) | (places == begin) | (places == 0) | (places == total_rows - 1)
    marked = jnp.where(starting, places, 0)
    return lax.cummax(marked).reshape(MICRO, MB)


def block_scale(key, shape, shards, low, largest):
    loudness = 1.0
    for axis_at, shards_of in shards:
        heights = jax.random.uniform(jax.random.fold_in(jax.random.fold_in(key, 6), axis_at), (shards_of,), jnp.float32, low / len(shards), largest / len(shards))
        loudness = loudness * jnp.repeat(jnp.exp(heights), shape[axis_at] // shards_of).reshape((-1,) + (1,) * (len(shape) - 1 - axis_at))
    return loudness


def noise(stream_key, dims, deviation, most, pieces=(), held_as=jnp.bfloat16):
    array = deviation * jax.random.normal(stream_key, dims, jnp.float32)
    if pieces:
        array = array * block_scale(stream_key, dims, pieces, -0.22, 0.18)
    return jnp.clip(array, -most, most).astype(held_as)


def setup_inputs(seed: int = 0) -> dict:
    splits = jax.random.split(jax.random.key(seed), 22)
    return {
        "inputs": noise(splits[0], (MICRO, MB, D), 1.0, 6.0, ((1, 16),)),
        "cotangent": noise(splits[1], (MICRO, MB, D), 1.0, 6.0, ((1, 4),)),
        "doc_start": draw_doc_start(jax.random.fold_in(splits[21], 71), 0),
        "norm_in": jnp.clip(1.0 + 0.1 * jax.random.normal(splits[3], (2, D), jnp.float32), 0.5, 1.5),
        "query_weight": noise(splits[4], (2, D, HEADS * DK), D ** -0.5, 0.125, ((0, 2), (2, 4))),
        "key_weight": noise(splits[5], (2, D, HEADS * DK), D ** -0.5, 0.125, ((0, 2), (2, 4))),
        "value_weight": noise(splits[6], (2, D, HEADS * DV), D ** -0.5, 0.125, ((0, 2), (2, 4))),
        "outgate_weight": noise(splits[7], (2, D, HEADS * DV), D ** -0.5, 0.125, ((0, 2), (2, 4))),
        "decay_weight": noise(splits[8], (2, D, HEADS), D ** -0.5, 0.125, ((0, 2), (2, 4))),
        "beta_weight": noise(splits[9], (2, D, HEADS), D ** -0.5, 0.125, ((0, 2), (2, 4))),
        "conv_query": jnp.clip(jax.random.uniform(splits[10], (2, CONV, HEADS * DK), jnp.float32, -0.6, 0.6) * block_scale(splits[10], (2, CONV, HEADS * DK), ((0, 2), (2, 4)), -0.4, 0.0), -0.6, 0.6),
        "conv_key": jnp.clip(jax.random.uniform(splits[11], (2, CONV, HEADS * DK), jnp.float32, -0.6, 0.6) * block_scale(splits[11], (2, CONV, HEADS * DK), ((0, 2), (2, 4)), -0.4, 0.0), -0.6, 0.6),
        "conv_value": jnp.clip(jax.random.uniform(splits[12], (2, CONV, HEADS * DV), jnp.float32, -0.6, 0.6) * block_scale(splits[12], (2, CONV, HEADS * DV), ((0, 2), (2, 4)), -0.4, 0.0), -0.6, 0.6),
        "decay_log": jnp.clip(-7.0 + 4.0 * jax.random.uniform(splits[13], (2, HEADS), jnp.float32) ** block_scale(splits[13], (2, HEADS), ((0, 2), (1, 4)), -0.2, 0.2), -7.0, -3.0),
        "decay_bias": jnp.clip(-2.0 + 3.0 * jax.random.uniform(splits[14], (2, HEADS), jnp.float32) ** block_scale(splits[14], (2, HEADS), ((0, 2), (1, 4)), -0.2, 0.2), -2.0, 1.0),
        "head_norm": jnp.clip(1.0 + 0.1 * jax.random.normal(splits[15], (2, DV), jnp.float32), 0.5, 1.5),
        "out_weight": noise(splits[16], (2, HEADS * DV, D), (HEADS * DV) ** -0.5, 0.125, ((0, 2), (1, 4))),
        "norm_feed": jnp.clip(1.0 + 0.1 * jax.random.normal(splits[17], (2, D), jnp.float32), 0.5, 1.5),
        "gate_weight": noise(splits[18], (2, D, FF), D ** -0.5, 0.125, ((0, 2), (2, 4))),
        "up_weight": noise(splits[19], (2, D, FF), D ** -0.5, 0.125, ((0, 2), (2, 4))),
        "down_weight": noise(splits[20], (2, FF, D), FF ** -0.5, 0.078125, ((0, 2), (1, 4))),
    }


EPSILON = 1e-06
TOP_PRECISION = lax.Precision.HIGHEST

@jax.custom_vjp
def low(v):
    return lax.optimization_barrier(v.astype(jnp.bfloat16)).astype(jnp.float32)

@jax.custom_vjp
def low_back(v):
    return v

def low_keep(v):
    return (low(v), None)

def low_pass(kept, grad):
    return (grad,)

def back_keep(v):
    return (v, None)

def back_low(kept, grad):
    return (low(grad),)
low.defvjp(low_keep, low_pass)
low_back.defvjp(back_keep, back_low)

def row_norm(values, gain_vector):
    return values * lax.rsqrt(lax.optimization_barrier(jnp.mean(values * values, -1, keepdims=True)) + EPSILON) * gain_vector

def matmul_high(first_matrix, second_matrix):
    return jnp.matmul(first_matrix, second_matrix, precision=TOP_PRECISION)

def causal_conv(values, taps):
    width = taps.shape[0]
    padded = jnp.concatenate([jnp.zeros((width - 1, values.shape[1]), jnp.float32), values], 0)
    summed = jnp.zeros_like(values)
    for offset in range(width):
        summed = summed + taps[offset] * padded[offset:offset + values.shape[0]]
    return summed

def unit_heads(values, head_size):
    shaped = values.reshape(values.shape[0], -1, head_size)
    return shaped * lax.rsqrt(lax.optimization_barrier(jnp.sum(shaped * shaped, -1, keepdims=True)) + EPSILON)

def delta_block(state_now, block_items):

    def token_step(carried_state, token_items):
        current_query, current_key, value_now, decay_now, beta_now = token_items
        projected_rows = jnp.einsum('al,alx->ax', current_key, carried_state, precision=TOP_PRECISION)
        carried_state = decay_now[:, None, None] * (carried_state - beta_now[:, None, None] * current_key[:, :, None] * projected_rows[:, None, :]) + beta_now[:, None, None] * current_key[:, :, None] * value_now[:, None, :]
        return (carried_state, jnp.einsum('al,alx->ax', current_query, carried_state, precision=TOP_PRECISION))
    return lax.scan(token_step, state_now, block_items)

def layer_forward(tokens, resets, params):
    norm_in, query_weight, key_weight, value_weight, outgate_weight, decay_weight, beta_weight, conv_query, conv_key, conv_value, decay_log, decay_bias, head_norm, out_weight, norm_feed, gate_weight, up_weight, down_weight = params
    row_count = tokens.shape[0]
    hidden = low(row_norm(tokens, norm_in))
    proj_query = low_back(matmul_high(hidden, query_weight))
    proj_key = low_back(matmul_high(hidden, key_weight))
    proj_value = low_back(matmul_high(hidden, value_weight))
    proj_outgate = low_back(matmul_high(hidden, outgate_weight))
    proj_decay = low_back(matmul_high(hidden, decay_weight))
    proj_beta = low_back(matmul_high(hidden, beta_weight))
    query_rows = unit_heads(jax.nn.silu(causal_conv(proj_query, conv_query)), DK) * DK ** (-0.5)
    key_rows = unit_heads(jax.nn.silu(causal_conv(proj_key, conv_key)), DK)
    value_rows = jax.nn.silu(causal_conv(proj_value, conv_value)).reshape(row_count, HEADS, DV)
    decay_gate = (1.0 - resets)[:, None] * jnp.exp(-jnp.exp(decay_log) * jax.nn.softplus(proj_decay + decay_bias))
    beta_gate = jax.nn.sigmoid(proj_beta)
    blocks = row_count // BLOCK

    def split_blocks(tensor_in):
        return tensor_in.reshape((blocks, BLOCK) + tensor_in.shape[1:])
    initial = jnp.zeros((HEADS, DK, DV), jnp.float32)
    _, output_rows = lax.scan(jax.checkpoint(delta_block), initial, (split_blocks(query_rows), split_blocks(key_rows), split_blocks(value_rows), split_blocks(decay_gate), split_blocks(beta_gate)))
    output_rows = output_rows.reshape(row_count, HEADS, DV)
    normed = output_rows * lax.rsqrt(lax.optimization_barrier(jnp.mean(output_rows * output_rows, -1, keepdims=True)) + EPSILON) * head_norm
    gated = low((normed * jax.nn.silu(proj_outgate.reshape(row_count, HEADS, DV))).reshape(row_count, HEADS * DV))
    mixed = tokens + low_back(matmul_high(gated, out_weight))
    hidden_feed = low(row_norm(mixed, norm_feed))
    gate_act = low_back(matmul_high(hidden_feed, gate_weight))
    up_act = low_back(matmul_high(hidden_feed, up_weight))
    inner_act = low(jax.nn.silu(gate_act) * up_act)
    return mixed + low_back(matmul_high(inner_act, down_weight))

def reference(inputs, cotangent, doc_start, norm_in, query_weight, key_weight, value_weight, outgate_weight, decay_weight, beta_weight, conv_query, conv_key, conv_value, decay_log, decay_bias, head_norm, out_weight, norm_feed, gate_weight, up_weight, down_weight):
    weights = (norm_in, query_weight, key_weight, value_weight, outgate_weight, decay_weight, beta_weight, conv_query, conv_key, conv_value, decay_log, decay_bias, head_norm, out_weight, norm_feed, gate_weight, up_weight, down_weight)
    places = jnp.arange(MICRO * MB, dtype=jnp.int32)
    resets = (doc_start.reshape(-1).astype(jnp.int32) == places).astype(jnp.float32)
    tokens = inputs.reshape(MICRO * MB, D).astype(jnp.float32)

    def run_layer(layer_input, params):
        return layer_forward(layer_input, resets, params)
    first_params = tuple((weight[0].astype(jnp.float32) for weight in weights))
    second_params = tuple((weight[1].astype(jnp.float32) for weight in weights))
    first_out, first_back = jax.vjp(run_layer, tokens, first_params)
    second_out, second_back = jax.vjp(run_layer, first_out, second_params)
    middle_grad, second_grads = second_back(cotangent.reshape(MICRO * MB, D).astype(jnp.float32))
    input_grad, first_grads = first_back(middle_grad)
    gradients = [jnp.stack([first_grad, second_grad]) for first_grad, second_grad in zip(first_grads, second_grads)]
    layout = (2, MICRO, MB, D)
    return (jnp.stack([first_out, second_out]).reshape(layout), jnp.stack([input_grad, middle_grad]).reshape(layout), gradients[0], gradients[1], gradients[2], gradients[3], gradients[4], gradients[5], gradients[6], gradients[7], gradients[8], gradients[9], gradients[10], gradients[11], gradients[12], gradients[13], gradients[14], gradients[15], gradients[16], gradients[17])
```

```python
from functools import partial

import jax
import jax.numpy as jnp
from jax import lax
from jax.experimental import pallas as pl
from jax.experimental.pallas import tpu as pltpu
from jax.sharding import PartitionSpec as P

EPSILON = 1e-06
F32 = jnp.float32
LOW = jnp.bfloat16
VMEM_BYTES = 48 * 1024 * 1024


def full_dot(a, b, contract=((1,), (0,))):
    return lax.dot_general(
        a, b, (contract, ((), ())), precision=lax.Precision.HIGHEST, preferred_element_type=F32
    )


def low_dot(a, b, contract=((1,), (0,))):
    return lax.dot_general(a, b, (contract, ((), ())), preferred_element_type=F32)


NN = ((1,), (0,))
NT = ((1,), (1,))
TN = ((0,), (0,))


def sigmoid(x):
    return 1.0 / (1.0 + jnp.exp(-x))


def places(size):
    return (
        lax.broadcasted_iota(jnp.int32, (size, size), 0),
        lax.broadcasted_iota(jnp.int32, (size, size), 1),
    )


def unit_lower_inverse(strict_part, rows, cols):
    size = strict_part.shape[0]
    inner = jnp.where((rows >> 3) == (cols >> 3), strict_part, 0.0)
    second = full_dot(inner, inner)
    fourth = full_dot(second, second)
    inverse = jnp.where(rows == cols, 1.0, 0.0) - inner
    inverse = inverse + full_dot(inverse, second)
    inverse = inverse + full_dot(inverse, fourth)
    level = 3
    while (1 << level) < size:
        joined = ((rows >> (level + 1)) == (cols >> (level + 1))) & ((rows >> level) != (cols >> level))
        inverse = inverse - full_dot(inverse, full_dot(jnp.where(joined, strict_part, 0.0), inverse))
        level += 1
    return inverse


def with_border(border, values):
    return jnp.concatenate([border, values], 0)


def taps_back(padded, steps):
    rolled = padded if steps == 0 else pltpu.roll(padded, steps, 0)
    return rolled[8:]


def conv_sum(padded, taps):
    count = taps.shape[0]
    total = taps[0:1] * taps_back(padded, count - 1)
    for member in range(1, count):
        total = total + taps[member : member + 1] * taps_back(padded, count - 1 - member)
    return total


def conv_transposed(grad, taps):
    count = taps.shape[0]
    padded = jnp.concatenate([jnp.zeros((8, grad.shape[1]), F32), grad], 0)
    size = padded.shape[0]
    total = taps[count - 1 : count] * padded
    for member in range(count - 1):
        total = total + taps[member : member + 1] * pltpu.roll(padded, size - (count - 1 - member), 0)
    return total


def conv_taps_grad(padded, grad, count):
    return jnp.concatenate(
        [
            jnp.sum(grad * taps_back(padded, count - 1 - member), 0, keepdims=True)
            for member in range(count)
        ],
        0,
    )


def pick_lane(values, lane):
    lanes = lax.broadcasted_iota(jnp.int32, values.shape, 1)
    return jnp.sum(jnp.where(lanes == lane, values, 0.0), 1, keepdims=True)


def softplus(x):
    return jnp.maximum(x, 0.0) + jnp.log(1.0 + jnp.exp(-jnp.abs(x)))


def token_gates(side, resets, head, heads, rate, bias):
    size = side.shape[0]
    rows, cols = places(size)
    shifted = pick_lane(side, head) + bias
    log_decay = -rate * softplus(shifted)
    beta = sigmoid(pick_lane(side, heads + head))
    lanes = lax.broadcasted_iota(jnp.int32, (size, 128), 1)
    pair = jnp.where(lanes == 0, log_decay, jnp.where(lanes == 1, resets, 0.0))
    lower = jnp.where(rows >= cols, 1.0, 0.0)
    as_columns = full_dot(lower, pair)
    as_rows = full_dot(pair, lower, ((0,), (1,)))
    total, count = as_columns[:, 0:1], as_columns[:, 1:2]
    linked = (jnp.abs(count - as_rows[1:2, :]) < 0.5) & (rows >= cols)
    decays = jnp.where(linked, jnp.exp(jnp.minimum(total - as_rows[0:1, :], 0.0)), 0.0)
    last_total, last_count = total[size - 1 : size], count[size - 1 : size]
    head_decay = jnp.where(count < 0.5, jnp.exp(total), 0.0)
    tail_decay = jnp.where(
        jnp.abs(count - last_count) < 0.5, jnp.exp(jnp.minimum(last_total - total, 0.0)), 0.0
    )
    return shifted, log_decay, beta, decays, head_decay, tail_decay, rows, cols, lower


def silu_unit(summed, scale):
    gate = sigmoid(summed)
    act = summed * gate
    inverse = lax.rsqrt(jnp.sum(act * act, 1, keepdims=True) + EPSILON)
    return act, gate, inverse, act * (inverse * scale)


def silu_unit_back(grad, summed, gate, act, inverse, scale):
    unit = act * inverse
    grad = grad * scale
    act_grad = inverse * (grad - unit * jnp.sum(grad * unit, 1, keepdims=True))
    return act_grad * gate * (1.0 + summed * (1.0 - gate))


def local_kernel(
    heads, query_ref, key_ref, value_ref, side_ref, resets_ref, border_q, border_k, border_v,
    taps_q, taps_k, taps_v, rate_ref, bias_ref, carried_ref, local_ref, map_ref, inverse_ref,
):
    head = pl.program_id(0)
    key_size = query_ref.shape[1]
    _, _, beta, decays, head_decay, tail_decay, rows, cols, _ = token_gates(
        side_ref[...], resets_ref[:, 0:1], head, heads, rate_ref[head], bias_ref[head]
    )
    query = silu_unit(conv_sum(with_border(border_q[...], query_ref[...]), taps_q[...]), key_size**-0.5)[3]
    key = silu_unit(conv_sum(with_border(border_k[...], key_ref[...]), taps_k[...]), 1.0)[3]
    summed = conv_sum(with_border(border_v[...], value_ref[...]), taps_v[...])
    value = summed * sigmoid(summed)
    gram = full_dot(key, key, NT)
    mixing = beta * jnp.where(rows > cols, decays * gram, 0.0)
    inverse = unit_lower_inverse(mixing, rows, cols)
    inverse_ref[0] = inverse
    both = full_dot(inverse, jnp.concatenate([(beta * head_decay) * key, beta * value], 1))
    scores = full_dot(query, key, NT) * decays
    read = full_dot(scores, both)
    carried_ref[...] = head_decay * query - read[:, :key_size]
    local_ref[...] = read[:, key_size:]
    written = full_dot(key * tail_decay, both, TN)
    size = key.shape[0]
    krows, kcols = places(key_size)
    kept = jnp.where(krows == kcols, head_decay[size - 1 : size], 0.0)
    map_ref[0] = jnp.concatenate([kept - written[:, :key_size], written[:, key_size:]], 1)


def gate_kernel(
    me_ref, maps_ref, state_ref, carried_ref, local_ref, outgate_ref, gain_ref,
    gated_ref, output_ref, entry_ref, end_ref,
):
    key_size = state_ref.shape[1]
    me = me_ref[0]
    state = state_ref[0]
    entry = state
    for at in range(maps_ref.shape[0]):
        if at:
            entry = jnp.where(me == at, state, entry)
        step = maps_ref[at, 0]
        state = full_dot(step[:, :key_size], state) + step[:, key_size:]
    entry_ref[0] = entry
    end_ref[0] = state
    output = local_ref[...] + full_dot(carried_ref[...], entry)
    output_ref[...] = output
    normed = output * lax.rsqrt(jnp.mean(output * output, 1, keepdims=True) + EPSILON) * gain_ref[...]
    gate = outgate_ref[...]
    gated_ref[...] = (normed * (gate * sigmoid(gate))).astype(LOW).astype(F32)


def gate_back_kernel(
    top_ref, weight_ref, output_ref, outgate_ref, gain_ref, carried_ref,
    top_low_ref, output_grad_ref, outgate_grad_ref, gain_grad_ref, entry_ref,
):
    top_low = top_ref[...].astype(LOW)
    top_low_ref[...] = top_low
    grad = low_dot(top_low, weight_ref[...], NT)
    output, gate, gain = output_ref[...], outgate_ref[...], gain_ref[...]
    inverse = lax.rsqrt(jnp.mean(output * output, 1, keepdims=True) + EPSILON)
    unit = output * inverse
    opened = sigmoid(gate)
    swished = gate * opened
    outgate_grad_ref[...] = (grad * unit * gain * (opened * (1.0 + gate * (1.0 - opened)))).astype(LOW)
    gain_grad_ref[0] = jnp.sum(grad * unit * swished, 0, keepdims=True)
    unit_grad = grad * gain * swished
    output_grad = inverse * (unit_grad - unit * jnp.mean(unit_grad * unit, 1, keepdims=True))
    output_grad_ref[...] = output_grad
    entry_ref[0] = full_dot(carried_ref[...], output_grad, TN)


def local_back_kernel(
    heads, me_ref, maps_ref, entries_ref, state_grad_ref, query_ref, key_ref, value_ref, side_ref,
    resets_ref, border_q, border_k, border_v, taps_q, taps_k, taps_v, rate_ref, bias_ref,
    inverse_ref, entry_state_ref, output_grad_ref,
    dquery_ref, dkey_ref, dvalue_ref, dborder_q, dborder_k, dborder_v, dtaps_q, dtaps_k, dtaps_v,
    dside_ref, start_grad_ref,
):
    head = pl.program_id(0)
    key_size = query_ref.shape[1]
    size = query_ref.shape[0]
    scale = key_size**-0.5
    me = me_ref[0]
    state_grad = state_grad_ref[0]
    end_grad = state_grad
    count = maps_ref.shape[0]
    for at in reversed(range(count)):
        if at < count - 1:
            end_grad = jnp.where(me == at, state_grad, end_grad)
        state_grad = full_dot(maps_ref[at, 0], state_grad, TN) + entries_ref[at, 0]
    start_grad_ref[0] = state_grad

    shifted, log_decay, beta, decays, head_decay, tail_decay, rows, cols, lower = token_gates(
        side_ref[...], resets_ref[:, 0:1], head, heads, rate_ref[head], bias_ref[head]
    )
    padded_q = with_border(border_q[...], query_ref[...])
    padded_k = with_border(border_k[...], key_ref[...])
    padded_v = with_border(border_v[...], value_ref[...])
    summed_q = conv_sum(padded_q, taps_q[...])
    summed_k = conv_sum(padded_k, taps_k[...])
    summed_v = conv_sum(padded_v, taps_v[...])
    act_q, gate_q, inverse_q, query = silu_unit(summed_q, scale)
    act_k, gate_k, inverse_k, key = silu_unit(summed_k, 1.0)
    gate_v = sigmoid(summed_v)
    value = summed_v * gate_v
    state = entry_state_ref[0]
    inverse = inverse_ref[0]
    output_grad = output_grad_ref[...]

    gram = full_dot(key, key, NT)
    pure = full_dot(query, key, NT)
    scores = pure * decays
    tail_key = key * tail_decay
    residue = value - head_decay * full_dot(key, state)
    update = full_dot(inverse, beta * residue)
    update_grad = full_dot(scores, output_grad, TN) + full_dot(tail_key, end_grad)
    target_grad = full_dot(inverse, update_grad, TN)
    strict = rows > cols
    mixing_grad = jnp.where(strict, -full_dot(target_grad, update, NT), 0.0)
    scores_grad = full_dot(output_grad, update, NT)
    pure_grad = scores_grad * decays
    reached = full_dot(output_grad, state, NT)
    erased = full_dot(target_grad, state, NT)
    kept = full_dot(update, end_grad, NT)
    weighted = mixing_grad * decays
    gram_grad = weighted * beta
    query_grad = head_decay * reached + full_dot(pure_grad, key)
    key_grad = (
        full_dot(pure_grad, query, TN)
        + tail_decay * kept
        - (beta * head_decay) * erased
        + full_dot(gram_grad, key)
        + full_dot(gram_grad, key, TN)
    )
    value_grad = beta * target_grad
    beta_grad = jnp.sum(target_grad * residue, 1, keepdims=True) + jnp.sum(
        weighted * gram, 1, keepdims=True
    )
    spread = pure_grad * pure + gram_grad * gram
    head_decay_grad = jnp.sum(query * reached, 1, keepdims=True) - beta * jnp.sum(
        key * erased, 1, keepdims=True
    )
    tail_part = tail_decay * jnp.sum(key * kept, 1, keepdims=True)
    ones = jnp.ones((size, 128), F32)
    column_sums = full_dot(spread, ones, TN)[:, 0:1]
    total_grad = (
        head_decay * head_decay_grad - tail_part + jnp.sum(spread, 1, keepdims=True) - column_sums
    )
    last_grad = jnp.sum(tail_part, 0, keepdims=True) + head_decay[size - 1 : size] * jnp.sum(
        jnp.sum(end_grad * state, 1, keepdims=True), 0, keepdims=True
    )
    places_col = lax.broadcasted_iota(jnp.int32, (size, 1), 0)
    total_grad = total_grad + jnp.where(places_col == size - 1, last_grad, 0.0)
    lanes = lax.broadcasted_iota(jnp.int32, (size, 128), 1)
    log_grad = full_dot(lower, jnp.where(lanes == 0, total_grad, 0.0), TN)[:, 0:1]
    decay_grad = log_grad * (-rate_ref[head]) * sigmoid(shifted)
    beta_in_grad = beta_grad * beta * (1.0 - beta)
    dside_ref[0] = jnp.where(
        lanes == 0,
        decay_grad,
        jnp.where(lanes == 1, beta_in_grad, jnp.where(lanes == 2, log_grad * log_decay, 0.0)),
    )

    summed_q_grad = silu_unit_back(query_grad, summed_q, gate_q, act_q, inverse_q, scale)
    summed_k_grad = silu_unit_back(key_grad, summed_k, gate_k, act_k, inverse_k, 1.0)
    summed_v_grad = value_grad * gate_v * (1.0 + summed_v * (1.0 - gate_v))
    for grad, padded, taps, out, border_out, taps_out in (
        (summed_q_grad, padded_q, taps_q, dquery_ref, dborder_q, dtaps_q),
        (summed_k_grad, padded_k, taps_k, dkey_ref, dborder_k, dtaps_k),
        (summed_v_grad, padded_v, taps_v, dvalue_ref, dborder_v, dtaps_v),
    ):
        spread_out = conv_transposed(grad, taps[...])
        border_out[...] = spread_out[:8]
        out[...] = spread_out[8:]
        taps_out[...] = conv_taps_grad(padded, grad, taps.shape[0])


def block(shape, place):
    return pl.BlockSpec(shape, place)


def smem():
    return pl.BlockSpec(memory_space=pltpu.SMEM)


def params():
    return pltpu.CompilerParams(vmem_limit_bytes=VMEM_BYTES)


def projection_specs(rows, heads, key_size, value_size, count):
    ratio = value_size // key_size
    return [
        block((rows, key_size), lambda h: (0, h)),
        block((rows, key_size), lambda h: (0, heads + h)),
        block((rows, value_size), lambda h: (0, 2 * heads // ratio + h)),
        block((rows, 128), lambda h: (0, (2 + 2 * ratio) * heads * key_size // 128)),
        block((rows, 128), lambda h: (0, 0)),
        block((8, key_size), lambda h: (0, h)),
        block((8, key_size), lambda h: (0, heads + h)),
        block((8, value_size), lambda h: (0, 2 * heads // ratio + h)),
        block((count, key_size), lambda h: (0, h)),
        block((count, key_size), lambda h: (0, h)),
        block((count, value_size), lambda h: (0, h)),
        smem(),
        smem(),
    ]


def mixer_local(sizes, projected, resets, border, taps, rate, bias):
    heads, key_size, value_size = sizes
    rows = projected.shape[0]
    return pl.pallas_call(
        partial(local_kernel, heads),
        grid=(heads,),
        in_specs=projection_specs(rows, heads, key_size, value_size, taps[0].shape[0]),
        out_specs=[
            block((rows, key_size), lambda h: (0, h)),
            block((rows, value_size), lambda h: (0, h)),
            block((1, key_size, key_size + value_size), lambda h: (h, 0, 0)),
            block((1, rows, rows), lambda h: (h, 0, 0)),
        ],
        out_shape=[
            jax.ShapeDtypeStruct((rows, heads * key_size), F32),
            jax.ShapeDtypeStruct((rows, heads * value_size), F32),
            jax.ShapeDtypeStruct((heads, key_size, key_size + value_size), F32),
            jax.ShapeDtypeStruct((heads, rows, rows), F32),
        ],
        compiler_params=params(),
        name="mixer_local",
    )(projected, projected, projected, projected, resets, border, border, border, *taps, rate, bias)


def mixer_gate(sizes, me, maps, state, carried, local, projected, gain):
    heads, key_size, value_size = sizes
    rows = projected.shape[0]
    ratio = value_size // key_size
    seq = maps.shape[0]
    return pl.pallas_call(
        gate_kernel,
        grid=(heads,),
        in_specs=[
            smem(),
            block((seq, 1, key_size, key_size + value_size), lambda h: (0, h, 0, 0)),
            block((1, key_size, value_size), lambda h: (h, 0, 0)),
            block((rows, key_size), lambda h: (0, h)),
            block((rows, value_size), lambda h: (0, h)),
            block((rows, value_size), lambda h: (0, 2 * heads // ratio + heads + h)),
            block((1, value_size), lambda h: (0, 0)),
        ],
        out_specs=[
            block((rows, value_size), lambda h: (0, h)),
            block((rows, value_size), lambda h: (0, h)),
            block((1, key_size, value_size), lambda h: (h, 0, 0)),
            block((1, key_size, value_size), lambda h: (h, 0, 0)),
        ],
        out_shape=[
            jax.ShapeDtypeStruct((rows, heads * value_size), F32),
            jax.ShapeDtypeStruct((rows, heads * value_size), F32),
            jax.ShapeDtypeStruct((heads, key_size, value_size), F32),
            jax.ShapeDtypeStruct((heads, key_size, value_size), F32),
        ],
        compiler_params=params(),
        name="mixer_gate",
    )(me, maps, state, carried, local, projected, gain)


def mixer_gate_back(sizes, top, weight, output, projected, gain, carried):
    heads, key_size, value_size = sizes
    rows, width = top.shape
    ratio = value_size // key_size
    return pl.pallas_call(
        gate_back_kernel,
        grid=(heads,),
        in_specs=[
            block((rows, width), lambda h: (0, 0)),
            block((value_size, width), lambda h: (h, 0)),
            block((rows, value_size), lambda h: (0, h)),
            block((rows, value_size), lambda h: (0, 2 * heads // ratio + heads + h)),
            block((1, value_size), lambda h: (0, 0)),
            block((rows, key_size), lambda h: (0, h)),
        ],
        out_specs=[
            block((rows, width), lambda h: (0, 0)),
            block((rows, value_size), lambda h: (0, h)),
            block((rows, value_size), lambda h: (0, h)),
            block((1, 1, value_size), lambda h: (h, 0, 0)),
            block((1, key_size, value_size), lambda h: (h, 0, 0)),
        ],
        out_shape=[
            jax.ShapeDtypeStruct((rows, width), LOW),
            jax.ShapeDtypeStruct((rows, heads * value_size), F32),
            jax.ShapeDtypeStruct((rows, heads * value_size), LOW),
            jax.ShapeDtypeStruct((heads, 1, value_size), F32),
            jax.ShapeDtypeStruct((heads, key_size, value_size), F32),
        ],
        compiler_params=params(),
        name="mixer_gate_back",
    )(top, weight, output, projected, gain, carried)


def mixer_local_back(
    sizes, me, maps, entries, state_grad, projected, resets, border, taps, rate, bias, inverse,
    entry_state, output_grad,
):
    heads, key_size, value_size = sizes
    rows = projected.shape[0]
    seq = maps.shape[0]
    count = taps[0].shape[0]
    q_block = block((rows, key_size), lambda h: (0, h))
    v_block = block((rows, value_size), lambda h: (0, h))
    s_block = block((1, key_size, value_size), lambda h: (h, 0, 0))
    return pl.pallas_call(
        partial(local_back_kernel, heads),
        grid=(heads,),
        in_specs=[
            smem(),
            block((seq, 1, key_size, key_size), lambda h: (0, h, 0, 0)),
            block((seq, 1, key_size, value_size), lambda h: (0, h, 0, 0)),
            s_block,
        ]
        + projection_specs(rows, heads, key_size, value_size, count)
        + [block((1, rows, rows), lambda h: (h, 0, 0)), s_block, v_block],
        out_specs=[
            q_block,
            q_block,
            v_block,
            block((8, key_size), lambda h: (0, h)),
            block((8, key_size), lambda h: (0, h)),
            block((8, value_size), lambda h: (0, h)),
            block((count, key_size), lambda h: (0, h)),
            block((count, key_size), lambda h: (0, h)),
            block((count, value_size), lambda h: (0, h)),
            block((1, rows, 128), lambda h: (h, 0, 0)),
            s_block,
        ],
        out_shape=[
            jax.ShapeDtypeStruct((rows, heads * key_size), F32),
            jax.ShapeDtypeStruct((rows, heads * key_size), F32),
            jax.ShapeDtypeStruct((rows, heads * value_size), F32),
            jax.ShapeDtypeStruct((8, heads * key_size), F32),
            jax.ShapeDtypeStruct((8, heads * key_size), F32),
            jax.ShapeDtypeStruct((8, heads * value_size), F32),
            jax.ShapeDtypeStruct((count, heads * key_size), F32),
            jax.ShapeDtypeStruct((count, heads * key_size), F32),
            jax.ShapeDtypeStruct((count, heads * value_size), F32),
            jax.ShapeDtypeStruct((heads, rows, 128), F32),
            jax.ShapeDtypeStruct((heads, key_size, value_size), F32),
        ],
        compiler_params=params(),
        name="mixer_local_back",
    )(
        me, maps, entries, state_grad, projected, projected, projected, projected, resets,
        border, border, border, *taps, rate, bias, inverse, entry_state, output_grad,
    )


def narrow_kernel(wide_ref, low_ref):
    low_ref[...] = wide_ref[...].astype(LOW)


def widen_kernel(low_ref, wide_ref):
    wide_ref[...] = low_ref[...].astype(F32)


def recast(kernel, values, dtype):
    rows, cols = values.shape
    tile = min(rows, 256)
    return pl.pallas_call(
        kernel,
        grid=(rows // tile,),
        in_specs=[block((tile, cols), lambda i: (i, 0))],
        out_specs=block((tile, cols), lambda i: (i, 0)),
        out_shape=jax.ShapeDtypeStruct((rows, cols), dtype),
        compiler_params=params(),
    )(values)


def join_kernel(rows_ref, gated_ref, weight_ref, gain_ref, mixed_ref, hidden_ref, total):
    step = pl.program_id(0)

    @pl.when(step == 0)
    def _():
        total[...] = rows_ref[...]

    total[...] += low_dot(gated_ref[0].astype(LOW), weight_ref[...])

    @pl.when(step == pl.num_programs(0) - 1)
    def _():
        mixed = total[...]
        mixed_ref[...] = mixed
        inverse = lax.rsqrt(jnp.mean(mixed * mixed, 1, keepdims=True) + EPSILON)
        hidden_ref[...] = (mixed * inverse * gain_ref[...]).astype(LOW)


def join_heads(rows, gated, weight, gain):
    parts, count, depth = gated.shape
    width = weight.shape[1]
    whole = block((count, width), lambda i: (0, 0))
    return pl.pallas_call(
        join_kernel,
        grid=(parts,),
        in_specs=[
            whole,
            block((1, count, depth), lambda i: (i, 0, 0)),
            block((depth, width), lambda i: (i, 0)),
            block((1, width), lambda i: (0, 0)),
        ],
        out_specs=[whole, whole],
        out_shape=[
            jax.ShapeDtypeStruct((count, width), F32),
            jax.ShapeDtypeStruct((count, width), LOW),
        ],
        scratch_shapes=[pltpu.VMEM((count, width), F32)],
        compiler_params=params(),
        name="join_heads",
    )(rows, gated, weight, gain)


def top_kernel(last_ref, given_ref, handed_ref, low_ref):
    given = given_ref[...].astype(F32)
    low_ref[...] = jnp.where(last_ref[0] == 1, given, handed_ref[...]).astype(LOW)


def pick_top(last, given, handed):
    rows, cols = given.shape
    tile = rows // 4
    spec = block((tile, cols), lambda i: (i, 0))
    return pl.pallas_call(
        top_kernel,
        grid=(4,),
        in_specs=[smem(), spec, spec],
        out_specs=spec,
        out_shape=jax.ShapeDtypeStruct((rows, cols), LOW),
        compiler_params=params(),
        name="pick_top",
    )(last, given, handed)


def row_norm(values, gain):
    return values * lax.rsqrt(jnp.mean(values * values, -1, keepdims=True) + EPSILON) * gain


def row_norm_back(values, gain, grad):
    inverse = lax.rsqrt(jnp.mean(values * values, -1, keepdims=True) + EPSILON)
    unit = values * inverse
    scaled = grad * gain
    back = inverse * (scaled - unit * jnp.mean(unit * scaled, -1, keepdims=True))
    return back, jnp.sum(unit * grad, 0)


def ring(value, axis, steps):
    count = lax.axis_size(axis)
    return lax.ppermute(value, axis, [(at, (at + steps) % count) for at in range(count)])


def handed_on(value, axis, steps):
    count = lax.axis_size(axis)
    first, last = max(0, -steps), min(count, count - steps)
    return lax.ppermute(value, axis, [(at, at + steps) for at in range(first, last)])


def scatter_sum(values, axis):
    count = lax.axis_size("seq")
    if count % 2:
        return lax.psum_scatter(values, "seq", scatter_dimension=axis, tiled=True)
    index = lax.axis_index("seq")
    core, chip = index % 2, index // 2
    chips = count // 2
    shape = values.shape
    chunk = shape[axis] // count
    split = values.reshape(shape[:axis] + (chips, 2, chunk) + shape[axis + 1 :])
    pick = lambda array, at, dim: lax.dynamic_index_in_dim(array, at, dim, keepdims=False)
    other = lax.ppermute(
        pick(split, 1 - core, axis + 1), "seq", [(at, at ^ 1) for at in range(count)]
    )
    summed = pick(split, core, axis + 1) + other
    if chips == 2:
        other = lax.ppermute(pick(summed, 1 - chip, axis), "seq", [(at, at ^ 2) for at in range(4)])
        return pick(summed, chip, axis) + other
    summed = summed.reshape(shape[:axis] + (chips * chunk,) + shape[axis + 1 :])
    groups = [[2 * at + half for at in range(chips)] for half in range(2)]
    return lax.psum_scatter(
        summed, "seq", scatter_dimension=axis, axis_index_groups=groups, tiled=True
    )


def local(
    inputs, cotangent, doc_start, norm_in, query_weight, key_weight, value_weight, outgate_weight,
    decay_weight, beta_weight, conv_query, conv_key, conv_value, decay_log, decay_bias, head_norm,
    out_weight, norm_feed, gate_weight, up_weight, down_weight,
):
    query_weight, key_weight, value_weight = query_weight[0], key_weight[0], value_weight[0]
    outgate_weight, decay_weight, beta_weight = outgate_weight[0], decay_weight[0], beta_weight[0]
    gate_weight, up_weight, down_weight, out_weight = (
        gate_weight[0], up_weight[0], down_weight[0], out_weight[0],
    )
    taps = (conv_query[0], conv_key[0], conv_value[0])
    rate, bias = jnp.exp(decay_log[0]), decay_bias[0]
    heads = bias.shape[0]
    key_size = query_weight.shape[1] // heads
    value_size = value_weight.shape[1] // heads
    sizes = (heads, key_size, value_size)
    key_cols, value_cols = heads * key_size, heads * value_size
    micros, own_rows, width = inputs.shape
    rows = cotangent.shape[1]
    seq_size, seq_index = lax.axis_size("seq"), lax.axis_index("seq")
    tp_index = lax.axis_index("tp")
    section = lax.axis_index("section")
    at_start, at_end = seq_index == 0, seq_index == seq_size - 1
    me = seq_index.astype(jnp.int32).reshape(1)
    last_section = section.astype(jnp.int32).reshape(1)
    group = 2 if micros % 2 == 0 else 1
    groups = micros // group

    def own(values):
        return lax.dynamic_slice_in_dim(values, tp_index * own_rows, own_rows, 0)

    part = width // seq_size
    piece = lax.dynamic_slice_in_dim(out_weight, seq_index * part, part, 1)
    piece = lax.all_gather(recast(widen_kernel, piece, F32), "tp", axis=0, tiled=True)
    pieces = lax.all_gather(piece, "seq", axis=0)
    low_pieces = recast(narrow_kernel, pieces.reshape(-1, part), LOW).reshape(pieces.shape)
    out_full = jnp.moveaxis(low_pieces, 0, 1).reshape(-1, width)

    spare = jnp.zeros((width, 128 - 2 * heads), LOW)
    in_weight = jnp.concatenate(
        [query_weight, key_weight, value_weight, outgate_weight, decay_weight, beta_weight, spare], 1
    )
    conv_cols = 2 * key_cols + value_cols
    offsets = jnp.arange(rows, dtype=jnp.int32)

    def micro_of(step, member):
        return jnp.clip(step - section, 0, groups - 1) * group + member

    def reset_flags(micro):
        starts = micro * (rows * seq_size) + seq_index * rows + offsets
        flags = lax.dynamic_index_in_dim(doc_start, micro, 0, keepdims=False) == starts
        return jnp.broadcast_to(flags.astype(F32)[:, None], (rows, 128))

    saved = {}
    section_rows = {}
    received = [jnp.zeros((own_rows, width), F32)] * group
    border_carry = jnp.zeros((8, conv_cols), F32)
    state = jnp.zeros((heads, key_size, value_size), F32)
    for step in range(groups + 1):
        sent = []
        for member in range(group):
            micro = micro_of(step, member)
            given = lax.dynamic_index_in_dim(inputs, micro, 0, keepdims=False).astype(F32)
            entering = jnp.where(section == 0, given, received[member])
            residual = lax.all_gather(entering, "tp", axis=0, tiled=True)
            hidden = row_norm(residual, norm_in).astype(LOW)
            tail = low_dot(hidden[rows - 8 :], in_weight[:, :conv_cols])
            moved = ring(tail, "seq", 1)
            border = jnp.where(at_start, border_carry, moved)
            border_carry = moved
            projected = low_dot(hidden, in_weight)
            resets = reset_flags(micro)
            carried, local_out, maps, inverse = mixer_local(
                sizes, projected, resets, border, taps, rate, bias
            )
            all_maps = lax.all_gather(maps, "seq", axis=0)
            gated, output, entry_state, state = mixer_gate(
                sizes, me, all_maps, state, carried, local_out, projected, head_norm
            )
            mixed, hidden_feed = join_heads(
                residual, lax.all_gather(gated, "tp", axis=0), out_full, norm_feed
            )
            gate_act = low_dot(hidden_feed, gate_weight)
            up_act = low_dot(hidden_feed, up_weight)
            inner = (gate_act * sigmoid(gate_act) * up_act).astype(LOW)
            out_rows = own(mixed) + lax.psum_scatter(
                low_dot(inner, down_weight), "tp", scatter_dimension=0, tiled=True
            )
            section_rows[step, member] = out_rows
            if step < groups:
                sent.append(handed_on(out_rows, "section", 1))
            saved[step, member] = dict(
                entering=entering, hidden=hidden, border=border, projected=projected, resets=resets,
                carried=carried, maps=all_maps[..., :key_size], inverse=inverse, gated=gated,
                output=output, entry_state=entry_state, mixed=own(mixed), hidden_feed=hidden_feed,
                gate_act=gate_act, up_act=up_act, inner=inner,
            )
        received = sent

    received = [jnp.zeros((own_rows, width), F32)] * group
    tail_carry = jnp.zeros((8, conv_cols), F32)
    state_grad = jnp.zeros((heads, key_size, value_size), F32)
    in_grads = {}
    norm_in_grad = jnp.zeros((width,), F32)
    norm_feed_grad = jnp.zeros((width,), F32)
    gain_grad = jnp.zeros((value_size,), F32)
    taps_grads = [jnp.zeros(member.shape, F32) for member in taps]
    side_grad = jnp.zeros((heads, 128), F32)
    for back_step in range(groups + 1):
        step = groups - back_step
        sent = [None] * group
        for member in reversed(range(group)):
            kept = saved[step, member]
            micro = micro_of(step, member)
            given = lax.dynamic_index_in_dim(cotangent, micro, 0, keepdims=False)
            if step == 0:
                given = jnp.where(section == 0, given, jnp.zeros_like(given))
            if back_step:
                handed = lax.all_gather(received[member], "tp", axis=0, tiled=True)
                top_low = pick_top(last_section, given, handed)
            else:
                top_low = jnp.where(section == 0, jnp.zeros_like(given), given)
            top_own = jnp.where(section == 0, received[member], own(given).astype(F32))
            kept["top_low"] = top_low
            inner_grad = low_dot(top_low, down_weight, NT)
            gate_act, up_act = kept["gate_act"], kept["up_act"]
            opened = sigmoid(gate_act)
            gate_low = (inner_grad * up_act * (opened * (1.0 + gate_act * (1.0 - opened)))).astype(LOW)
            up_low = (inner_grad * gate_act * opened).astype(LOW)
            kept["gate_low"], kept["up_low"] = gate_low, up_low
            feed_grad = lax.psum_scatter(
                low_dot(gate_low, gate_weight, NT) + low_dot(up_low, up_weight, NT),
                "tp",
                scatter_dimension=0,
                tiled=True,
            )
            mixed_back, feed_part = row_norm_back(kept["mixed"], norm_feed[0], feed_grad)
            norm_feed_grad = norm_feed_grad + feed_part
            mixed_grad = top_own + mixed_back
            mixed_full = lax.all_gather(mixed_grad, "tp", axis=0, tiled=True)
            mixed_low, output_grad, outgate_low, gain_part, entry_grad = mixer_gate_back(
                sizes, mixed_full, out_weight, kept["output"], kept["projected"], head_norm,
                kept["carried"],
            )
            kept["mixed_low"] = mixed_low
            gain_grad = gain_grad + jnp.sum(gain_part, (0, 1))
            all_entries = lax.all_gather(entry_grad, "seq", axis=0)
            (
                query_grad, key_grad, value_grad, border_q, border_k, border_v, taps_q, taps_k,
                taps_v, side, state_grad,
            ) = mixer_local_back(
                sizes, me, kept["maps"], all_entries, state_grad, kept["projected"],
                kept["resets"], kept["border"], taps, rate, bias, kept["inverse"],
                kept["entry_state"], output_grad,
            )
            moved = ring(jnp.concatenate([border_q, border_k, border_v], 1), "seq", -1)
            tail = jnp.where(at_end, tail_carry, moved)
            tail_carry = moved
            conv_grad = jnp.concatenate([query_grad, key_grad, value_grad], 1)
            conv_grad = jnp.concatenate([conv_grad[: rows - 8], conv_grad[rows - 8 :] + tail], 0)
            projected_low = jnp.concatenate(
                [
                    conv_grad.astype(LOW),
                    outgate_low,
                    side[:, :, 0].T.astype(LOW),
                    side[:, :, 1].T.astype(LOW),
                    jnp.zeros((rows, 128 - 2 * heads), LOW),
                ],
                1,
            )
            kept["projected_low"] = projected_low
            taps_grads = [
                total + part for total, part in zip(taps_grads, (taps_q, taps_k, taps_v))
            ]
            side_grad = side_grad + jnp.sum(side, 1)
            hidden_grad = lax.psum_scatter(
                low_dot(projected_low, in_weight, NT), "tp", scatter_dimension=0, tiled=True
            )
            entering_back, in_part = row_norm_back(kept["entering"], norm_in[0], hidden_grad)
            norm_in_grad = norm_in_grad + in_part
            own_grad = mixed_grad + entering_back
            in_grads[step, member] = own_grad
            if back_step < groups:
                sent[member] = handed_on(own_grad, "section", -1)
        received = sent

    def of_section(values):
        return [
            jnp.where(section == 0, values[at, member], values[at + 1, member])
            for at in range(groups)
            for member in range(group)
        ]

    def all_rows(name):
        outer = [
            jnp.where(section == 0, saved[0, member][name], saved[groups, member][name])
            for member in range(group)
        ]
        inner = [saved[at, member][name] for at in range(1, groups) for member in range(group)]
        return jnp.concatenate(outer + inner, 0)

    hidden_all, hidden_feed_all = all_rows("hidden"), all_rows("hidden_feed")
    top_all = all_rows("top_low")
    grad_gate = scatter_sum(low_dot(hidden_feed_all, all_rows("gate_low"), TN), 0)
    grad_up = scatter_sum(low_dot(hidden_feed_all, all_rows("up_low"), TN), 0)
    grad_down = scatter_sum(low_dot(all_rows("inner"), top_all, TN), 1)
    grad_out = scatter_sum(low_dot(all_rows("gated").astype(LOW), all_rows("mixed_low"), TN), 1)
    grad_in = scatter_sum(low_dot(hidden_all, all_rows("projected_low"), TN), 0)

    own_tp = jnp.arange(lax.axis_size("tp")) == tp_index
    per_tp = jnp.concatenate(
        [member.reshape(-1) for member in taps_grads] + [side_grad[:, 2], side_grad[:, 0]]
    )
    small = lax.psum(
        jnp.concatenate(
            [
                norm_in_grad,
                norm_feed_grad,
                gain_grad,
                jnp.where(own_tp[:, None], per_tp[None], 0.0).reshape(-1),
            ]
        ),
        ("seq", "tp"),
    )
    norm_in_grad, norm_feed_grad = small[:width], small[width : 2 * width]
    gain_grad = small[2 * width : 2 * width + value_size]
    per_tp = lax.dynamic_slice_in_dim(
        small, 2 * width + value_size + tp_index * per_tp.shape[0], per_tp.shape[0], 0
    )
    pieces, at = [], 0
    for member in taps:
        pieces.append(per_tp[at : at + member.size].reshape(member.shape))
        at += member.size
    log_grad, bias_grad = per_tp[at : at + heads], per_tp[at + heads : at + 2 * heads]
    bounds = [
        0, key_cols, 2 * key_cols, conv_cols, conv_cols + value_cols, conv_cols + value_cols + heads,
        conv_cols + value_cols + 2 * heads,
    ]
    in_parts = [grad_in[:, low:high] for low, high in zip(bounds[:-1], bounds[1:])]
    return (
        jnp.stack(of_section(section_rows))[None],
        jnp.stack(of_section(in_grads))[None],
        norm_in_grad[None],
        *[member[None] for member in in_parts],
        *[member[None] for member in pieces],
        log_grad[None],
        bias_grad[None],
        gain_grad[None],
        grad_out[None],
        norm_feed_grad[None],
        grad_gate[None],
        grad_up[None],
        grad_down[None],
    )


def solution(mesh):
    by_column, by_row = P("section", None, "tp"), P("section", "tp", None)
    placed = (
        P(None, ("seq", "tp"), None),
        P(None, "seq", None),
        P(None, "seq"),
        P("section", None),
        *[by_column] * 9,
        P("section", "tp"),
        P("section", "tp"),
        P("section", None),
        by_row,
        P("section", None),
        by_column,
        by_column,
        by_row,
    )
    rows_out = P("section", None, ("seq", "tp"), None)
    both = P("section", "seq", "tp")
    return jax.shard_map(
        local,
        mesh=mesh,
        in_specs=placed,
        out_specs=(
            rows_out,
            rows_out,
            P("section", None),
            *[both] * 6,
            *[by_column] * 3,
            P("section", "tp"),
            P("section", "tp"),
            P("section", None),
            P("section", "tp", "seq"),
            P("section", None),
            both,
            both,
            P("section", "tp", "seq"),
        ),
        check_vma=False,
    )
```

```python
from functools import partial

import jax
import jax.numpy as jnp
from jax import lax
from jax.experimental import pallas as pl
from jax.experimental.pallas import tpu as pltpu
from jax.sharding import PartitionSpec as P

EPSILON = 1e-06
F32 = jnp.float32
LOW = jnp.bfloat16
VMEM_BYTES = 48 * 1024 * 1024
GROUP = 2
NN = ((1,), (0,))
NT = ((1,), (1,))
TN = ((0,), (0,))


def low_dot(a, b, contract=NN):
    return lax.dot_general(a, b, (contract, ((), ())), preferred_element_type=F32)


def halves(x):
    high = x.astype(LOW)
    return high, (x - high.astype(F32)).astype(LOW)


def thirds(x):
    high = x.astype(LOW)
    rest = x - high.astype(F32)
    middle = rest.astype(LOW)
    return high, middle, (rest - middle.astype(F32)).astype(LOW)


def pair_dot(a, b, contract=NN):
    left, right = contract[0][0], contract[1][0]
    return low_dot(
        jnp.concatenate([a[0], a[0], a[1]], left),
        jnp.concatenate([b[0], b[1], b[0]], right),
        contract,
    )


def fine_dot(a, b, contract=NN):
    return pair_dot(halves(a), halves(b), contract)


def sigmoid(x):
    return 1.0 / (1.0 + jnp.exp(-x))


def places(size):
    return (
        lax.broadcasted_iota(jnp.int32, (size, size), 0),
        lax.broadcasted_iota(jnp.int32, (size, size), 1),
    )


def unit_lower_inverses(strict_parts, rows, cols):
    size = strict_parts[0].shape[0]
    near = (rows >> 3) == (cols >> 3)
    eye = jnp.where(rows == cols, 1.0, 0.0)
    inner = [jnp.where(near, part, 0.0) for part in strict_parts]
    split = [halves(part) for part in inner]
    second = [halves(pair_dot(part, part)) for part in split]
    fourth = [halves(pair_dot(part, part)) for part in second]
    inverse = [eye - part for part in inner]
    inverse = [part + pair_dot(halves(part), power) for part, power in zip(inverse, second)]
    inverse = [part + pair_dot(halves(part), power) for part, power in zip(inverse, fourth)]
    level = 3
    while (1 << level) < size:
        joined = ((rows >> (level + 1)) == (cols >> (level + 1))) & ((rows >> level) != (cols >> level))
        split = [halves(part) for part in inverse]
        middle = [
            halves(pair_dot(halves(jnp.where(joined, strict, 0.0)), part))
            for strict, part in zip(strict_parts, split)
        ]
        inverse = [
            part - pair_dot(pair, between) for part, pair, between in zip(inverse, split, middle)
        ]
        level += 1
    return inverse


def taps_back(padded, steps):
    rolled = padded if steps == 0 else pltpu.roll(padded, steps, 0)
    return rolled[8:]


def conv_sum(padded, taps):
    count = taps.shape[0]
    total = taps[0:1] * taps_back(padded, count - 1)
    for member in range(1, count):
        total = total + taps[member : member + 1] * taps_back(padded, count - 1 - member)
    return total


def conv_transposed(grad, taps):
    count = taps.shape[0]
    padded = jnp.concatenate([jnp.zeros((8, grad.shape[1]), F32), grad], 0)
    size = padded.shape[0]
    total = taps[count - 1 : count] * padded
    for member in range(count - 1):
        total = total + taps[member : member + 1] * pltpu.roll(padded, size - (count - 1 - member), 0)
    return total


def conv_taps_grad(padded, grad, count):
    return jnp.concatenate(
        [
            jnp.sum(grad * taps_back(padded, count - 1 - member), 0, keepdims=True)
            for member in range(count)
        ],
        0,
    )


def softplus(x):
    return jnp.maximum(x, 0.0) + jnp.log(1.0 + jnp.exp(-jnp.abs(x)))


class Gates:
    def __init__(self, side, resets, head, heads, rate, bias, rows, cols):
        size = side.shape[0]
        self.rate = rate
        self.shifted = side[:, head : head + 1] + bias
        self.log_decay = -rate * softplus(self.shifted)
        self.beta = sigmoid(side[:, heads + head : heads + head + 1])
        lanes = lax.broadcasted_iota(jnp.int32, (size, 128), 1)
        pair = jnp.where(lanes == 0, self.log_decay, jnp.where(lanes == 1, resets, 0.0))
        lower = jnp.where(rows >= cols, 1.0, 0.0).astype(LOW)
        split = thirds(pair)
        as_columns = low_dot(
            jnp.concatenate([lower] * 3, 1), jnp.concatenate(split, 0)
        )
        as_rows = low_dot(
            jnp.concatenate(split, 0), jnp.concatenate([lower] * 3, 1), ((0,), (1,))
        )
        total, count = as_columns[:, 0:1], as_columns[:, 1:2]
        linked = (jnp.abs(count - as_rows[1:2, :]) < 0.5) & (rows >= cols)
        self.decays = jnp.where(linked, jnp.exp(jnp.minimum(total - as_rows[0:1, :], 0.0)), 0.0)
        last_total, last_count = total[size - 1 : size], count[size - 1 : size]
        self.head_decay = jnp.where(count < 0.5, jnp.exp(total), 0.0)
        self.tail_decay = jnp.where(
            jnp.abs(count - last_count) < 0.5, jnp.exp(jnp.minimum(last_total - total, 0.0)), 0.0
        )


def silu_unit(summed, scale):
    gate = sigmoid(summed)
    act = summed * gate
    inverse = lax.rsqrt(jnp.sum(act * act, 1, keepdims=True) + EPSILON)
    return act, gate, inverse, act * (inverse * scale)


def silu_unit_back(grad, summed, gate, act, inverse, scale):
    unit = act * inverse
    grad = grad * scale
    act_grad = inverse * (grad - unit * jnp.sum(grad * unit, 1, keepdims=True))
    return act_grad * gate * (1.0 + summed * (1.0 - gate))


def head_columns(sizes, head):
    heads, key_size, value_size = sizes
    base = 2 * heads * key_size
    return (
        slice(head * key_size, (head + 1) * key_size),
        slice((heads + head) * key_size, (heads + head + 1) * key_size),
        slice(base + head * value_size, base + (head + 1) * value_size),
    )


def side_columns(sizes):
    heads, key_size, value_size = sizes
    start = 2 * heads * (key_size + value_size)
    return slice(start, start + 128)


def local_kernel(
    sizes, projected_ref, resets_ref, border_ref, taps_ref, rate_ref, bias_ref,
    carried_ref, local_ref, map_ref, inverse_ref,
):
    heads, key_size, value_size = sizes
    size = projected_ref.shape[0]
    rows, cols = places(size)
    side, resets = projected_ref[:, side_columns(sizes)], resets_ref[:, 0:1]
    gates, queries, keys, values, mixing = [], [], [], [], []
    for head in range(heads):
        gate = Gates(side, resets, head, heads, rate_ref[head], bias_ref[head], rows, cols)
        summed = [
            conv_sum(jnp.concatenate([border_ref[:, at], projected_ref[:, at]], 0), taps_ref[:, at])
            for at in head_columns(sizes, head)
        ]
        gates.append(gate)
        queries.append(silu_unit(summed[0], key_size**-0.5)[3])
        keys.append(silu_unit(summed[1], 1.0)[3])
        values.append(summed[2] * sigmoid(summed[2]))
        split = halves(keys[head])
        gram = pair_dot(split, split, NT)
        mixing.append(gate.beta * jnp.where(rows > cols, gate.decays * gram, 0.0))
    inverses = [halves(part) for part in unit_lower_inverses(mixing, rows, cols)]
    krows, kcols = places(key_size)
    for head in range(heads):
        gate, query, key, value, inverse = (
            gates[head], queries[head], keys[head], values[head], inverses[head],
        )
        inverse_ref[head, 0] = inverse[0]
        inverse_ref[head, 1] = inverse[1]
        both = halves(
            pair_dot(
                inverse,
                halves(jnp.concatenate([(gate.beta * gate.head_decay) * key, gate.beta * value], 1)),
            )
        )
        scores = fine_dot(query, key, NT) * gate.decays
        read = pair_dot(halves(scores), both)
        carried_ref[:, head * key_size : (head + 1) * key_size] = (
            gate.head_decay * query - read[:, :key_size]
        )
        local_ref[:, head * value_size : (head + 1) * value_size] = read[:, key_size:]
        written = pair_dot(halves(key * gate.tail_decay), both, TN)
        kept = jnp.where(krows == kcols, gate.head_decay[size - 1 : size], 0.0)
        map_ref[head, :, :key_size] = kept - written[:, :key_size]
        map_ref[head, :, key_size:] = written[:, key_size:]


def pick(refs, index, head):
    value = refs[0][head]
    for at in range(1, len(refs)):
        value = jnp.where(index == at, refs[at][head], value)
    return value


def gate_kernel(sizes, count, order_ref, *refs):
    heads, key_size, value_size = sizes
    maps = refs[:count]
    (
        state_ref, carried_ref, local_ref, outgate_ref, gain_ref, gated_ref, output_ref, entry_ref, end_ref,
    ) = refs[count:]
    states = [state_ref[head] for head in range(heads)]
    entries = list(states)
    for at in range(count):
        index = order_ref[at]
        for head in range(heads):
            if at:
                entries[head] = jnp.where(index == 0, states[head], entries[head])
            step = pick(maps, index, head)
            states[head] = fine_dot(step[:, :key_size], states[head]) + step[:, key_size:]
    for head in range(heads):
        at = slice(head * value_size, (head + 1) * value_size)
        entry_ref[head] = entries[head]
        end_ref[head] = states[head]
        output = local_ref[:, at] + fine_dot(
            carried_ref[:, head * key_size : (head + 1) * key_size], entries[head]
        )
        output_ref[:, at] = output
        normed = output * lax.rsqrt(jnp.mean(output * output, 1, keepdims=True) + EPSILON)
        gate = outgate_ref[:, at]
        gated_ref[:, at] = (normed * gain_ref[...] * (gate * sigmoid(gate))).astype(LOW).astype(F32)


def gate_back_kernel(sizes, count, order_ref, *refs):
    heads, key_size, value_size = sizes
    pieces = refs[:count]
    (
        output_ref, outgate_ref, gain_ref, carried_ref,
        output_grad_ref, outgate_grad_ref, gain_grad_ref, entry_ref, grads,
    ) = refs[count:]
    part = pieces[0].shape[0]
    for at, piece in enumerate(pieces):
        grads[pl.ds(pl.multiple_of(order_ref[at] * part, part), part), :] = piece[...]
    gain = gain_ref[...]
    total = jnp.zeros_like(gain)
    for head in range(heads):
        at = slice(head * value_size, (head + 1) * value_size)
        grad, output, gate = grads[:, at], output_ref[:, at], outgate_ref[:, at]
        inverse = lax.rsqrt(jnp.mean(output * output, 1, keepdims=True) + EPSILON)
        unit = output * inverse
        opened = sigmoid(gate)
        swished = gate * opened
        outgate_grad_ref[:, at] = (
            grad * unit * gain * (opened * (1.0 + gate * (1.0 - opened)))
        ).astype(LOW)
        total = total + jnp.sum(grad * unit * swished, 0, keepdims=True)
        unit_grad = grad * gain * swished
        output_grad = inverse * (unit_grad - unit * jnp.mean(unit_grad * unit, 1, keepdims=True))
        output_grad_ref[:, at] = output_grad
        entry_ref[head] = fine_dot(
            carried_ref[:, head * key_size : (head + 1) * key_size], output_grad, TN
        )
    gain_grad_ref[...] = total


def mix_back_kernel(count, target_ref, grad_ref, mixed_ref, top_ref, gain_ref, weight_ref, sum_ref, *refs):
    values, grad = mixed_ref[...], grad_ref[...]
    inverse = lax.rsqrt(jnp.mean(values * values, 1, keepdims=True) + EPSILON)
    unit = values * inverse
    scaled = grad * gain_ref[...]
    mixed_grad = top_ref[...] + inverse * (scaled - unit * jnp.mean(unit * scaled, 1, keepdims=True))
    refs[0][...] = mixed_grad
    sum_ref[...] = jnp.sum(unit * grad, 0, keepdims=True)
    low = mixed_grad.astype(LOW)
    part = weight_ref.shape[0] // count
    for at in range(count):
        place = pl.multiple_of(target_ref[at] * part, part)
        refs[1 + at][...] = low_dot(low, weight_ref[pl.ds(place, part), :], NT)


def local_back_kernel(sizes, count, order_ref, *refs):
    heads, key_size, value_size = sizes
    maps, entries = refs[:count], refs[count : 2 * count]
    (
        state_grad_ref, projected_ref, resets_ref, border_ref, taps_ref, rate_ref, bias_ref,
        inverse_ref, entry_state_ref, output_grad_ref,
        conv_grad_ref, border_grad_ref, taps_grad_ref, side_grad_ref, sums_ref, start_grad_ref,
    ) = refs[2 * count :]
    size = projected_ref.shape[0]
    scale = key_size**-0.5
    state_grads = [state_grad_ref[head] for head in range(heads)]
    end_grads = list(state_grads)
    for at in reversed(range(count)):
        index = order_ref[at]
        for head in range(heads):
            if at < count - 1:
                end_grads[head] = jnp.where(index == 0, state_grads[head], end_grads[head])
            step = pick(maps, index, head)[:, :key_size]
            state_grads[head] = fine_dot(step, state_grads[head], TN) + pick(entries, index, head)
    rows, cols = places(size)
    strict = rows > cols
    lower = jnp.where(rows >= cols, 1.0, 0.0).astype(LOW)
    lanes = lax.broadcasted_iota(jnp.int32, (size, 128), 1)
    at_row = lax.broadcasted_iota(jnp.int32, (size, 1), 0)
    sum_lanes = lax.broadcasted_iota(jnp.int32, (8, 128), 1)
    sum_rows = lax.broadcasted_iota(jnp.int32, (8, 128), 0)
    side, resets = projected_ref[:, side_columns(sizes)], resets_ref[:, 0:1]
    side_grad = jnp.zeros((size, 128), F32)
    sums = jnp.zeros((8, 128), F32)
    for head in range(heads):
        start_grad_ref[head] = state_grads[head]
        gate = Gates(side, resets, head, heads, rate_ref[head], bias_ref[head], rows, cols)
        columns = head_columns(sizes, head)
        padded = [jnp.concatenate([border_ref[:, at], projected_ref[:, at]], 0) for at in columns]
        summed = [conv_sum(part, taps_ref[:, at]) for part, at in zip(padded, columns)]
        act_q, gate_q, inverse_q, query = silu_unit(summed[0], scale)
        act_k, gate_k, inverse_k, key = silu_unit(summed[1], 1.0)
        gate_v = sigmoid(summed[2])
        value = summed[2] * gate_v
        beta, decays, head_decay, tail_decay = gate.beta, gate.decays, gate.head_decay, gate.tail_decay
        end_grad, state = end_grads[head], entry_state_ref[head]
        inverse = (inverse_ref[head, 0], inverse_ref[head, 1])
        output_grad = halves(output_grad_ref[:, head * value_size : (head + 1) * value_size])
        query_s, key_s, state_s, end_s = halves(query), halves(key), halves(state), halves(end_grad)

        gram = pair_dot(key_s, key_s, NT)
        pure = pair_dot(query_s, key_s, NT)
        residue = value - head_decay * pair_dot(key_s, state_s)
        update = halves(pair_dot(inverse, halves(beta * residue)))
        update_grad = pair_dot(halves(pure * decays), output_grad, TN) + pair_dot(
            halves(key * tail_decay), end_s
        )
        target_grad = pair_dot(inverse, halves(update_grad), TN)
        target_s = halves(target_grad)
        weighted = jnp.where(strict, -pair_dot(target_s, update, NT), 0.0) * decays
        pure_grad = pair_dot(output_grad, update, NT) * decays
        reached = pair_dot(output_grad, state_s, NT)
        erased = pair_dot(target_s, state_s, NT)
        kept = pair_dot(update, end_s, NT)
        gram_grad = weighted * beta
        pure_s, gram_s = halves(pure_grad), halves(gram_grad)
        query_grad = head_decay * reached + pair_dot(pure_s, key_s)
        key_grad = (
            pair_dot(pure_s, query_s, TN)
            + tail_decay * kept
            - (beta * head_decay) * erased
            + pair_dot(gram_s, key_s)
            + pair_dot(gram_s, key_s, TN)
        )
        value_grad = beta * target_grad
        beta_grad = jnp.sum(target_grad * residue, 1, keepdims=True) + jnp.sum(
            weighted * gram, 1, keepdims=True
        )
        spread = pure_grad * pure + gram_grad * gram
        head_decay_grad = jnp.sum(query * reached, 1, keepdims=True) - beta * jnp.sum(
            key * erased, 1, keepdims=True
        )
        tail_part = tail_decay * jnp.sum(key * kept, 1, keepdims=True)
        spread_s = jnp.concatenate(thirds(spread), 0)
        column_sums = low_dot(spread_s, jnp.ones((3 * size, 128), LOW), TN)[:, 0:1]
        total_grad = (
            head_decay * head_decay_grad - tail_part + jnp.sum(spread, 1, keepdims=True) - column_sums
        )
        last_grad = jnp.sum(tail_part, 0, keepdims=True) + head_decay[size - 1 : size] * jnp.sum(
            jnp.sum(end_grad * state, 1, keepdims=True), 0, keepdims=True
        )
        total_grad = total_grad + jnp.where(at_row == size - 1, last_grad, 0.0)
        total_s = jnp.concatenate(thirds(jnp.where(lanes == 0, total_grad, 0.0)), 0)
        log_grad = low_dot(jnp.concatenate([lower] * 3, 0), total_s, TN)[:, 0:1]
        decay_grad = log_grad * (-gate.rate) * sigmoid(gate.shifted)
        beta_in_grad = beta_grad * beta * (1.0 - beta)
        side_grad = jnp.where(
            lanes == head, decay_grad, jnp.where(lanes == heads + head, beta_in_grad, side_grad)
        )
        log_sum = jnp.sum(log_grad * gate.log_decay, 0, keepdims=True)
        bias_sum = jnp.sum(decay_grad, 0, keepdims=True)
        sums = jnp.where(
            (sum_lanes == head) & (sum_rows == 0),
            log_sum,
            jnp.where((sum_lanes == head) & (sum_rows == 1), bias_sum, sums),
        )
        grads = (
            silu_unit_back(query_grad, summed[0], gate_q, act_q, inverse_q, scale),
            silu_unit_back(key_grad, summed[1], gate_k, act_k, inverse_k, 1.0),
            value_grad * gate_v * (1.0 + summed[2] * (1.0 - gate_v)),
        )
        for grad, part, at in zip(grads, padded, columns):
            spread_out = conv_transposed(grad, taps_ref[:, at])
            border_grad_ref[:, at] = spread_out[:8]
            conv_grad_ref[:, at] = spread_out[8:]
            taps_grad_ref[:, at] = conv_taps_grad(part, grad, taps_ref.shape[0])
    side_grad_ref[...] = side_grad.astype(LOW)
    sums_ref[...] = sums


def smem():
    return pl.BlockSpec(memory_space=pltpu.SMEM)


def anywhere():
    return pl.BlockSpec(memory_space=pl.ANY)


def call(kernel, out_shape, operands, name, micros, in_specs=None, scratch=(), vmem=VMEM_BYTES):
    whole = lambda array: pl.BlockSpec(array.shape, lambda i: (0,) * len(array.shape))
    specs = [whole(array) for array in operands] if in_specs is None else in_specs
    specs = [whole(array) if spec is None else spec for spec, array in zip(specs, operands)]
    return pl.pallas_call(
        kernel,
        grid=(1,),
        in_specs=specs,
        out_specs=[whole(array) for array in out_shape],
        out_shape=out_shape,
        scratch_shapes=list(scratch),
        compiler_params=pltpu.CompilerParams(vmem_limit_bytes=vmem),
        cost_estimate=pl.CostEstimate(
            flops=int(micros * 3e+08), bytes_accessed=int(micros * 900000), transcendentals=0
        ),
        name=name,
    )(*operands)


def shape(dims, dtype=F32):
    return jax.ShapeDtypeStruct(tuple(dims), dtype)


def columns_spec(rows, width, at):
    return pl.BlockSpec((rows, width), lambda i: (0, at))


def mixer_local(sizes, projected, resets, border, taps, rate, bias):
    heads, key_size, value_size = sizes
    rows = projected.shape[0]
    return call(
        partial(local_kernel, sizes),
        [
            shape((rows, heads * key_size)),
            shape((rows, heads * value_size)),
            shape((heads, key_size, key_size + value_size)),
            shape((heads, 2, rows, rows), LOW),
        ],
        [projected, resets, border, taps, rate, bias],
        "mixer_local",
        12,
        [None, None, None, None, smem(), smem()],
    )


def mixer_gate(sizes, order, maps, state, carried, local, projected, gain):
    heads, key_size, value_size = sizes
    rows = projected.shape[0]
    count = len(maps)
    value_cols = heads * value_size
    outgate = columns_spec(rows, value_cols, (2 * heads * key_size + value_cols) // value_cols)
    return call(
        partial(gate_kernel, sizes, count),
        [
            shape((rows, value_cols)),
            shape((rows, value_cols)),
            shape((heads, key_size, value_size)),
            shape((heads, key_size, value_size)),
        ],
        [order, *maps, state, carried, local, projected, gain],
        "mixer_gate",
        5,
        [smem()] + [None] * (count + 3) + [outgate, None],
    )


def mix_back(target, grad, mixed, top, gain, weight):
    rows, width = grad.shape
    count = target.shape[0]
    return call(
        partial(mix_back_kernel, count),
        [shape((1, width)), shape((rows, width))] + [shape((rows, weight.shape[0] // count))] * count,
        [target, grad, mixed, top, gain, weight],
        "mix_back",
        5,
        [smem()] + [None] * 5,
    )


def mixer_gate_back(sizes, order, pieces, output, projected, gain, carried):
    heads, key_size, value_size = sizes
    rows = projected.shape[0]
    count = len(pieces)
    value_cols = heads * value_size
    outgate = columns_spec(rows, value_cols, (2 * heads * key_size + value_cols) // value_cols)
    return call(
        partial(gate_back_kernel, sizes, count),
        [
            shape((rows, value_cols)),
            shape((rows, value_cols), LOW),
            shape((1, value_size)),
            shape((heads, key_size, value_size)),
        ],
        [order, *pieces, output, projected, gain, carried],
        "mixer_gate_back",
        4,
        [smem()] + [None] * (count + 1) + [outgate, None, None],
        [pltpu.VMEM((rows, value_cols), F32)],
    )


def mixer_local_back(
    sizes, order, maps, entries, state_grad, projected, resets, border, taps, rate, bias, inverse,
    entry_state, output_grad,
):
    heads, key_size, value_size = sizes
    rows = projected.shape[0]
    count = len(maps)
    conv_cols = taps.shape[1]
    return call(
        partial(local_back_kernel, sizes, count),
        [
            shape((rows, conv_cols)),
            shape((8, conv_cols)),
            shape(taps.shape),
            shape((rows, 128), LOW),
            shape((8, 128)),
            shape((heads, key_size, value_size)),
        ],
        [
            order, *maps, *entries, state_grad, projected, resets, border, taps, rate, bias, inverse,
            entry_state, output_grad,
        ],
        "mixer_local_back",
        12,
        [smem()] + [None] * (2 * count + 5) + [smem(), smem(), None, None, None],
    )


def recast_kernel(index_ref, source_ref, *refs):
    refs[-1][...] = source_ref[...].astype(refs[-1].dtype)


def widen(values):
    rows, cols = values.shape
    tile = min(rows, 256)
    spec = pl.BlockSpec((tile, cols), lambda i, index: (i, 0))
    return pl.pallas_call(
        recast_kernel,
        grid_spec=pltpu.PrefetchScalarGridSpec(
            num_scalar_prefetch=1, grid=(rows // tile,), in_specs=[spec], out_specs=spec
        ),
        out_shape=shape((rows, cols)),
        name="widen",
    )(jnp.zeros((1,), jnp.int32), values)


def narrow_into(whole, values, index, total, member, members, pieces):
    rows, cols = values.shape
    tile = rows // pieces
    source = pl.BlockSpec((tile, cols), lambda i, index: (i, 0))
    placed = pl.BlockSpec((tile, cols), lambda i, index: (i * members + member, index[0]))
    more = [] if whole is None else [whole]
    return pl.pallas_call(
        recast_kernel,
        grid_spec=pltpu.PrefetchScalarGridSpec(
            num_scalar_prefetch=1,
            grid=(pieces,),
            in_specs=[source] + [anywhere()] * len(more),
            out_specs=placed,
        ),
        out_shape=shape((rows * members, total), LOW),
        input_output_aliases={2: 0} if more else {},
        name="narrow_into",
    )(index, values, *more)


def enter_kernel(rows_ref, gain_ref, weight_ref, hidden_ref, projected_ref):
    values = rows_ref[...]
    inverse = lax.rsqrt(jnp.mean(values * values, 1, keepdims=True) + EPSILON)
    hidden = (values * inverse * gain_ref[...]).astype(LOW)
    hidden_ref[...] = hidden
    projected_ref[...] = low_dot(hidden, weight_ref[...])


def enter(rows, gain, weight):
    count, width = rows.shape
    return call(
        enter_kernel,
        [shape((count, width), LOW), shape((count, weight.shape[1]))],
        [rows, gain, weight],
        "enter",
        6,
    )


def join_kernel(
    rows_ref, gated_ref, weight_ref, gain_ref, gate_hbm, up_hbm, down_hbm,
    mixed_ref, hidden_ref, gate_ref, up_ref, inner_ref, sums_ref,
    gate_weight, up_weight, down_weight, arrived,
):
    copies = [
        pltpu.make_async_copy(source, target, arrived.at[at])
        for at, (source, target) in enumerate(
            ((gate_hbm, gate_weight), (up_hbm, up_weight), (down_hbm, down_weight))
        )
    ]
    for copy in copies:
        copy.start()
    depth = gated_ref.shape[2]
    mixed = rows_ref[...]
    for part in range(gated_ref.shape[0]):
        mixed = mixed + low_dot(
            gated_ref[part].astype(LOW), weight_ref[part * depth : (part + 1) * depth, :]
        )
    mixed_ref[...] = mixed
    inverse = lax.rsqrt(jnp.mean(mixed * mixed, 1, keepdims=True) + EPSILON)
    hidden = (mixed * inverse * gain_ref[...]).astype(LOW)
    hidden_ref[...] = hidden
    copies[0].wait()
    gate = low_dot(hidden, gate_weight[...])
    gate_ref[...] = gate
    copies[1].wait()
    up = low_dot(hidden, up_weight[...])
    up_ref[...] = up
    inner = (gate * sigmoid(gate) * up).astype(LOW)
    inner_ref[...] = inner
    copies[2].wait()
    sums_ref[...] = low_dot(inner, down_weight[...])


def join_heads(rows, gated, weight, gain, gate_weight, up_weight, down_weight):
    count, width = rows.shape
    hidden = gate_weight.shape[1]
    return call(
        join_kernel,
        [
            shape((count, width)),
            shape((count, width), LOW),
            shape((count, hidden)),
            shape((count, hidden)),
            shape((count, hidden), LOW),
            shape((count, width)),
        ],
        [rows, gated, weight, gain, gate_weight, up_weight, down_weight],
        "join_heads",
        12,
        [None] * 4 + [anywhere()] * 3,
        [
            pltpu.VMEM(gate_weight.shape, LOW),
            pltpu.VMEM(up_weight.shape, LOW),
            pltpu.VMEM(down_weight.shape, LOW),
            pltpu.SemaphoreType.DMA((3,)),
        ],
        56 * 1024 * 1024,
    )


def feed_back_kernel(
    last_ref, given_ref, handed_ref, gate_ref, up_ref, gate_hbm, up_hbm, down_hbm,
    top_ref, gate_grad_ref, up_grad_ref, sums_ref, gate_weight, up_weight, down_weight, arrived,
):
    copies = [
        pltpu.make_async_copy(source, target, arrived.at[at])
        for at, (source, target) in enumerate(
            ((down_hbm, down_weight), (gate_hbm, gate_weight), (up_hbm, up_weight))
        )
    ]
    for copy in copies:
        copy.start()
    top = jnp.where(last_ref[0] == 1, given_ref[...].astype(F32), handed_ref[...]).astype(LOW)
    top_ref[...] = top
    copies[0].wait()
    grad = low_dot(top, down_weight[...], NT)
    gate = gate_ref[...]
    opened = sigmoid(gate)
    gate_grad = (grad * up_ref[...] * (opened * (1.0 + gate * (1.0 - opened)))).astype(LOW)
    up_grad = (grad * gate * opened).astype(LOW)
    gate_grad_ref[...] = gate_grad
    up_grad_ref[...] = up_grad
    copies[1].wait()
    sums = low_dot(gate_grad, gate_weight[...], NT)
    copies[2].wait()
    sums_ref[...] = sums + low_dot(up_grad, up_weight[...], NT)


def feed_back(last, given, handed, gate_act, up_act, gate_weight, up_weight, down_weight):
    count, width = given.shape
    hidden = gate_weight.shape[1]
    return call(
        feed_back_kernel,
        [
            shape((count, width), LOW),
            shape((count, hidden), LOW),
            shape((count, hidden), LOW),
            shape((count, width)),
        ],
        [last, given, handed, gate_act, up_act, gate_weight, up_weight, down_weight],
        "feed_back",
        12,
        [smem()] + [None] * 4 + [anywhere()] * 3,
        [
            pltpu.VMEM(gate_weight.shape, LOW),
            pltpu.VMEM(up_weight.shape, LOW),
            pltpu.VMEM(down_weight.shape, LOW),
            pltpu.SemaphoreType.DMA((3,)),
        ],
    )


def leave_kernel(conv_ref, tail_ref, outgate_ref, side_ref, weight_ref, low_ref, sums_ref):
    rows, conv_cols = conv_ref.shape
    conv = conv_ref[...]
    conv = jnp.concatenate([conv[: rows - 8], conv[rows - 8 :] + tail_ref[...]], 0)
    low = jnp.concatenate([conv.astype(LOW), outgate_ref[...], side_ref[...]], 1)
    low_ref[...] = low
    sums_ref[...] = low_dot(low, weight_ref[...], NT)


def leave(conv, tail, outgate, side, weight):
    count, width = conv.shape[0], weight.shape[0]
    return call(
        leave_kernel,
        [shape((count, weight.shape[1]), LOW), shape((count, width))],
        [conv, tail, outgate, side, weight],
        "leave",
        7,
    )


def row_norm_back(values, gain, grad):
    inverse = lax.rsqrt(jnp.mean(values * values, -1, keepdims=True) + EPSILON)
    unit = values * inverse
    scaled = grad * gain
    back = inverse * (scaled - unit * jnp.mean(unit * scaled, -1, keepdims=True))
    return back, jnp.sum(unit * grad, 0)


def ring(value, axis, steps):
    count = lax.axis_size(axis)
    return lax.ppermute(value, axis, [(at, (at + steps) % count) for at in range(count)])


def all_seq(value):
    return [value] + [ring(value, "seq", step) for step in range(1, lax.axis_size("seq"))]


def handed_on(value, axis, steps):
    count = lax.axis_size(axis)
    first, last = max(0, -steps), min(count, count - steps)
    return lax.ppermute(value, axis, [(at, at + steps) for at in range(first, last)])


def gather_tp(values):
    return lax.all_gather(values, "tp", axis=0, tiled=True)


def scatter_tp(values):
    return lax.psum_scatter(values, "tp", scatter_dimension=0, tiled=True)


def crossed(value, bit):
    return lax.ppermute(value, "seq", [(at, at ^ bit) for at in range(lax.axis_size("seq"))])


def butterfly(value, axis):
    count = lax.axis_size(axis)
    step = 1
    while step < count:
        value = value + lax.ppermute(value, axis, [(at, at ^ step) for at in range(count)])
        step *= 2
    return value


def core_sums(left, right, axis):
    count = lax.axis_size("seq")
    chunk = (left, right)[axis].shape[1] // count
    index = lax.axis_index("seq")
    core, chip, chips = index % 2, index // 2, count // 2

    def product(chip, core):
        place = (chip * 2 + core) * chunk
        if axis:
            return low_dot(left, lax.dynamic_slice_in_dim(right, place, chunk, 1), TN)
        return low_dot(lax.dynamic_slice_in_dim(left, place, chunk, 1), right, TN)

    order = [(chip + step) % chips for step in range(1, chips)] + [chip]
    received = [crossed(product(at, 1 - core), 1) for at in order]
    return [product(at, core) + part for at, part in zip(order, received)]


def chip_sums(parts):
    total = parts[-1]
    for step, part in enumerate(parts[:-1], 1):
        total = total + ring(part, "seq", 2 * step)
    return total


def after(value, *others):
    return lax.optimization_barrier((value, *others))[0]


def local(
    inputs, cotangent, doc_start, norm_in, query_weight, key_weight, value_weight, outgate_weight,
    decay_weight, beta_weight, conv_query, conv_key, conv_value, decay_log, decay_bias, head_norm,
    out_weight, norm_feed, gate_weight, up_weight, down_weight,
):
    query_weight, key_weight, value_weight = query_weight[0], key_weight[0], value_weight[0]
    outgate_weight, decay_weight, beta_weight = outgate_weight[0], decay_weight[0], beta_weight[0]
    gate_weight, up_weight, down_weight, out_weight = (
        gate_weight[0], up_weight[0], down_weight[0], out_weight[0],
    )
    taps = jnp.concatenate([conv_query[0], conv_key[0], conv_value[0]], 1)
    rate, bias = jnp.exp(decay_log[0]), decay_bias[0]
    heads = bias.shape[0]
    key_size = query_weight.shape[1] // heads
    value_size = value_weight.shape[1] // heads
    sizes = (heads, key_size, value_size)
    key_cols, value_cols = heads * key_size, heads * value_size
    micros, own_rows, width = inputs.shape
    rows = cotangent.shape[1]
    seq_size, seq_index = lax.axis_size("seq"), lax.axis_index("seq")
    tp_index = lax.axis_index("tp")
    section = lax.axis_index("section")
    at_start, at_end = seq_index == 0, seq_index == seq_size - 1
    order = (seq_index - jnp.arange(seq_size, dtype=jnp.int32)) % seq_size
    tp_size = lax.axis_size("tp")
    sources = (tp_index - jnp.arange(tp_size, dtype=jnp.int32)) % tp_size
    targets = (tp_index + jnp.arange(tp_size, dtype=jnp.int32)) % tp_size
    last_section = section.astype(jnp.int32).reshape(1)
    group = GROUP if micros % GROUP == 0 else 1
    groups = micros // group

    def own(values):
        return lax.dynamic_slice_in_dim(values, tp_index * own_rows, own_rows, 0)

    def whole_out_weight(whole, piece, member, members):
        for step in range(0, seq_size, 2):
            moved = ring(piece, "seq", step) if step else piece
            for at, values in (
                ((seq_index - step) % seq_size, moved),
                (((seq_index ^ 1) - step) % seq_size, crossed(moved, 1)),
            ):
                if whole is not None:
                    values = after(values, whole)
                whole = narrow_into(
                    whole, values, at.astype(jnp.int32).reshape(1), width, member, members, tp_size
                )
        return whole

    spare = jnp.zeros((width, 128 - 2 * heads), LOW)
    in_weight = jnp.concatenate(
        [query_weight, key_weight, value_weight, outgate_weight, decay_weight, beta_weight, spare], 1
    )
    conv_cols = 2 * key_cols + value_cols
    offsets = jnp.arange(rows, dtype=jnp.int32)

    def micro_of(step, member):
        return jnp.clip(step - section, 0, groups - 1) * group + member

    def reset_flags(micro):
        starts = micro * (rows * seq_size) + seq_index * rows + offsets
        flags = lax.dynamic_index_in_dim(doc_start, micro, 0, keepdims=False) == starts
        return jnp.broadcast_to(flags.astype(F32)[:, None], (rows, 128))

    def mix(residual, step, member, border_carry):
        micro = micro_of(step, member)
        hidden, projected = enter(residual, norm_in, in_weight)
        moved = ring(projected[rows - 8 :, :conv_cols], "seq", 1)
        border = jnp.where(at_start, border_carry, moved)
        resets = reset_flags(micro)
        carried, local_out, maps, inverse = mixer_local(
            sizes, projected, resets, border, taps, rate, bias
        )
        saved[step, member] = dict(
            hidden=hidden, border=border, projected=projected, resets=resets, carried=carried,
            maps=all_seq(maps), inverse=inverse,
        )
        return moved, local_out

    def gate(step, member, local_out, state):
        kept = saved[step, member]
        kept["gated"], kept["output"], kept["entry_state"], state = mixer_gate(
            sizes, order, kept["maps"], state, kept["carried"], local_out, kept["projected"], head_norm
        )
        return state

    def rows_outer(name):
        return jnp.concatenate(
            [
                jnp.where(section == 0, saved[0, member][name], saved[groups, member][name])
                for member in range(group)
            ],
            0,
        )

    def rows_inner(name):
        return jnp.concatenate(
            [saved[at, member][name] for at in range(1, groups) for member in range(group)], 0
        )

    def all_rows(name):
        return jnp.concatenate([rows_outer(name), rows_inner(name)], 0)

    saved = {}
    section_rows = {}
    part = width // seq_size
    entering = [inputs[member].astype(F32) * (section == 0) for member in range(group)]
    residuals = [gather_tp(values) for values in entering]
    out_piece = widen(lax.dynamic_slice_in_dim(out_weight, seq_index * part, part, 1))
    out_pieces = [
        gather_tp(after(values, *entering)) for values in jnp.split(out_piece, 2, 0)
    ]
    out_full = None
    border_carry = jnp.zeros((8, conv_cols), F32)
    state = jnp.zeros((heads, key_size, value_size), F32)
    late_sums = []
    for step in range(groups + 1):
        all_gated = []
        last = None
        for member in range(group):
            residual = residuals[member] if last is None else after(residuals[member], last)
            border_carry, local_out = mix(residual, step, member, border_carry)
            if step == groups and all_gated:
                local_out = after(local_out, all_gated[-1])
            state = gate(step, member, local_out, state)
            last = saved[step, member]["gated"]
            saved[step, member]["entering"] = entering[member]
            residuals[member] = residual
            all_gated.append(lax.all_gather(last, "tp", axis=0))
        if out_full is None:
            for member, piece in enumerate(out_pieces):
                out_full = whole_out_weight(out_full, after(piece, last), member, 2)
        next_entering, next_residuals = [], []
        all_sums = []
        for member in range(group):
            kept = saved[step, member]
            mixed, kept["hidden_feed"], kept["gate_act"], kept["up_act"], kept["inner"], sums = join_heads(
                residuals[member], after(all_gated[member], last), out_full, norm_feed,
                gate_weight, up_weight, down_weight,
            )
            kept["mixed"] = own(mixed)
            all_sums.append(scatter_tp(sums) if step < groups else sums)
        if step == groups:
            late_sums = all_sums
            break
        ready = None
        for member in range(group):
            summed = all_sums[member] if ready is None else after(all_sums[member], ready)
            out_rows = saved[step, member]["mixed"] + summed
            section_rows[step, member] = out_rows
            handed = handed_on(out_rows, "section", 1)
            micro = micro_of(step + 1, member)
            given = lax.dynamic_index_in_dim(inputs, micro, 0, keepdims=False).astype(F32)
            ready = jnp.where(section == 0, given, handed)
            next_entering.append(ready)
            next_residuals.append(gather_tp(ready))
        entering, residuals = next_entering, next_residuals

    nothing = jnp.zeros((rows, width), F32)
    tail_carry = jnp.zeros((8, conv_cols), F32)
    state_grad = jnp.zeros((heads, key_size, value_size), F32)
    in_grads = {}
    norm_in_grad = jnp.zeros((width,), F32)
    norm_feed_grad = jnp.zeros((width,), F32)
    gain_grad = jnp.zeros((value_size,), F32)
    taps_grad = jnp.zeros(taps.shape, F32)
    side_sums = jnp.zeros((8, 128), F32)
    received = [jnp.zeros((own_rows, width), F32)] * group
    handed = [nothing] * group
    members = list(reversed(range(group)))
    for back_step in range(groups + 1):
        step = groups - back_step
        tops, feed_grads = {}, {}
        for member in members:
            kept = saved[step, member]
            given = lax.dynamic_index_in_dim(cotangent, micro_of(step, member), 0, keepdims=False)
            if step == 0:
                given = jnp.where(section == 0, given, jnp.zeros_like(given))
            kept["top_low"], kept["gate_low"], kept["up_low"], sums = feed_back(
                last_section, given, handed[member], kept["gate_act"], kept["up_act"],
                gate_weight, up_weight, down_weight,
            )
            tops[member] = jnp.where(section == 0, received[member], own(given).astype(F32))
            if back_step < groups:
                feed_grads[member] = scatter_tp(sums)
            else:
                summed = scatter_tp(jnp.where(section == 0, sums, late_sums[member]))
                section_rows[groups, member] = saved[groups, member]["mixed"] + summed
                feed_grads[member] = jnp.where(section == 0, summed, 0.0)
        if back_step == groups:
            feed_all, top_all = all_rows("hidden_feed"), all_rows("top_low")
            gate_parts = core_sums(feed_all, all_rows("gate_low"), 0)
            feed_grads[members[0]] = after(feed_grads[members[0]], *gate_parts)
            up_parts = core_sums(feed_all, all_rows("up_low"), 0)
            feed_grads[members[-1]] = after(feed_grads[members[-1]], *up_parts)
        last = None
        all_sums = {}
        for member in members:
            kept = saved[step, member]
            feed_grad = feed_grads[member] if last is None else after(feed_grads[member], conv_grad)
            feed_part, mixed_grad, *pieces = mix_back(
                targets, feed_grad, kept["mixed"], tops[member], norm_feed, out_full
            )
            kept["mixed_grad"] = mixed_grad
            norm_feed_grad = norm_feed_grad + feed_part[0]
            pieces = [ring(piece, "tp", at) if at else piece for at, piece in enumerate(pieces)]
            if last is not None:
                pieces[0] = after(pieces[0], last)
            output_grad, outgate_low, gain_part, entry_grad = mixer_gate_back(
                sizes, sources, pieces, kept["output"], kept["projected"], head_norm, kept["carried"]
            )
            gain_grad = gain_grad + gain_part[0]
            conv_grad, border_grad, taps_part, side_low, sums_part, state_grad = mixer_local_back(
                sizes, order, kept["maps"], all_seq(entry_grad), state_grad, kept["projected"],
                kept["resets"], kept["border"], taps, rate, bias, kept["inverse"],
                kept["entry_state"], output_grad,
            )
            moved = ring(border_grad, "seq", -1)
            tail = jnp.where(at_end, tail_carry, moved)
            tail_carry = moved
            if back_step == groups and member == members[0]:
                grad_gate = chip_sums([after(part, tail) for part in gate_parts])
            elif back_step == groups and member == members[-1]:
                tail = after(tail, grad_gate, all_sums[members[0]])
            taps_grad = taps_grad + taps_part
            side_sums = side_sums + sums_part
            kept["projected_low"], last = leave(conv_grad, tail, outgate_low, side_low, in_weight)
            all_sums[member] = scatter_tp(last)
            if back_step == groups and member == members[0]:
                inner_mixed = gather_tp(after(rows_inner("mixed_grad"), last))
        ready = None
        received, handed = [None] * group, [None] * group
        if back_step == groups:
            outer_mixed = gather_tp(after(rows_outer("mixed_grad"), last))
            in_parts = core_sums(all_rows("hidden"), all_rows("projected_low"), 0)
            down_parts = core_sums(after(all_rows("inner"), in_parts[0]), top_all, 1)
            grad_up = chip_sums([after(part, tail) for part in up_parts])
            inner_mixed = narrow_into(
                None, after(inner_mixed, grad_up, down_parts[0]), jnp.zeros((1,), jnp.int32), width, 0, 1, tp_size
            )
            ready = inner_mixed
        for member in members:
            kept = saved[step, member]
            summed = all_sums[member]
            if ready is not None and (back_step < groups or member == members[-1]):
                summed = after(summed, ready)
            entering_back, in_part = row_norm_back(kept["entering"], norm_in[0], summed)
            norm_in_grad = norm_in_grad + in_part
            own_grad = kept["mixed_grad"] + entering_back
            in_grads[step, member] = own_grad
            if back_step < groups:
                ready = handed_on(own_grad, "section", -1)
                received[member] = ready
                handed[member] = gather_tp(ready)
    def of_section(values):
        return [
            jnp.where(section == 0, values[at, member], values[at + 1, member])
            for at in range(groups)
            for member in range(group)
        ]

    grad_in = chip_sums([after(part, tail) for part in in_parts])
    grad_down = chip_sums([after(part, tail) for part in down_parts])
    outer_mixed = after(outer_mixed, grad_in)
    zero = jnp.zeros((1,), jnp.int32)

    def by_device(name, rows_of, count):
        split = rows_of(name).astype(LOW).reshape(count, tp_size, own_rows, value_cols)
        return jnp.moveaxis(split, 0, 1).reshape(count * rows, value_cols)

    mixed_all = jnp.concatenate(
        [narrow_into(None, outer_mixed, zero, width, 0, 1, tp_size), inner_mixed], 0
    )
    gated_all = jnp.concatenate(
        [by_device("gated", rows_outer, group), by_device("gated", rows_inner, micros - group)], 0
    )
    out_parts = core_sums(gated_all, mixed_all, 1)
    grad_out = chip_sums(out_parts)

    shared = butterfly(jnp.concatenate([norm_in_grad, norm_feed_grad, gain_grad]), "tp")
    small = butterfly(
        jnp.concatenate(
            [
                after(shared, out_parts[0]), taps_grad.reshape(-1), side_sums[0, :heads],
                side_sums[1, :heads],
            ]
        ),
        "seq",
    )
    bounds = [0, width, 2 * width, 2 * width + value_size]
    bounds += [bounds[-1] + taps.size, bounds[-1] + taps.size + heads, bounds[-1] + taps.size + 2 * heads]
    norm_in_grad, norm_feed_grad, gain_grad, taps_grad, log_grad, bias_grad = [
        small[low:high] for low, high in zip(bounds[:-1], bounds[1:])
    ]
    taps_grad = taps_grad.reshape(taps.shape)
    bounds = [
        0, key_cols, 2 * key_cols, conv_cols, conv_cols + value_cols, conv_cols + value_cols + heads,
        conv_cols + value_cols + 2 * heads,
    ]
    in_parts = [grad_in[:, low:high] for low, high in zip(bounds[:-1], bounds[1:])]
    return (
        jnp.stack(of_section(section_rows))[None],
        jnp.stack(of_section(in_grads))[None],
        norm_in_grad[None],
        *[member[None] for member in in_parts],
        taps_grad[None, :, :key_cols],
        taps_grad[None, :, key_cols : 2 * key_cols],
        taps_grad[None, :, 2 * key_cols :],
        log_grad[None],
        bias_grad[None],
        gain_grad[None],
        grad_out[None],
        norm_feed_grad[None],
        grad_gate[None],
        grad_up[None],
        grad_down[None],
    )


def solution(mesh):
    by_column, by_row = P("section", None, "tp"), P("section", "tp", None)
    placed = (
        P(None, ("seq", "tp"), None),
        P(None, "seq", None),
        P(None, "seq"),
        P("section", None),
        *[by_column] * 9,
        P("section", "tp"),
        P("section", "tp"),
        P("section", None),
        by_row,
        P("section", None),
        by_column,
        by_column,
        by_row,
    )
    rows_out = P("section", None, ("seq", "tp"), None)
    both = P("section", "seq", "tp")
    return jax.shard_map(
        local,
        mesh=mesh,
        in_specs=placed,
        out_specs=(
            rows_out,
            rows_out,
            P("section", None),
            *[both] * 6,
            *[by_column] * 3,
            P("section", "tp"),
            P("section", "tp"),
            P("section", None),
            P("section", "tp", "seq"),
            P("section", None),
            both,
            both,
            P("section", "tp", "seq"),
        ),
        check_vma=False,
    )
```

```python
from functools import partial

import jax
import jax.numpy as jnp
from jax import lax
from jax.experimental import pallas as pl
from jax.experimental.pallas import tpu as pltpu
from jax.sharding import PartitionSpec as P

EPSILON = 1e-06
F32 = jnp.float32
LOW = jnp.bfloat16
VMEM_BYTES = 48 * 1024 * 1024
NN = ((1,), (0,))
NT = ((1,), (1,))
TN = ((0,), (0,))


def low_dot(a, b, contract=NN):
    return lax.dot_general(a, b, (contract, ((), ())), preferred_element_type=F32)


def halves(x):
    high = x.astype(LOW)
    return high, (x - high.astype(F32)).astype(LOW)


def thirds(x):
    high = x.astype(LOW)
    rest = x - high.astype(F32)
    middle = rest.astype(LOW)
    return high, middle, (rest - middle.astype(F32)).astype(LOW)


def pair_dot(a, b, contract=NN):
    left, right = contract[0][0], contract[1][0]
    return low_dot(
        jnp.concatenate([a[0], a[0], a[1]], left),
        jnp.concatenate([b[0], b[1], b[0]], right),
        contract,
    )


def fine_dot(a, b, contract=NN):
    return pair_dot(halves(a), halves(b), contract)


def sigmoid(x):
    return 1.0 / (1.0 + jnp.exp(-x))


def places(size):
    return (
        lax.broadcasted_iota(jnp.int32, (size, size), 0),
        lax.broadcasted_iota(jnp.int32, (size, size), 1),
    )


def unit_lower_inverses(strict_parts, rows, cols):
    size = strict_parts[0].shape[0]
    near = (rows >> 3) == (cols >> 3)
    eye = jnp.where(rows == cols, 1.0, 0.0)
    inner = [jnp.where(near, part, 0.0) for part in strict_parts]
    split = [halves(part) for part in inner]
    second = [halves(pair_dot(part, part)) for part in split]
    fourth = [halves(pair_dot(part, part)) for part in second]
    inverse = [eye - part for part in inner]
    inverse = [part + pair_dot(halves(part), power) for part, power in zip(inverse, second)]
    inverse = [part + pair_dot(halves(part), power) for part, power in zip(inverse, fourth)]
    level = 3
    while (1 << level) < size:
        joined = ((rows >> (level + 1)) == (cols >> (level + 1))) & ((rows >> level) != (cols >> level))
        split = [halves(part) for part in inverse]
        middle = [
            halves(pair_dot(halves(jnp.where(joined, strict, 0.0)), part))
            for strict, part in zip(strict_parts, split)
        ]
        inverse = [
            part - pair_dot(pair, between) for part, pair, between in zip(inverse, split, middle)
        ]
        level += 1
    return inverse


def taps_back(padded, steps):
    rolled = padded if steps == 0 else pltpu.roll(padded, steps, 0)
    return rolled[8:]


def conv_sum(padded, taps):
    count = taps.shape[0]
    total = taps[0:1] * taps_back(padded, count - 1)
    for member in range(1, count):
        total = total + taps[member : member + 1] * taps_back(padded, count - 1 - member)
    return total


def conv_transposed(grad, taps):
    count = taps.shape[0]
    padded = jnp.concatenate([jnp.zeros((8, grad.shape[1]), F32), grad], 0)
    size = padded.shape[0]
    total = taps[count - 1 : count] * padded
    for member in range(count - 1):
        total = total + taps[member : member + 1] * pltpu.roll(padded, size - (count - 1 - member), 0)
    return total


def conv_taps_grad(padded, grad, count):
    return jnp.concatenate(
        [
            jnp.sum(grad * taps_back(padded, count - 1 - member), 0, keepdims=True)
            for member in range(count)
        ],
        0,
    )


def softplus(x):
    return jnp.maximum(x, 0.0) + jnp.log(1.0 + jnp.exp(-jnp.abs(x)))


class Gates:
    def __init__(self, side, resets, head, heads, rate, bias, rows, cols):
        size = side.shape[0]
        self.rate = rate
        self.shifted = side[:, head : head + 1] + bias
        self.log_decay = -rate * softplus(self.shifted)
        self.beta = sigmoid(side[:, heads + head : heads + head + 1])
        lanes = lax.broadcasted_iota(jnp.int32, (size, 128), 1)
        pair = jnp.where(lanes == 0, self.log_decay, jnp.where(lanes == 1, resets, 0.0))
        lower = jnp.where(rows >= cols, 1.0, 0.0).astype(LOW)
        split = thirds(pair)
        as_columns = low_dot(
            jnp.concatenate([lower] * 3, 1), jnp.concatenate(split, 0)
        )
        as_rows = low_dot(
            jnp.concatenate(split, 0), jnp.concatenate([lower] * 3, 1), ((0,), (1,))
        )
        total, count = as_columns[:, 0:1], as_columns[:, 1:2]
        linked = (jnp.abs(count - as_rows[1:2, :]) < 0.5) & (rows >= cols)
        self.decays = jnp.where(linked, jnp.exp(jnp.minimum(total - as_rows[0:1, :], 0.0)), 0.0)
        last_total, last_count = total[size - 1 : size], count[size - 1 : size]
        self.head_decay = jnp.where(count < 0.5, jnp.exp(total), 0.0)
        self.tail_decay = jnp.where(
            jnp.abs(count - last_count) < 0.5, jnp.exp(jnp.minimum(last_total - total, 0.0)), 0.0
        )


def silu_unit(summed, scale):
    gate = sigmoid(summed)
    act = summed * gate
    inverse = lax.rsqrt(jnp.sum(act * act, 1, keepdims=True) + EPSILON)
    return act, gate, inverse, act * (inverse * scale)


def silu_unit_back(grad, summed, gate, act, inverse, scale):
    unit = act * inverse
    grad = grad * scale
    act_grad = inverse * (grad - unit * jnp.sum(grad * unit, 1, keepdims=True))
    return act_grad * gate * (1.0 + summed * (1.0 - gate))


def head_columns(sizes, head):
    heads, key_size, value_size = sizes
    base = 2 * heads * key_size
    return (
        slice(head * key_size, (head + 1) * key_size),
        slice((heads + head) * key_size, (heads + head + 1) * key_size),
        slice(base + head * value_size, base + (head + 1) * value_size),
    )


def side_columns(sizes):
    heads, key_size, value_size = sizes
    start = 2 * heads * (key_size + value_size)
    return slice(start, start + 128)


def local_kernel(
    sizes, projected_ref, resets_ref, border_ref, taps_ref, rate_ref, bias_ref,
    carried_ref, local_ref, map_ref, inverse_ref,
):
    heads, key_size, value_size = sizes
    size = projected_ref.shape[0]
    rows, cols = places(size)
    side, resets = projected_ref[:, side_columns(sizes)], resets_ref[:, 0:1]
    gates, queries, keys, values, mixing = [], [], [], [], []
    for head in range(heads):
        gate = Gates(side, resets, head, heads, rate_ref[head], bias_ref[head], rows, cols)
        summed = [
            conv_sum(jnp.concatenate([border_ref[:, at], projected_ref[:, at]], 0), taps_ref[:, at])
            for at in head_columns(sizes, head)
        ]
        gates.append(gate)
        queries.append(silu_unit(summed[0], key_size**-0.5)[3])
        keys.append(silu_unit(summed[1], 1.0)[3])
        values.append(summed[2] * sigmoid(summed[2]))
        split = halves(keys[head])
        gram = pair_dot(split, split, NT)
        mixing.append(gate.beta * jnp.where(rows > cols, gate.decays * gram, 0.0))
    inverses = [halves(part) for part in unit_lower_inverses(mixing, rows, cols)]
    krows, kcols = places(key_size)
    for head in range(heads):
        gate, query, key, value, inverse = (
            gates[head], queries[head], keys[head], values[head], inverses[head],
        )
        inverse_ref[head, 0] = inverse[0]
        inverse_ref[head, 1] = inverse[1]
        both = halves(
            pair_dot(
                inverse,
                halves(jnp.concatenate([(gate.beta * gate.head_decay) * key, gate.beta * value], 1)),
            )
        )
        scores = fine_dot(query, key, NT) * gate.decays
        read = pair_dot(halves(scores), both)
        carried_ref[:, head * key_size : (head + 1) * key_size] = (
            gate.head_decay * query - read[:, :key_size]
        )
        local_ref[:, head * value_size : (head + 1) * value_size] = read[:, key_size:]
        written = pair_dot(halves(key * gate.tail_decay), both, TN)
        kept = jnp.where(krows == kcols, gate.head_decay[size - 1 : size], 0.0)
        map_ref[head, :, :key_size] = kept - written[:, :key_size]
        map_ref[head, :, key_size:] = written[:, key_size:]


def pick(refs, index, head):
    value = refs[0][head]
    for at in range(1, len(refs)):
        value = jnp.where(index == at, refs[at][head], value)
    return value


def gate_kernel(sizes, count, order_ref, *refs):
    heads, key_size, value_size = sizes
    maps = refs[:count]
    (
        state_ref, carried_ref, local_ref, outgate_ref, gain_ref, gated_ref, output_ref, entry_ref, end_ref,
    ) = refs[count:]
    states = [state_ref[head] for head in range(heads)]
    entries = list(states)
    for at in range(count):
        index = order_ref[at]
        for head in range(heads):
            if at:
                entries[head] = jnp.where(index == 0, states[head], entries[head])
            step = pick(maps, index, head)
            states[head] = fine_dot(step[:, :key_size], states[head]) + step[:, key_size:]
    for head in range(heads):
        at = slice(head * value_size, (head + 1) * value_size)
        entry_ref[head] = entries[head]
        end_ref[head] = states[head]
        output = local_ref[:, at] + fine_dot(
            carried_ref[:, head * key_size : (head + 1) * key_size], entries[head]
        )
        output_ref[:, at] = output
        normed = output * lax.rsqrt(jnp.mean(output * output, 1, keepdims=True) + EPSILON)
        gate = outgate_ref[:, at]
        gated_ref[:, at] = (normed * gain_ref[...] * (gate * sigmoid(gate))).astype(LOW).astype(F32)


def gate_back_kernel(sizes, count, order_ref, *refs):
    heads, key_size, value_size = sizes
    pieces = refs[:count]
    (
        output_ref, outgate_ref, gain_ref, carried_ref,
        output_grad_ref, outgate_grad_ref, gain_grad_ref, entry_ref, grads,
    ) = refs[count:]
    part = pieces[0].shape[0]
    for at, piece in enumerate(pieces):
        grads[pl.ds(pl.multiple_of(order_ref[at] * part, part), part), :] = piece[...]
    gain = gain_ref[...]
    total = jnp.zeros_like(gain)
    for head in range(heads):
        at = slice(head * value_size, (head + 1) * value_size)
        grad, output, gate = grads[:, at], output_ref[:, at], outgate_ref[:, at]
        inverse = lax.rsqrt(jnp.mean(output * output, 1, keepdims=True) + EPSILON)
        unit = output * inverse
        opened = sigmoid(gate)
        swished = gate * opened
        outgate_grad_ref[:, at] = (
            grad * unit * gain * (opened * (1.0 + gate * (1.0 - opened)))
        ).astype(LOW)
        total = total + jnp.sum(grad * unit * swished, 0, keepdims=True)
        unit_grad = grad * gain * swished
        output_grad = inverse * (unit_grad - unit * jnp.mean(unit_grad * unit, 1, keepdims=True))
        output_grad_ref[:, at] = output_grad
        entry_ref[head] = fine_dot(
            carried_ref[:, head * key_size : (head + 1) * key_size], output_grad, TN
        )
    gain_grad_ref[...] = total


def mix_back_kernel(count, target_ref, grad_ref, mixed_ref, top_ref, gain_ref, weight_ref, sum_ref, *refs):
    values, grad = mixed_ref[...], grad_ref[...]
    inverse = lax.rsqrt(jnp.mean(values * values, 1, keepdims=True) + EPSILON)
    unit = values * inverse
    scaled = grad * gain_ref[...]
    mixed_grad = top_ref[...] + inverse * (scaled - unit * jnp.mean(unit * scaled, 1, keepdims=True))
    refs[0][...] = mixed_grad
    sum_ref[...] = jnp.sum(unit * grad, 0, keepdims=True)
    low = mixed_grad.astype(LOW)
    part = weight_ref.shape[0] // count
    for at in range(count):
        place = pl.multiple_of(target_ref[at] * part, part)
        refs[1 + at][...] = low_dot(low, weight_ref[pl.ds(place, part), :], NT)


def local_back_kernel(sizes, count, order_ref, *refs):
    heads, key_size, value_size = sizes
    maps, entries = refs[:count], refs[count : 2 * count]
    (
        state_grad_ref, projected_ref, resets_ref, border_ref, taps_ref, rate_ref, bias_ref,
        inverse_ref, entry_state_ref, output_grad_ref,
        conv_grad_ref, border_grad_ref, taps_grad_ref, side_grad_ref, sums_ref, start_grad_ref,
    ) = refs[2 * count :]
    size = projected_ref.shape[0]
    scale = key_size**-0.5
    state_grads = [state_grad_ref[head] for head in range(heads)]
    end_grads = list(state_grads)
    for at in reversed(range(count)):
        index = order_ref[at]
        for head in range(heads):
            if at < count - 1:
                end_grads[head] = jnp.where(index == 0, state_grads[head], end_grads[head])
            step = pick(maps, index, head)[:, :key_size]
            state_grads[head] = fine_dot(step, state_grads[head], TN) + pick(entries, index, head)
    rows, cols = places(size)
    strict = rows > cols
    lower = jnp.where(rows >= cols, 1.0, 0.0).astype(LOW)
    lanes = lax.broadcasted_iota(jnp.int32, (size, 128), 1)
    at_row = lax.broadcasted_iota(jnp.int32, (size, 1), 0)
    sum_lanes = lax.broadcasted_iota(jnp.int32, (8, 128), 1)
    sum_rows = lax.broadcasted_iota(jnp.int32, (8, 128), 0)
    side, resets = projected_ref[:, side_columns(sizes)], resets_ref[:, 0:1]
    side_grad = jnp.zeros((size, 128), F32)
    sums = jnp.zeros((8, 128), F32)
    for head in range(heads):
        start_grad_ref[head] = state_grads[head]
        gate = Gates(side, resets, head, heads, rate_ref[head], bias_ref[head], rows, cols)
        columns = head_columns(sizes, head)
        padded = [jnp.concatenate([border_ref[:, at], projected_ref[:, at]], 0) for at in columns]
        summed = [conv_sum(part, taps_ref[:, at]) for part, at in zip(padded, columns)]
        act_q, gate_q, inverse_q, query = silu_unit(summed[0], scale)
        act_k, gate_k, inverse_k, key = silu_unit(summed[1], 1.0)
        gate_v = sigmoid(summed[2])
        value = summed[2] * gate_v
        beta, decays, head_decay, tail_decay = gate.beta, gate.decays, gate.head_decay, gate.tail_decay
        end_grad, state = end_grads[head], entry_state_ref[head]
        inverse = (inverse_ref[head, 0], inverse_ref[head, 1])
        output_grad = halves(output_grad_ref[:, head * value_size : (head + 1) * value_size])
        query_s, key_s, state_s, end_s = halves(query), halves(key), halves(state), halves(end_grad)

        gram = pair_dot(key_s, key_s, NT)
        pure = pair_dot(query_s, key_s, NT)
        residue = value - head_decay * pair_dot(key_s, state_s)
        update = halves(pair_dot(inverse, halves(beta * residue)))
        update_grad = pair_dot(halves(pure * decays), output_grad, TN) + pair_dot(
            halves(key * tail_decay), end_s
        )
        target_grad = pair_dot(inverse, halves(update_grad), TN)
        target_s = halves(target_grad)
        weighted = jnp.where(strict, -pair_dot(target_s, update, NT), 0.0) * decays
        pure_grad = pair_dot(output_grad, update, NT) * decays
        reached = pair_dot(output_grad, state_s, NT)
        erased = pair_dot(target_s, state_s, NT)
        kept = pair_dot(update, end_s, NT)
        gram_grad = weighted * beta
        pure_s, gram_s = halves(pure_grad), halves(gram_grad)
        query_grad = head_decay * reached + pair_dot(pure_s, key_s)
        key_grad = (
            pair_dot(pure_s, query_s, TN)
            + tail_decay * kept
            - (beta * head_decay) * erased
            + pair_dot(gram_s, key_s)
            + pair_dot(gram_s, key_s, TN)
        )
        value_grad = beta * target_grad
        beta_grad = jnp.sum(target_grad * residue, 1, keepdims=True) + jnp.sum(
            weighted * gram, 1, keepdims=True
        )
        spread = pure_grad * pure + gram_grad * gram
        head_decay_grad = jnp.sum(query * reached, 1, keepdims=True) - beta * jnp.sum(
            key * erased, 1, keepdims=True
        )
        tail_part = tail_decay * jnp.sum(key * kept, 1, keepdims=True)
        spread_s = jnp.concatenate(thirds(spread), 0)
        column_sums = low_dot(spread_s, jnp.ones((3 * size, 128), LOW), TN)[:, 0:1]
        total_grad = (
            head_decay * head_decay_grad - tail_part + jnp.sum(spread, 1, keepdims=True) - column_sums
        )
        last_grad = jnp.sum(tail_part, 0, keepdims=True) + head_decay[size - 1 : size] * jnp.sum(
            jnp.sum(end_grad * state, 1, keepdims=True), 0, keepdims=True
        )
        total_grad = total_grad + jnp.where(at_row == size - 1, last_grad, 0.0)
        total_s = jnp.concatenate(thirds(jnp.where(lanes == 0, total_grad, 0.0)), 0)
        log_grad = low_dot(jnp.concatenate([lower] * 3, 0), total_s, TN)[:, 0:1]
        decay_grad = log_grad * (-gate.rate) * sigmoid(gate.shifted)
        beta_in_grad = beta_grad * beta * (1.0 - beta)
        side_grad = jnp.where(
            lanes == head, decay_grad, jnp.where(lanes == heads + head, beta_in_grad, side_grad)
        )
        log_sum = jnp.sum(log_grad * gate.log_decay, 0, keepdims=True)
        bias_sum = jnp.sum(decay_grad, 0, keepdims=True)
        sums = jnp.where(
            (sum_lanes == head) & (sum_rows == 0),
            log_sum,
            jnp.where((sum_lanes == head) & (sum_rows == 1), bias_sum, sums),
        )
        grads = (
            silu_unit_back(query_grad, summed[0], gate_q, act_q, inverse_q, scale),
            silu_unit_back(key_grad, summed[1], gate_k, act_k, inverse_k, 1.0),
            value_grad * gate_v * (1.0 + summed[2] * (1.0 - gate_v)),
        )
        for grad, part, at in zip(grads, padded, columns):
            spread_out = conv_transposed(grad, taps_ref[:, at])
            border_grad_ref[:, at] = spread_out[:8]
            conv_grad_ref[:, at] = spread_out[8:]
            taps_grad_ref[:, at] = conv_taps_grad(part, grad, taps_ref.shape[0])
    side_grad_ref[...] = side_grad.astype(LOW)
    sums_ref[...] = sums


class Clock:
    latest = None


def tick(value):
    if Clock.latest is None:
        return value
    return lax.optimization_barrier((value, Clock.latest))[0]


def tock(results):
    Clock.latest = min(results, key=lambda array: array.size)
    return results


def smem():
    return pl.BlockSpec(memory_space=pltpu.SMEM)


def anywhere():
    return pl.BlockSpec(memory_space=pl.ANY)


def call(kernel, out_shape, operands, name, micros, in_specs=None, scratch=(), vmem=VMEM_BYTES):
    whole = lambda array: pl.BlockSpec(array.shape, lambda i: (0,) * len(array.shape))
    vectors = [at for at in range(len(operands)) if in_specs is None or in_specs[at] is None]
    least = min(vectors, key=lambda at: operands[at].size)
    operands = list(operands)
    operands[least] = tick(operands[least])
    specs = [whole(array) for array in operands] if in_specs is None else in_specs
    specs = [whole(array) if spec is None else spec for spec, array in zip(specs, operands)]
    results = pl.pallas_call(
        kernel,
        grid=(1,),
        in_specs=specs,
        out_specs=[whole(array) for array in out_shape],
        out_shape=out_shape,
        scratch_shapes=list(scratch),
        compiler_params=pltpu.CompilerParams(vmem_limit_bytes=vmem),
        cost_estimate=pl.CostEstimate(
            flops=int(micros * 1e+07), bytes_accessed=int(micros * 30000), transcendentals=0
        ),
        name=name,
    )(*operands)
    return tock(results)


def shape(dims, dtype=F32):
    return jax.ShapeDtypeStruct(tuple(dims), dtype)


def columns_spec(rows, width, at):
    return pl.BlockSpec((rows, width), lambda i: (0, at))


def mixer_local(sizes, projected, resets, border, taps, rate, bias):
    heads, key_size, value_size = sizes
    rows = projected.shape[0]
    return call(
        partial(local_kernel, sizes),
        [
            shape((rows, heads * key_size)),
            shape((rows, heads * value_size)),
            shape((heads, key_size, key_size + value_size)),
            shape((heads, 2, rows, rows), LOW),
        ],
        [projected, resets, border, taps, rate, bias],
        "mixer_local",
        12,
        [None, None, None, None, smem(), smem()],
    )


def mixer_gate(sizes, order, maps, state, carried, local, projected, gain):
    heads, key_size, value_size = sizes
    rows = projected.shape[0]
    count = len(maps)
    value_cols = heads * value_size
    outgate = columns_spec(rows, value_cols, (2 * heads * key_size + value_cols) // value_cols)
    return call(
        partial(gate_kernel, sizes, count),
        [
            shape((rows, value_cols)),
            shape((rows, value_cols)),
            shape((heads, key_size, value_size)),
            shape((heads, key_size, value_size)),
        ],
        [order, *maps, state, carried, local, projected, gain],
        "mixer_gate",
        5,
        [smem()] + [None] * (count + 3) + [outgate, None],
    )


def mix_back(target, grad, mixed, top, gain, weight):
    rows, width = grad.shape
    count = target.shape[0]
    return call(
        partial(mix_back_kernel, count),
        [shape((1, width)), shape((rows, width))] + [shape((rows, weight.shape[0] // count))] * count,
        [target, grad, mixed, top, gain, weight],
        "mix_back",
        5,
        [smem()] + [None] * 5,
    )


def mixer_gate_back(sizes, order, pieces, output, projected, gain, carried):
    heads, key_size, value_size = sizes
    rows = projected.shape[0]
    count = len(pieces)
    value_cols = heads * value_size
    outgate = columns_spec(rows, value_cols, (2 * heads * key_size + value_cols) // value_cols)
    return call(
        partial(gate_back_kernel, sizes, count),
        [
            shape((rows, value_cols)),
            shape((rows, value_cols), LOW),
            shape((1, value_size)),
            shape((heads, key_size, value_size)),
        ],
        [order, *pieces, output, projected, gain, carried],
        "mixer_gate_back",
        4,
        [smem()] + [None] * (count + 1) + [outgate, None, None],
        [pltpu.VMEM((rows, value_cols), F32)],
    )


def mixer_local_back(
    sizes, order, maps, entries, state_grad, projected, resets, border, taps, rate, bias, inverse,
    entry_state, output_grad,
):
    heads, key_size, value_size = sizes
    rows = projected.shape[0]
    count = len(maps)
    conv_cols = taps.shape[1]
    return call(
        partial(local_back_kernel, sizes, count),
        [
            shape((rows, conv_cols)),
            shape((8, conv_cols)),
            shape(taps.shape),
            shape((rows, 128), LOW),
            shape((8, 128)),
            shape((heads, key_size, value_size)),
        ],
        [
            order, *maps, *entries, state_grad, projected, resets, border, taps, rate, bias, inverse,
            entry_state, output_grad,
        ],
        "mixer_local_back",
        12,
        [smem()] + [None] * (2 * count + 5) + [smem(), smem(), None, None, None],
    )


def recast_kernel(index_ref, source_ref, *refs):
    refs[-1][...] = source_ref[...].astype(refs[-1].dtype)


def widen(values):
    rows, cols = values.shape
    tile = min(rows, 256)
    spec = pl.BlockSpec((tile, cols), lambda i, index: (i, 0))
    return pl.pallas_call(
        recast_kernel,
        grid_spec=pltpu.PrefetchScalarGridSpec(
            num_scalar_prefetch=1, grid=(rows // tile,), in_specs=[spec], out_specs=spec
        ),
        out_shape=shape((rows, cols)),
        name="widen",
    )(jnp.zeros((1,), jnp.int32), values)


def narrow_into(whole, values, index, total, member, members, pieces):
    rows, cols = values.shape
    tile = rows // pieces
    source = pl.BlockSpec((tile, cols), lambda i, index: (i, 0))
    placed = pl.BlockSpec((tile, cols), lambda i, index: (i * members + member, index[0]))
    more = [] if whole is None else [whole]
    return pl.pallas_call(
        recast_kernel,
        grid_spec=pltpu.PrefetchScalarGridSpec(
            num_scalar_prefetch=1,
            grid=(pieces,),
            in_specs=[source] + [anywhere()] * len(more),
            out_specs=placed,
        ),
        out_shape=shape((rows * members, total), LOW),
        input_output_aliases={2: 0} if more else {},
        name="narrow_into",
    )(tick(index), values, *more)


def choose_kernel(first_ref, own_ref, other_ref, low_ref):
    low_ref[...] = jnp.where(first_ref[0] == 1, own_ref[...], other_ref[...]).astype(LOW)


def choose(first, paired, single, member, members, pieces):
    rows, cols = single.shape
    tile = rows // pieces
    return pl.pallas_call(
        choose_kernel,
        grid=(pieces,),
        in_specs=[
            smem(),
            pl.BlockSpec((tile, cols), lambda i: (i, 0)),
            pl.BlockSpec((tile, cols), lambda i: (i * members + member, 0)),
        ],
        out_specs=pl.BlockSpec((tile, cols), lambda i: (i, 0)),
        out_shape=shape((rows, cols), LOW),
        name="choose",
    )(tick(first), single, paired)


def enter_kernel(rows_ref, gain_ref, weight_ref, hidden_ref, projected_ref):
    values = rows_ref[...]
    inverse = lax.rsqrt(jnp.mean(values * values, 1, keepdims=True) + EPSILON)
    hidden = (values * inverse * gain_ref[...]).astype(LOW)
    hidden_ref[...] = hidden
    projected_ref[...] = low_dot(hidden, weight_ref[...])


def enter(rows, gain, weight):
    count, width = rows.shape
    return call(
        enter_kernel,
        [shape((count, width), LOW), shape((count, weight.shape[1]))],
        [rows, gain, weight],
        "enter",
        6,
    )


def join_kernel(
    rows_ref, gated_ref, weight_ref, gain_ref, gate_hbm, up_hbm, down_hbm,
    mixed_ref, hidden_ref, gate_ref, up_ref, inner_ref, sums_ref,
    gate_weight, up_weight, down_weight, arrived,
):
    copies = [
        pltpu.make_async_copy(source, target, arrived.at[at])
        for at, (source, target) in enumerate(
            ((gate_hbm, gate_weight), (up_hbm, up_weight), (down_hbm, down_weight))
        )
    ]
    for copy in copies:
        copy.start()
    depth = gated_ref.shape[2]
    mixed = rows_ref[...]
    for part in range(gated_ref.shape[0]):
        mixed = mixed + low_dot(
            gated_ref[part].astype(LOW), weight_ref[part * depth : (part + 1) * depth, :]
        )
    mixed_ref[...] = mixed
    inverse = lax.rsqrt(jnp.mean(mixed * mixed, 1, keepdims=True) + EPSILON)
    hidden = (mixed * inverse * gain_ref[...]).astype(LOW)
    hidden_ref[...] = hidden
    copies[0].wait()
    gate = low_dot(hidden, gate_weight[...])
    gate_ref[...] = gate
    copies[1].wait()
    up = low_dot(hidden, up_weight[...])
    up_ref[...] = up
    inner = (gate * sigmoid(gate) * up).astype(LOW)
    inner_ref[...] = inner
    copies[2].wait()
    sums_ref[...] = low_dot(inner, down_weight[...])


def join_heads(rows, gated, weight, gain, gate_weight, up_weight, down_weight):
    count, width = rows.shape
    hidden = gate_weight.shape[1]
    return call(
        join_kernel,
        [
            shape((count, width)),
            shape((count, width), LOW),
            shape((count, hidden)),
            shape((count, hidden)),
            shape((count, hidden), LOW),
            shape((count, width)),
        ],
        [rows, gated, weight, gain, gate_weight, up_weight, down_weight],
        "join_heads",
        12,
        [None] * 4 + [anywhere()] * 3,
        [
            pltpu.VMEM(gate_weight.shape, LOW),
            pltpu.VMEM(up_weight.shape, LOW),
            pltpu.VMEM(down_weight.shape, LOW),
            pltpu.SemaphoreType.DMA((3,)),
        ],
        56 * 1024 * 1024,
    )


def feed_back_kernel(
    last_ref, given_ref, handed_ref, gate_ref, up_ref, gate_hbm, up_hbm, down_hbm,
    top_ref, gate_grad_ref, up_grad_ref, sums_ref, gate_weight, up_weight, down_weight, arrived,
):
    copies = [
        pltpu.make_async_copy(source, target, arrived.at[at])
        for at, (source, target) in enumerate(
            ((down_hbm, down_weight), (gate_hbm, gate_weight), (up_hbm, up_weight))
        )
    ]
    for copy in copies:
        copy.start()
    top = jnp.where(last_ref[0] == 1, given_ref[...].astype(F32), handed_ref[...]).astype(LOW)
    top_ref[...] = top
    copies[0].wait()
    grad = low_dot(top, down_weight[...], NT)
    gate = gate_ref[...]
    opened = sigmoid(gate)
    gate_grad = (grad * up_ref[...] * (opened * (1.0 + gate * (1.0 - opened)))).astype(LOW)
    up_grad = (grad * gate * opened).astype(LOW)
    gate_grad_ref[...] = gate_grad
    up_grad_ref[...] = up_grad
    copies[1].wait()
    sums = low_dot(gate_grad, gate_weight[...], NT)
    copies[2].wait()
    sums_ref[...] = sums + low_dot(up_grad, up_weight[...], NT)


def feed_back(last, given, handed, gate_act, up_act, gate_weight, up_weight, down_weight):
    count, width = given.shape
    hidden = gate_weight.shape[1]
    return call(
        feed_back_kernel,
        [
            shape((count, width), LOW),
            shape((count, hidden), LOW),
            shape((count, hidden), LOW),
            shape((count, width)),
        ],
        [last, given, handed, gate_act, up_act, gate_weight, up_weight, down_weight],
        "feed_back",
        12,
        [smem()] + [None] * 4 + [anywhere()] * 3,
        [
            pltpu.VMEM(gate_weight.shape, LOW),
            pltpu.VMEM(up_weight.shape, LOW),
            pltpu.VMEM(down_weight.shape, LOW),
            pltpu.SemaphoreType.DMA((3,)),
        ],
    )


def leave_kernel(conv_ref, tail_ref, outgate_ref, side_ref, weight_ref, low_ref, sums_ref):
    rows, conv_cols = conv_ref.shape
    conv = conv_ref[...]
    conv = jnp.concatenate([conv[: rows - 8], conv[rows - 8 :] + tail_ref[...]], 0)
    low = jnp.concatenate([conv.astype(LOW), outgate_ref[...], side_ref[...]], 1)
    low_ref[...] = low
    sums_ref[...] = low_dot(low, weight_ref[...], NT)


def leave(conv, tail, outgate, side, weight):
    count, width = conv.shape[0], weight.shape[0]
    return call(
        leave_kernel,
        [shape((count, weight.shape[1]), LOW), shape((count, width))],
        [conv, tail, outgate, side, weight],
        "leave",
        7,
    )


def row_norm_back(values, gain, grad):
    inverse = lax.rsqrt(jnp.mean(values * values, -1, keepdims=True) + EPSILON)
    unit = values * inverse
    scaled = grad * gain
    back = inverse * (scaled - unit * jnp.mean(unit * scaled, -1, keepdims=True))
    return back, jnp.sum(unit * grad, 0)


def ring(value, axis, steps):
    count = lax.axis_size(axis)
    return lax.ppermute(value, axis, [(at, (at + steps) % count) for at in range(count)])


def all_seq(value):
    return [value] + [ring(value, "seq", step) for step in range(1, lax.axis_size("seq"))]


def handed_on(value, axis, steps):
    count = lax.axis_size(axis)
    first, last = max(0, -steps), min(count, count - steps)
    return lax.ppermute(value, axis, [(at, at + steps) for at in range(first, last)])


def gather_tp(values):
    return lax.all_gather(values, "tp", axis=0, tiled=True)


def scatter_tp(values):
    return lax.psum_scatter(values, "tp", scatter_dimension=0, tiled=True)


def crossed(value, bit):
    return lax.ppermute(value, "seq", [(at, at ^ bit) for at in range(lax.axis_size("seq"))])


def butterfly(value, axis):
    count = lax.axis_size(axis)
    step = 1
    while step < count:
        value = value + lax.ppermute(value, axis, [(at, at ^ step) for at in range(count)])
        step *= 2
    return value


class CoreSums:
    def __init__(self, left, right, axis):
        count = lax.axis_size("seq")
        index = lax.axis_index("seq")
        self.left, self.right, self.axis = left, right, axis
        self.chunk = (left, right)[axis].shape[1] // count
        self.core, chip, chips = index % 2, index // 2, count // 2
        self.order = [(chip + step) % chips for step in range(1, chips)] + [chip]

    def product(self, chip, core):
        place = (chip * 2 + core) * self.chunk
        left, right = self.left, self.right
        if self.axis:
            right = lax.dynamic_slice_in_dim(right, place, self.chunk, 1)
        else:
            left = lax.dynamic_slice_in_dim(left, place, self.chunk, 1)
        return tock([low_dot(tick(left), right, TN)])[0]

    def send(self):
        self.received = [crossed(self.product(at, 1 - self.core), 1) for at in self.order]
        return self

    def sums(self):
        return [
            tock([self.product(at, self.core) + part])[0]
            for at, part in zip(self.order, self.received)
        ]


def chip_moves(parts):
    return [ring(part, "seq", 2 * step) for step, part in enumerate(parts[:-1], 1)]


def total(parts, moved):
    return sum(moved, parts[-1])


def after(value, *others):
    return lax.optimization_barrier((value, *others))[0]


def after_all(parts, *others):
    return [None if part is None else after(part, *others) for part in parts]


def local(
    inputs, cotangent, doc_start, norm_in, query_weight, key_weight, value_weight, outgate_weight,
    decay_weight, beta_weight, conv_query, conv_key, conv_value, decay_log, decay_bias, head_norm,
    out_weight, norm_feed, gate_weight, up_weight, down_weight,
):
    Clock.latest = None
    query_weight, key_weight, value_weight = query_weight[0], key_weight[0], value_weight[0]
    outgate_weight, decay_weight, beta_weight = outgate_weight[0], decay_weight[0], beta_weight[0]
    gate_weight, up_weight, down_weight, out_weight = (
        gate_weight[0], up_weight[0], down_weight[0], out_weight[0],
    )
    taps = jnp.concatenate([conv_query[0], conv_key[0], conv_value[0]], 1)
    rate, bias = jnp.exp(decay_log[0]), decay_bias[0]
    heads = bias.shape[0]
    key_size = query_weight.shape[1] // heads
    value_size = value_weight.shape[1] // heads
    sizes = (heads, key_size, value_size)
    key_cols, value_cols = heads * key_size, heads * value_size
    micros, own_rows, width = inputs.shape
    rows = cotangent.shape[1]
    seq_size, seq_index = lax.axis_size("seq"), lax.axis_index("seq")
    tp_index = lax.axis_index("tp")
    section = lax.axis_index("section")
    at_start, at_end = seq_index == 0, seq_index == seq_size - 1
    order = (seq_index - jnp.arange(seq_size, dtype=jnp.int32)) % seq_size
    tp_size = lax.axis_size("tp")
    sources = (tp_index - jnp.arange(tp_size, dtype=jnp.int32)) % tp_size
    targets = (tp_index + jnp.arange(tp_size, dtype=jnp.int32)) % tp_size
    last_section = section.astype(jnp.int32).reshape(1)
    groups = 2
    group = micros // groups

    def own(values):
        return lax.dynamic_slice_in_dim(values, tp_index * own_rows, own_rows, 0)

    def whole_out_weight(whole, piece, member, members):
        for step in range(0, seq_size, 2):
            moved = ring(piece, "seq", step) if step else piece
            for at, values in (
                ((seq_index - step) % seq_size, moved),
                (((seq_index ^ 1) - step) % seq_size, crossed(moved, 1)),
            ):
                whole = narrow_into(
                    whole, values, at.astype(jnp.int32).reshape(1), width, member, members, tp_size
                )
                tock([whole])
        return whole

    spare = jnp.zeros((width, 128 - 2 * heads), LOW)
    in_weight = jnp.concatenate(
        [query_weight, key_weight, value_weight, outgate_weight, decay_weight, beta_weight, spare], 1
    )
    conv_cols = 2 * key_cols + value_cols
    offsets = jnp.arange(rows, dtype=jnp.int32)

    def micro_of(step, member):
        return jnp.clip(step - section, 0, groups - 1) * group + member

    def reset_flags(micro):
        starts = micro * (rows * seq_size) + seq_index * rows + offsets
        flags = lax.dynamic_index_in_dim(doc_start, micro, 0, keepdims=False) == starts
        return jnp.broadcast_to(flags.astype(F32)[:, None], (rows, 128))

    def enter_mixer(residual, step, member, border_carry):
        micro = micro_of(step, member)
        hidden, projected = enter(residual, norm_in, in_weight)
        moved = ring(projected[rows - 8 :, :conv_cols], "seq", 1)
        border = jnp.where(at_start, border_carry, moved)
        resets = reset_flags(micro)
        carried, local_out, maps, inverse = mixer_local(
            sizes, projected, resets, border, taps, rate, bias
        )
        saved[step, member] = dict(
            hidden=hidden, border=border, projected=projected, resets=resets, carried=carried,
            maps=all_seq(maps), inverse=inverse,
        )
        return moved, local_out

    def gate(step, member, local_out, state):
        kept = saved[step, member]
        kept["gated"], kept["output"], kept["entry_state"], state = mixer_gate(
            sizes, order, kept["maps"], state, kept["carried"], local_out, kept["projected"], head_norm
        )
        return state

    def rows_outer(name):
        return jnp.concatenate(
            [
                jnp.where(section == 0, saved[0, member][name], saved[2, member][name])
                for member in range(group)
            ],
            0,
        )

    def rows_inner(name):
        return jnp.concatenate([saved[1, member][name] for member in range(group)], 0)

    def rows_of(name):
        return jnp.concatenate([rows_outer(name), rows_inner(name)], 0)

    def rounded(values):
        zero = jnp.zeros((1,), jnp.int32)
        return tock([narrow_into(None, values, zero, width, 0, 1, tp_size)])[0]

    def enter_mixer(residual, step, member, border_carry):
        micro = micro_of(step, member)
        hidden, projected = enter(residual, norm_in, in_weight)
        moved = ring(projected[rows - 8 :, :conv_cols], "seq", 1)
        border = jnp.where(at_start, border_carry, moved)
        resets = reset_flags(micro)
        carried, local_out, maps, inverse = mixer_local(
            sizes, projected, resets, border, taps, rate, bias
        )
        saved[step, member] = dict(
            hidden=hidden, border=border, projected=projected, resets=resets, carried=carried,
            maps=all_seq(maps), inverse=inverse,
        )
        return moved, local_out

    def gate(step, member, local_out, state):
        kept = saved[step, member]
        kept["gated"], kept["output"], kept["entry_state"], state = mixer_gate(
            sizes, order, kept["maps"], state, kept["carried"], local_out, kept["projected"], head_norm
        )
        return state

    def rows_of(name):
        outer = [
            jnp.where(section == 0, saved[0, member][name], saved[2, member][name])
            for member in range(group)
        ]
        return jnp.concatenate(outer + [saved[1, member][name] for member in range(group)], 0)

    saved = {}
    section_rows = {}
    part = width // seq_size
    entering = [inputs[member].astype(F32) * (section == 0) for member in range(group)]
    residuals = [gather_tp(values) for values in entering]
    out_piece = widen(lax.dynamic_slice_in_dim(out_weight, seq_index * part, part, 1))
    out_pieces = [
        gather_tp(after(values, *entering)) for values in jnp.split(out_piece, 2, 0)
    ]
    out_full = None
    border_carry = jnp.zeros((8, conv_cols), F32)
    state = jnp.zeros((heads, key_size, value_size), F32)
    nothing = jnp.zeros((rows, width), F32)
    members = list(reversed(range(group)))
    early, late = members[0], members[-1]
    tops, feed_grads, late_sums = {}, {}, {}

    def feed(back_step, member, received, handed):
        step = groups - back_step
        kept = saved[step, member]
        given = lax.dynamic_index_in_dim(cotangent, micro_of(step, member), 0, keepdims=False)
        if step == 0:
            given = jnp.where(section == 0, given, jnp.zeros_like(given))
        kept["top_low"], kept["gate_low"], kept["up_low"], sums = feed_back(
            last_section, given, handed, kept["gate_act"], kept["up_act"],
            gate_weight, up_weight, down_weight,
        )
        tops[member] = jnp.where(section == 0, received, own(given).astype(F32))
        if step:
            feed_grads[member] = scatter_tp(sums)
        else:
            summed = scatter_tp(jnp.where(section == 0, sums, late_sums[member]))
            section_rows[groups, member] = saved[groups, member]["mixed"] + summed
            feed_grads[member] = jnp.where(section == 0, summed, 0.0)

    for step in range(groups + 1):
        all_gated = []
        for member in range(group):
            border_carry, local_out = enter_mixer(residuals[member], step, member, border_carry)
            state = gate(step, member, local_out, state)
            saved[step, member]["entering"] = entering[member]
            all_gated.append(lax.all_gather(saved[step, member]["gated"], "tp", axis=0))
        if out_full is None:
            for member, piece in enumerate(out_pieces):
                out_full = whole_out_weight(out_full, after(piece, state), member, 2)
        all_sums = []
        for member in range(group):
            kept = saved[step, member]
            mixed, kept["hidden_feed"], kept["gate_act"], kept["up_act"], kept["inner"], sums = join_heads(
                residuals[member], all_gated[member], out_full, norm_feed,
                gate_weight, up_weight, down_weight,
            )
            kept["mixed"] = own(mixed)
            if step < groups:
                all_sums.append(scatter_tp(sums))
            else:
                late_sums[member] = sums
                feed(0, member, jnp.zeros((own_rows, width), F32), nothing)
        if step == groups:
            break
        ready = None
        entering, residuals = [], []
        for member in range(group):
            summed = all_sums[member] if ready is None else after(all_sums[member], ready)
            out_rows = saved[step, member]["mixed"] + summed
            section_rows[step, member] = out_rows
            handed = handed_on(out_rows, "section", 1)
            micro = micro_of(step + 1, member)
            given = lax.dynamic_index_in_dim(inputs, micro, 0, keepdims=False).astype(F32)
            ready = jnp.where(section == 0, given, handed)
            entering.append(ready)
            residuals.append(gather_tp(ready))

    tail_carry = jnp.zeros((8, conv_cols), F32)
    state_grad = jnp.zeros((heads, key_size, value_size), F32)
    in_grads = {}
    norm_in_grad = jnp.zeros((width,), F32)
    norm_feed_grad = jnp.zeros((width,), F32)
    gain_grad = jnp.zeros((value_size,), F32)
    taps_grad = jnp.zeros(taps.shape, F32)
    side_sums = jnp.zeros((8, 128), F32)
    received, handed = [None] * group, [None] * group
    for back_step in range(groups + 1):
        step = groups - back_step
        final = back_step == groups
        if back_step:
            for member in members:
                feed(back_step, member, received[member], handed[member])
        if final:
            feed_all, top_all = rows_of("hidden_feed"), rows_of("top_low")
            gate_sums = CoreSums(feed_all, rows_of("gate_low"), 0).send()
            gate_parts = gate_sums.sums()
        all_sums = {}

        def depart(member, tail):
            kept = saved[step, member]
            kept["projected_low"], sums = leave(
                kept["conv_grad"], tail, kept["outgate_low"], kept["side_low"], in_weight
            )
            all_sums[member] = scatter_tp(sums)
            return sums

        def mix(member):
            kept = saved[step, member]
            feed_part, kept["mixed_grad"], *pieces = mix_back(
                targets, feed_grads[member], kept["mixed"], tops[member], norm_feed, out_full
            )
            return feed_part[0], [ring(piece, "tp", at) if at else piece for at, piece in enumerate(pieces)]

        for member in members:
            kept = saved[step, member]
            feed_part, pieces = mix(member)
            norm_feed_grad = norm_feed_grad + feed_part
            if final and member == early:
                up_sums = CoreSums(feed_all, rows_of("up_low"), 0).send()
            elif final:
                inner_mixed = gather_tp(rows_inner("mixed_grad"))
                outer_mixed = gather_tp(rows_outer("mixed_grad"))
                pieces[0] = after(pieces[0], *gate_moved)
            output_grad, kept["outgate_low"], gain_part, entry_grad = mixer_gate_back(
                sizes, sources, pieces, kept["output"], kept["projected"], head_norm, kept["carried"]
            )
            gain_grad = gain_grad + gain_part[0]
            all_entries = all_seq(entry_grad)
            if final and member == early:
                up_parts = up_sums.sums()
            elif final:
                down_parts = CoreSums(rows_of("inner"), top_all, 1).send().sums()
                output_grad = after(output_grad, *up_parts)
            kept["conv_grad"], border_grad, taps_part, kept["side_low"], sums_part, state_grad = mixer_local_back(
                sizes, order, kept["maps"], all_entries, state_grad, kept["projected"],
                kept["resets"], kept["border"], taps, rate, bias, kept["inverse"],
                kept["entry_state"], output_grad,
            )
            moved = ring(border_grad, "seq", -1)
            tail = jnp.where(at_end, tail_carry, moved)
            tail_carry = moved
            if final and member == early:
                gate_moved = chip_moves(after_all(gate_parts, tail))
            elif final:
                up_moved = chip_moves(after_all(up_parts, tail))
                down_moved = chip_moves(after_all(down_parts, tail))
                tail = after(tail, all_sums[early])
            taps_grad = taps_grad + taps_part
            side_sums = side_sums + sums_part
            last = depart(member, tail)
        ready = None
        received, handed = [None] * group, [None] * group
        if final:
            in_sums = CoreSums(rows_of("hidden"), rows_of("projected_low"), 0).send()
            in_sums.left = after(in_sums.left, *up_moved)
            in_parts = in_sums.sums()
            in_moved = chip_moves(in_parts)
            inner_mixed = rounded(inner_mixed)
            outer_mixed = rounded(outer_mixed)
            ready = outer_mixed
        for member in members:
            kept = saved[step, member]
            summed = all_sums[member]
            if ready is not None and (not final or member == late):
                summed = after(summed, ready)
            entering_back, in_part = row_norm_back(kept["entering"], norm_in[0], summed)
            norm_in_grad = norm_in_grad + in_part
            own_grad = kept["mixed_grad"] + entering_back
            in_grads[step, member] = own_grad
            if not final:
                ready = handed_on(own_grad, "section", -1)
                received[member] = ready
                handed[member] = gather_tp(ready)
    def of_section(values):
        return [
            jnp.where(section == 0, values[at, member], values[at + 1, member])
            for at in range(groups)
            for member in range(group)
        ]

    def by_device(values):
        split = values.astype(LOW).reshape(-1, tp_size, own_rows, value_cols)
        return jnp.moveaxis(split, 0, 1).reshape(-1, value_cols)

    out_sums = CoreSums(
        jnp.concatenate([by_device(rows_outer("gated")), by_device(rows_inner("gated"))], 0),
        jnp.concatenate([outer_mixed, inner_mixed], 0),
        1,
    )
    out_parts = out_sums.send().sums()
    grad_out = total(out_parts, chip_moves(after_all(out_parts, *down_moved)))
    grad_gate, grad_up, grad_in, grad_down = [
        total(after_all(parts, out_parts[-1]), moved)
        for parts, moved in (
            (gate_parts, gate_moved), (up_parts, up_moved), (in_parts, in_moved),
            (down_parts, down_moved),
        )
    ]

    shared = butterfly(jnp.concatenate([norm_in_grad, norm_feed_grad, gain_grad]), "tp")
    small = butterfly(
        jnp.concatenate(
            [
                after(shared, out_parts[0]), taps_grad.reshape(-1), side_sums[0, :heads],
                side_sums[1, :heads],
            ]
        ),
        "seq",
    )
    bounds = [0, width, 2 * width, 2 * width + value_size]
    bounds += [bounds[-1] + taps.size, bounds[-1] + taps.size + heads, bounds[-1] + taps.size + 2 * heads]
    norm_in_grad, norm_feed_grad, gain_grad, taps_grad, log_grad, bias_grad = [
        small[low:high] for low, high in zip(bounds[:-1], bounds[1:])
    ]
    taps_grad = taps_grad.reshape(taps.shape)
    bounds = [
        0, key_cols, 2 * key_cols, conv_cols, conv_cols + value_cols, conv_cols + value_cols + heads,
        conv_cols + value_cols + 2 * heads,
    ]
    in_parts = [grad_in[:, low:high] for low, high in zip(bounds[:-1], bounds[1:])]
    return (
        jnp.stack(of_section(section_rows))[None],
        jnp.stack(of_section(in_grads))[None],
        norm_in_grad[None],
        *[member[None] for member in in_parts],
        taps_grad[None, :, :key_cols],
        taps_grad[None, :, key_cols : 2 * key_cols],
        taps_grad[None, :, 2 * key_cols :],
        log_grad[None],
        bias_grad[None],
        gain_grad[None],
        grad_out[None],
        norm_feed_grad[None],
        grad_gate[None],
        grad_up[None],
        grad_down[None],
    )


def solution(mesh):
    by_column, by_row = P("section", None, "tp"), P("section", "tp", None)
    placed = (
        P(None, ("seq", "tp"), None),
        P(None, "seq", None),
        P(None, "seq"),
        P("section", None),
        *[by_column] * 9,
        P("section", "tp"),
        P("section", "tp"),
        P("section", None),
        by_row,
        P("section", None),
        by_column,
        by_column,
        by_row,
    )
    rows_out = P("section", None, ("seq", "tp"), None)
    both = P("section", "seq", "tp")
    return jax.shard_map(
        local,
        mesh=mesh,
        in_specs=placed,
        out_specs=(
            rows_out,
            rows_out,
            P("section", None),
            *[both] * 6,
            *[by_column] * 3,
            P("section", "tp"),
            P("section", "tp"),
            P("section", None),
            P("section", "tp", "seq"),
            P("section", None),
            both,
            both,
            P("section", "tp", "seq"),
        ),
        check_vma=False,
    )
```

```python
from functools import partial

import jax
import jax.numpy as jnp
from jax import lax
from jax.experimental import pallas as pl
from jax.experimental.pallas import tpu as pltpu
from jax.sharding import PartitionSpec as P

EPSILON = 1e-06
F32 = jnp.float32
LOW = jnp.bfloat16
VMEM_BYTES = 48 * 1024 * 1024
NN = ((1,), (0,))
NT = ((1,), (1,))
TN = ((0,), (0,))


def low_dot(a, b, contract=NN):
    return lax.dot_general(a, b, (contract, ((), ())), preferred_element_type=F32)


def halves(x):
    high = x.astype(LOW)
    return high, (x - high.astype(F32)).astype(LOW)


def thirds(x):
    high = x.astype(LOW)
    rest = x - high.astype(F32)
    middle = rest.astype(LOW)
    return high, middle, (rest - middle.astype(F32)).astype(LOW)


def pair_dot(a, b, contract=NN):
    left, right = contract[0][0], contract[1][0]
    return low_dot(
        jnp.concatenate([a[0], a[0], a[1]], left),
        jnp.concatenate([b[0], b[1], b[0]], right),
        contract,
    )


def fine_dot(a, b, contract=NN):
    return pair_dot(halves(a), halves(b), contract)


def sigmoid(x):
    return 1.0 / (1.0 + jnp.exp(-x))


def places(size):
    return (
        lax.broadcasted_iota(jnp.int32, (size, size), 0),
        lax.broadcasted_iota(jnp.int32, (size, size), 1),
    )


def unit_lower_inverses(strict_parts, rows, cols):
    size = strict_parts[0].shape[0]
    near = (rows >> 3) == (cols >> 3)
    eye = jnp.where(rows == cols, 1.0, 0.0)
    inner = [jnp.where(near, part, 0.0) for part in strict_parts]
    split = [halves(part) for part in inner]
    second = [halves(pair_dot(part, part)) for part in split]
    fourth = [halves(pair_dot(part, part)) for part in second]
    inverse = [eye - part for part in inner]
    inverse = [part + pair_dot(halves(part), power) for part, power in zip(inverse, second)]
    inverse = [part + pair_dot(halves(part), power) for part, power in zip(inverse, fourth)]
    level = 3
    while (1 << level) < size:
        joined = ((rows >> (level + 1)) == (cols >> (level + 1))) & ((rows >> level) != (cols >> level))
        split = [halves(part) for part in inverse]
        middle = [
            halves(pair_dot(halves(jnp.where(joined, strict, 0.0)), part))
            for strict, part in zip(strict_parts, split)
        ]
        inverse = [
            part - pair_dot(pair, between) for part, pair, between in zip(inverse, split, middle)
        ]
        level += 1
    return inverse


def taps_back(padded, steps):
    rolled = padded if steps == 0 else pltpu.roll(padded, steps, 0)
    return rolled[8:]


def conv_sum(padded, taps):
    count = taps.shape[0]
    total = taps[0:1] * taps_back(padded, count - 1)
    for member in range(1, count):
        total = total + taps[member : member + 1] * taps_back(padded, count - 1 - member)
    return total


def conv_transposed(grad, taps):
    count = taps.shape[0]
    padded = jnp.concatenate([jnp.zeros((8, grad.shape[1]), F32), grad], 0)
    size = padded.shape[0]
    total = taps[count - 1 : count] * padded
    for member in range(count - 1):
        total = total + taps[member : member + 1] * pltpu.roll(padded, size - (count - 1 - member), 0)
    return total


def conv_taps_grad(padded, grad, count):
    return jnp.concatenate(
        [
            jnp.sum(grad * taps_back(padded, count - 1 - member), 0, keepdims=True)
            for member in range(count)
        ],
        0,
    )


def softplus(x):
    return jnp.maximum(x, 0.0) + jnp.log(1.0 + jnp.exp(-jnp.abs(x)))


class Gates:
    def __init__(self, side, resets, head, heads, rate, bias, rows, cols):
        size = side.shape[0]
        self.rate = rate
        self.shifted = side[:, head : head + 1] + bias
        self.log_decay = -rate * softplus(self.shifted)
        self.beta = sigmoid(side[:, heads + head : heads + head + 1])
        lanes = lax.broadcasted_iota(jnp.int32, (size, 128), 1)
        pair = jnp.where(lanes == 0, self.log_decay, jnp.where(lanes == 1, resets, 0.0))
        lower = jnp.where(rows >= cols, 1.0, 0.0).astype(LOW)
        split = thirds(pair)
        as_columns = low_dot(
            jnp.concatenate([lower] * 3, 1), jnp.concatenate(split, 0)
        )
        as_rows = low_dot(
            jnp.concatenate(split, 0), jnp.concatenate([lower] * 3, 1), ((0,), (1,))
        )
        total, count = as_columns[:, 0:1], as_columns[:, 1:2]
        linked = (jnp.abs(count - as_rows[1:2, :]) < 0.5) & (rows >= cols)
        self.decays = jnp.where(linked, jnp.exp(jnp.minimum(total - as_rows[0:1, :], 0.0)), 0.0)
        last_total, last_count = total[size - 1 : size], count[size - 1 : size]
        self.head_decay = jnp.where(count < 0.5, jnp.exp(total), 0.0)
        self.tail_decay = jnp.where(
            jnp.abs(count - last_count) < 0.5, jnp.exp(jnp.minimum(last_total - total, 0.0)), 0.0
        )


def silu_unit(summed, scale):
    gate = sigmoid(summed)
    act = summed * gate
    inverse = lax.rsqrt(jnp.sum(act * act, 1, keepdims=True) + EPSILON)
    return act, gate, inverse, act * (inverse * scale)


def silu_unit_back(grad, summed, gate, act, inverse, scale):
    unit = act * inverse
    grad = grad * scale
    act_grad = inverse * (grad - unit * jnp.sum(grad * unit, 1, keepdims=True))
    return act_grad * gate * (1.0 + summed * (1.0 - gate))


def head_columns(sizes, head):
    heads, key_size, value_size = sizes
    base = 2 * heads * key_size
    return (
        slice(head * key_size, (head + 1) * key_size),
        slice((heads + head) * key_size, (heads + head + 1) * key_size),
        slice(base + head * value_size, base + (head + 1) * value_size),
    )


def side_columns(sizes):
    heads, key_size, value_size = sizes
    start = 2 * heads * (key_size + value_size)
    return slice(start, start + 128)


def local_kernel(
    sizes, projected_ref, resets_ref, border_ref, taps_ref, rate_ref, bias_ref,
    carried_ref, local_ref, map_ref, inverse_ref,
):
    heads, key_size, value_size = sizes
    size = projected_ref.shape[0]
    rows, cols = places(size)
    side, resets = projected_ref[:, side_columns(sizes)], resets_ref[:, 0:1]
    gates, queries, keys, values, mixing = [], [], [], [], []
    for head in range(heads):
        gate = Gates(side, resets, head, heads, rate_ref[head], bias_ref[head], rows, cols)
        summed = [
            conv_sum(jnp.concatenate([border_ref[:, at], projected_ref[:, at]], 0), taps_ref[:, at])
            for at in head_columns(sizes, head)
        ]
        gates.append(gate)
        queries.append(silu_unit(summed[0], key_size**-0.5)[3])
        keys.append(silu_unit(summed[1], 1.0)[3])
        values.append(summed[2] * sigmoid(summed[2]))
        split = halves(keys[head])
        gram = pair_dot(split, split, NT)
        mixing.append(gate.beta * jnp.where(rows > cols, gate.decays * gram, 0.0))
    inverses = [halves(part) for part in unit_lower_inverses(mixing, rows, cols)]
    krows, kcols = places(key_size)
    for head in range(heads):
        gate, query, key, value, inverse = (
            gates[head], queries[head], keys[head], values[head], inverses[head],
        )
        inverse_ref[head, 0] = inverse[0]
        inverse_ref[head, 1] = inverse[1]
        both = halves(
            pair_dot(
                inverse,
                halves(jnp.concatenate([(gate.beta * gate.head_decay) * key, gate.beta * value], 1)),
            )
        )
        scores = fine_dot(query, key, NT) * gate.decays
        read = pair_dot(halves(scores), both)
        carried_ref[:, head * key_size : (head + 1) * key_size] = (
            gate.head_decay * query - read[:, :key_size]
        )
        local_ref[:, head * value_size : (head + 1) * value_size] = read[:, key_size:]
        written = pair_dot(halves(key * gate.tail_decay), both, TN)
        kept = jnp.where(krows == kcols, gate.head_decay[size - 1 : size], 0.0)
        map_ref[head, :, :key_size] = kept - written[:, :key_size]
        map_ref[head, :, key_size:] = written[:, key_size:]


def pick(refs, index, head):
    value = refs[0][head]
    for at in range(1, len(refs)):
        value = jnp.where(index == at, refs[at][head], value)
    return value


def gate_kernel(sizes, count, order_ref, *refs):
    heads, key_size, value_size = sizes
    maps = refs[:count]
    (
        state_ref, carried_ref, local_ref, outgate_ref, gain_ref, gated_ref, output_ref, entry_ref, end_ref,
    ) = refs[count:]
    states = [state_ref[head] for head in range(heads)]
    entries = list(states)
    for at in range(count):
        index = order_ref[at]
        for head in range(heads):
            if at:
                entries[head] = jnp.where(index == 0, states[head], entries[head])
            step = pick(maps, index, head)
            states[head] = fine_dot(step[:, :key_size], states[head]) + step[:, key_size:]
    for head in range(heads):
        at = slice(head * value_size, (head + 1) * value_size)
        entry_ref[head] = entries[head]
        end_ref[head] = states[head]
        output = local_ref[:, at] + fine_dot(
            carried_ref[:, head * key_size : (head + 1) * key_size], entries[head]
        )
        output_ref[:, at] = output
        normed = output * lax.rsqrt(jnp.mean(output * output, 1, keepdims=True) + EPSILON)
        gate = outgate_ref[:, at]
        gated_ref[:, at] = (normed * gain_ref[...] * (gate * sigmoid(gate))).astype(LOW).astype(F32)


def gate_back_kernel(sizes, count, order_ref, *refs):
    heads, key_size, value_size = sizes
    pieces = refs[:count]
    (
        output_ref, outgate_ref, gain_ref, carried_ref,
        output_grad_ref, outgate_grad_ref, gain_grad_ref, entry_ref, grads,
    ) = refs[count:]
    part = pieces[0].shape[0]
    for at, piece in enumerate(pieces):
        grads[pl.ds(pl.multiple_of(order_ref[at] * part, part), part), :] = piece[...]
    gain = gain_ref[...]
    total = jnp.zeros_like(gain)
    for head in range(heads):
        at = slice(head * value_size, (head + 1) * value_size)
        grad, output, gate = grads[:, at], output_ref[:, at], outgate_ref[:, at]
        inverse = lax.rsqrt(jnp.mean(output * output, 1, keepdims=True) + EPSILON)
        unit = output * inverse
        opened = sigmoid(gate)
        swished = gate * opened
        outgate_grad_ref[:, at] = (
            grad * unit * gain * (opened * (1.0 + gate * (1.0 - opened)))
        ).astype(LOW)
        total = total + jnp.sum(grad * unit * swished, 0, keepdims=True)
        unit_grad = grad * gain * swished
        output_grad = inverse * (unit_grad - unit * jnp.mean(unit_grad * unit, 1, keepdims=True))
        output_grad_ref[:, at] = output_grad
        entry_ref[head] = fine_dot(
            carried_ref[:, head * key_size : (head + 1) * key_size], output_grad, TN
        )
    gain_grad_ref[...] = total


def mix_back_kernel(count, target_ref, grad_ref, mixed_ref, top_ref, gain_ref, weight_ref, sum_ref, *refs):
    values, grad = mixed_ref[...], grad_ref[...]
    inverse = lax.rsqrt(jnp.mean(values * values, 1, keepdims=True) + EPSILON)
    unit = values * inverse
    scaled = grad * gain_ref[...]
    mixed_grad = top_ref[...] + inverse * (scaled - unit * jnp.mean(unit * scaled, 1, keepdims=True))
    refs[0][...] = mixed_grad
    sum_ref[...] = jnp.sum(unit * grad, 0, keepdims=True)
    low = mixed_grad.astype(LOW)
    part = weight_ref.shape[0] // count
    for at in range(count):
        place = pl.multiple_of(target_ref[at] * part, part)
        refs[1 + at][...] = low_dot(low, weight_ref[pl.ds(place, part), :], NT)


def local_back_kernel(sizes, count, order_ref, *refs):
    heads, key_size, value_size = sizes
    maps, entries = refs[:count], refs[count : 2 * count]
    (
        state_grad_ref, projected_ref, resets_ref, border_ref, taps_ref, rate_ref, bias_ref,
        inverse_ref, entry_state_ref, output_grad_ref,
        conv_grad_ref, border_grad_ref, taps_grad_ref, side_grad_ref, sums_ref, start_grad_ref,
    ) = refs[2 * count :]
    size = projected_ref.shape[0]
    scale = key_size**-0.5
    state_grads = [state_grad_ref[head] for head in range(heads)]
    end_grads = list(state_grads)
    for at in reversed(range(count)):
        index = order_ref[at]
        for head in range(heads):
            if at < count - 1:
                end_grads[head] = jnp.where(index == 0, state_grads[head], end_grads[head])
            step = pick(maps, index, head)[:, :key_size]
            state_grads[head] = fine_dot(step, state_grads[head], TN) + pick(entries, index, head)
    rows, cols = places(size)
    strict = rows > cols
    lower = jnp.where(rows >= cols, 1.0, 0.0).astype(LOW)
    lanes = lax.broadcasted_iota(jnp.int32, (size, 128), 1)
    at_row = lax.broadcasted_iota(jnp.int32, (size, 1), 0)
    sum_lanes = lax.broadcasted_iota(jnp.int32, (8, 128), 1)
    sum_rows = lax.broadcasted_iota(jnp.int32, (8, 128), 0)
    side, resets = projected_ref[:, side_columns(sizes)], resets_ref[:, 0:1]
    side_grad = jnp.zeros((size, 128), F32)
    sums = jnp.zeros((8, 128), F32)
    for head in range(heads):
        start_grad_ref[head] = state_grads[head]
        gate = Gates(side, resets, head, heads, rate_ref[head], bias_ref[head], rows, cols)
        columns = head_columns(sizes, head)
        padded = [jnp.concatenate([border_ref[:, at], projected_ref[:, at]], 0) for at in columns]
        summed = [conv_sum(part, taps_ref[:, at]) for part, at in zip(padded, columns)]
        act_q, gate_q, inverse_q, query = silu_unit(summed[0], scale)
        act_k, gate_k, inverse_k, key = silu_unit(summed[1], 1.0)
        gate_v = sigmoid(summed[2])
        value = summed[2] * gate_v
        beta, decays, head_decay, tail_decay = gate.beta, gate.decays, gate.head_decay, gate.tail_decay
        end_grad, state = end_grads[head], entry_state_ref[head]
        inverse = (inverse_ref[head, 0], inverse_ref[head, 1])
        output_grad = halves(output_grad_ref[:, head * value_size : (head + 1) * value_size])
        query_s, key_s, state_s, end_s = halves(query), halves(key), halves(state), halves(end_grad)

        gram = pair_dot(key_s, key_s, NT)
        pure = pair_dot(query_s, key_s, NT)
        residue = value - head_decay * pair_dot(key_s, state_s)
        update = halves(pair_dot(inverse, halves(beta * residue)))
        update_grad = pair_dot(halves(pure * decays), output_grad, TN) + pair_dot(
            halves(key * tail_decay), end_s
        )
        target_grad = pair_dot(inverse, halves(update_grad), TN)
        target_s = halves(target_grad)
        weighted = jnp.where(strict, -pair_dot(target_s, update, NT), 0.0) * decays
        pure_grad = pair_dot(output_grad, update, NT) * decays
        reached = pair_dot(output_grad, state_s, NT)
        erased = pair_dot(target_s, state_s, NT)
        kept = pair_dot(update, end_s, NT)
        gram_grad = weighted * beta
        pure_s, gram_s = halves(pure_grad), halves(gram_grad)
        query_grad = head_decay * reached + pair_dot(pure_s, key_s)
        key_grad = (
            pair_dot(pure_s, query_s, TN)
            + tail_decay * kept
            - (beta * head_decay) * erased
            + pair_dot(gram_s, key_s)
            + pair_dot(gram_s, key_s, TN)
        )
        value_grad = beta * target_grad
        beta_grad = jnp.sum(target_grad * residue, 1, keepdims=True) + jnp.sum(
            weighted * gram, 1, keepdims=True
        )
        spread = pure_grad * pure + gram_grad * gram
        head_decay_grad = jnp.sum(query * reached, 1, keepdims=True) - beta * jnp.sum(
            key * erased, 1, keepdims=True
        )
        tail_part = tail_decay * jnp.sum(key * kept, 1, keepdims=True)
        spread_s = jnp.concatenate(thirds(spread), 0)
        column_sums = low_dot(spread_s, jnp.ones((3 * size, 128), LOW), TN)[:, 0:1]
        total_grad = (
            head_decay * head_decay_grad - tail_part + jnp.sum(spread, 1, keepdims=True) - column_sums
        )
        last_grad = jnp.sum(tail_part, 0, keepdims=True) + head_decay[size - 1 : size] * jnp.sum(
            jnp.sum(end_grad * state, 1, keepdims=True), 0, keepdims=True
        )
        total_grad = total_grad + jnp.where(at_row == size - 1, last_grad, 0.0)
        total_s = jnp.concatenate(thirds(jnp.where(lanes == 0, total_grad, 0.0)), 0)
        log_grad = low_dot(jnp.concatenate([lower] * 3, 0), total_s, TN)[:, 0:1]
        decay_grad = log_grad * (-gate.rate) * sigmoid(gate.shifted)
        beta_in_grad = beta_grad * beta * (1.0 - beta)
        side_grad = jnp.where(
            lanes == head, decay_grad, jnp.where(lanes == heads + head, beta_in_grad, side_grad)
        )
        log_sum = jnp.sum(log_grad * gate.log_decay, 0, keepdims=True)
        bias_sum = jnp.sum(decay_grad, 0, keepdims=True)
        sums = jnp.where(
            (sum_lanes == head) & (sum_rows == 0),
            log_sum,
            jnp.where((sum_lanes == head) & (sum_rows == 1), bias_sum, sums),
        )
        grads = (
            silu_unit_back(query_grad, summed[0], gate_q, act_q, inverse_q, scale),
            silu_unit_back(key_grad, summed[1], gate_k, act_k, inverse_k, 1.0),
            value_grad * gate_v * (1.0 + summed[2] * (1.0 - gate_v)),
        )
        for grad, part, at in zip(grads, padded, columns):
            spread_out = conv_transposed(grad, taps_ref[:, at])
            border_grad_ref[:, at] = spread_out[:8]
            conv_grad_ref[:, at] = spread_out[8:]
            taps_grad_ref[:, at] = conv_taps_grad(part, grad, taps_ref.shape[0])
    side_grad_ref[...] = side_grad.astype(LOW)
    sums_ref[...] = sums


class Clock:
    latest = None


def tick(value):
    if Clock.latest is None:
        return value
    return lax.optimization_barrier((value, Clock.latest))[0]


def tock(results):
    Clock.latest = min(results, key=lambda array: array.size)
    return results


def smem():
    return pl.BlockSpec(memory_space=pltpu.SMEM)


def anywhere():
    return pl.BlockSpec(memory_space=pl.ANY)


def call(kernel, out_shape, operands, name, micros, in_specs=None, scratch=(), vmem=VMEM_BYTES):
    whole = lambda array: pl.BlockSpec(array.shape, lambda i: (0,) * len(array.shape))
    vectors = [at for at in range(len(operands)) if in_specs is None or in_specs[at] is None]
    least = min(vectors, key=lambda at: operands[at].size)
    operands = list(operands)
    operands[least] = tick(operands[least])
    specs = [whole(array) for array in operands] if in_specs is None else in_specs
    specs = [whole(array) if spec is None else spec for spec, array in zip(specs, operands)]
    results = pl.pallas_call(
        kernel,
        grid=(1,),
        in_specs=specs,
        out_specs=[whole(array) for array in out_shape],
        out_shape=out_shape,
        scratch_shapes=list(scratch),
        compiler_params=pltpu.CompilerParams(vmem_limit_bytes=vmem),
        cost_estimate=pl.CostEstimate(
            flops=int(micros * 1e+07), bytes_accessed=int(micros * 30000), transcendentals=0
        ),
        name=name,
    )(*operands)
    return tock(results)


def shape(dims, dtype=F32):
    return jax.ShapeDtypeStruct(tuple(dims), dtype)


def columns_spec(rows, width, at):
    return pl.BlockSpec((rows, width), lambda i: (0, at))


def mixer_local(sizes, projected, resets, border, taps, rate, bias):
    heads, key_size, value_size = sizes
    rows = projected.shape[0]
    return call(
        partial(local_kernel, sizes),
        [
            shape((rows, heads * key_size)),
            shape((rows, heads * value_size)),
            shape((heads, key_size, key_size + value_size)),
            shape((heads, 2, rows, rows), LOW),
        ],
        [projected, resets, border, taps, rate, bias],
        "mixer_local",
        12,
        [None, None, None, None, smem(), smem()],
    )


def mixer_gate(sizes, order, maps, state, carried, local, projected, gain):
    heads, key_size, value_size = sizes
    rows = projected.shape[0]
    count = len(maps)
    value_cols = heads * value_size
    outgate = columns_spec(rows, value_cols, (2 * heads * key_size + value_cols) // value_cols)
    return call(
        partial(gate_kernel, sizes, count),
        [
            shape((rows, value_cols)),
            shape((rows, value_cols)),
            shape((heads, key_size, value_size)),
            shape((heads, key_size, value_size)),
        ],
        [order, *maps, state, carried, local, projected, gain],
        "mixer_gate",
        5,
        [smem()] + [None] * (count + 3) + [outgate, None],
    )


def mix_back(target, grad, mixed, top, gain, weight):
    rows, width = grad.shape
    count = target.shape[0]
    return call(
        partial(mix_back_kernel, count),
        [shape((1, width)), shape((rows, width))] + [shape((rows, weight.shape[0] // count))] * count,
        [target, grad, mixed, top, gain, weight],
        "mix_back",
        5,
        [smem()] + [None] * 5,
    )


def mixer_gate_back(sizes, order, pieces, output, projected, gain, carried):
    heads, key_size, value_size = sizes
    rows = projected.shape[0]
    count = len(pieces)
    value_cols = heads * value_size
    outgate = columns_spec(rows, value_cols, (2 * heads * key_size + value_cols) // value_cols)
    return call(
        partial(gate_back_kernel, sizes, count),
        [
            shape((rows, value_cols)),
            shape((rows, value_cols), LOW),
            shape((1, value_size)),
            shape((heads, key_size, value_size)),
        ],
        [order, *pieces, output, projected, gain, carried],
        "mixer_gate_back",
        4,
        [smem()] + [None] * (count + 1) + [outgate, None, None],
        [pltpu.VMEM((rows, value_cols), F32)],
    )


def mixer_local_back(
    sizes, order, maps, entries, state_grad, projected, resets, border, taps, rate, bias, inverse,
    entry_state, output_grad,
):
    heads, key_size, value_size = sizes
    rows = projected.shape[0]
    count = len(maps)
    conv_cols = taps.shape[1]
    return call(
        partial(local_back_kernel, sizes, count),
        [
            shape((rows, conv_cols)),
            shape((8, conv_cols)),
            shape(taps.shape),
            shape((rows, 128), LOW),
            shape((8, 128)),
            shape((heads, key_size, value_size)),
        ],
        [
            order, *maps, *entries, state_grad, projected, resets, border, taps, rate, bias, inverse,
            entry_state, output_grad,
        ],
        "mixer_local_back",
        12,
        [smem()] + [None] * (2 * count + 5) + [smem(), smem(), None, None, None],
    )


def recast_kernel(index_ref, source_ref, *refs):
    refs[-1][...] = source_ref[...].astype(refs[-1].dtype)


def widen(values):
    rows, cols = values.shape
    tile = min(rows, 256)
    spec = pl.BlockSpec((tile, cols), lambda i, index: (i, 0))
    return pl.pallas_call(
        recast_kernel,
        grid_spec=pltpu.PrefetchScalarGridSpec(
            num_scalar_prefetch=1, grid=(rows // tile,), in_specs=[spec], out_specs=spec
        ),
        out_shape=shape((rows, cols)),
        name="widen",
    )(jnp.zeros((1,), jnp.int32), values)


def narrow_into(whole, values, index, total, member, members, pieces):
    rows, cols = values.shape
    tile = rows // pieces
    source = pl.BlockSpec((tile, cols), lambda i, index: (i, 0))
    placed = pl.BlockSpec((tile, cols), lambda i, index: (i * members + member, index[0]))
    more = [] if whole is None else [whole]
    return pl.pallas_call(
        recast_kernel,
        grid_spec=pltpu.PrefetchScalarGridSpec(
            num_scalar_prefetch=1,
            grid=(pieces,),
            in_specs=[source] + [anywhere()] * len(more),
            out_specs=placed,
        ),
        out_shape=shape((rows * members, total), LOW),
        input_output_aliases={2: 0} if more else {},
        name="narrow_into",
    )(tick(index), values, *more)


def choose_kernel(first_ref, own_ref, other_ref, low_ref):
    low_ref[...] = jnp.where(first_ref[0] == 1, own_ref[...], other_ref[...]).astype(LOW)


def choose(first, paired, single, member, members, pieces):
    rows, cols = single.shape
    tile = rows // pieces
    return pl.pallas_call(
        choose_kernel,
        grid=(pieces,),
        in_specs=[
            smem(),
            pl.BlockSpec((tile, cols), lambda i: (i, 0)),
            pl.BlockSpec((tile, cols), lambda i: (i * members + member, 0)),
        ],
        out_specs=pl.BlockSpec((tile, cols), lambda i: (i, 0)),
        out_shape=shape((rows, cols), LOW),
        name="choose",
    )(tick(first), single, paired)


def enter_kernel(rows_ref, gain_ref, weight_ref, hidden_ref, projected_ref):
    values = rows_ref[...]
    inverse = lax.rsqrt(jnp.mean(values * values, 1, keepdims=True) + EPSILON)
    hidden = (values * inverse * gain_ref[...]).astype(LOW)
    hidden_ref[...] = hidden
    projected_ref[...] = low_dot(hidden, weight_ref[...])


def enter(rows, gain, weight):
    count, width = rows.shape
    return call(
        enter_kernel,
        [shape((count, width), LOW), shape((count, weight.shape[1]))],
        [rows, gain, weight],
        "enter",
        6,
    )


def join_kernel(
    rows_ref, gated_ref, weight_ref, gain_ref, gate_hbm, up_hbm, down_hbm,
    mixed_ref, hidden_ref, gate_ref, up_ref, inner_ref, sums_ref,
    gate_weight, up_weight, down_weight, arrived,
):
    copies = [
        pltpu.make_async_copy(source, target, arrived.at[at])
        for at, (source, target) in enumerate(
            ((gate_hbm, gate_weight), (up_hbm, up_weight), (down_hbm, down_weight))
        )
    ]
    for copy in copies:
        copy.start()
    depth = gated_ref.shape[2]
    mixed = rows_ref[...]
    for part in range(gated_ref.shape[0]):
        mixed = mixed + low_dot(
            gated_ref[part].astype(LOW), weight_ref[part * depth : (part + 1) * depth, :]
        )
    mixed_ref[...] = mixed
    inverse = lax.rsqrt(jnp.mean(mixed * mixed, 1, keepdims=True) + EPSILON)
    hidden = (mixed * inverse * gain_ref[...]).astype(LOW)
    hidden_ref[...] = hidden
    copies[0].wait()
    gate = low_dot(hidden, gate_weight[...])
    gate_ref[...] = gate
    copies[1].wait()
    up = low_dot(hidden, up_weight[...])
    up_ref[...] = up
    inner = (gate * sigmoid(gate) * up).astype(LOW)
    inner_ref[...] = inner
    copies[2].wait()
    sums_ref[...] = low_dot(inner, down_weight[...])


def join_heads(rows, gated, weight, gain, gate_weight, up_weight, down_weight):
    count, width = rows.shape
    hidden = gate_weight.shape[1]
    return call(
        join_kernel,
        [
            shape((count, width)),
            shape((count, width), LOW),
            shape((count, hidden)),
            shape((count, hidden)),
            shape((count, hidden), LOW),
            shape((count, width)),
        ],
        [rows, gated, weight, gain, gate_weight, up_weight, down_weight],
        "join_heads",
        12,
        [None] * 4 + [anywhere()] * 3,
        [
            pltpu.VMEM(gate_weight.shape, LOW),
            pltpu.VMEM(up_weight.shape, LOW),
            pltpu.VMEM(down_weight.shape, LOW),
            pltpu.SemaphoreType.DMA((3,)),
        ],
        56 * 1024 * 1024,
    )


def feed_back_kernel(
    last_ref, given_ref, handed_ref, gate_ref, up_ref, gate_hbm, up_hbm, down_hbm,
    top_ref, gate_grad_ref, up_grad_ref, sums_ref, gate_weight, up_weight, down_weight, arrived,
):
    copies = [
        pltpu.make_async_copy(source, target, arrived.at[at])
        for at, (source, target) in enumerate(
            ((down_hbm, down_weight), (gate_hbm, gate_weight), (up_hbm, up_weight))
        )
    ]
    for copy in copies:
        copy.start()
    top = jnp.where(last_ref[0] == 1, given_ref[...].astype(F32), handed_ref[...]).astype(LOW)
    top_ref[...] = top
    copies[0].wait()
    grad = low_dot(top, down_weight[...], NT)
    gate = gate_ref[...]
    opened = sigmoid(gate)
    gate_grad = (grad * up_ref[...] * (opened * (1.0 + gate * (1.0 - opened)))).astype(LOW)
    up_grad = (grad * gate * opened).astype(LOW)
    gate_grad_ref[...] = gate_grad
    up_grad_ref[...] = up_grad
    copies[1].wait()
    sums = low_dot(gate_grad, gate_weight[...], NT)
    copies[2].wait()
    sums_ref[...] = sums + low_dot(up_grad, up_weight[...], NT)


def feed_back(last, given, handed, gate_act, up_act, gate_weight, up_weight, down_weight):
    count, width = given.shape
    hidden = gate_weight.shape[1]
    return call(
        feed_back_kernel,
        [
            shape((count, width), LOW),
            shape((count, hidden), LOW),
            shape((count, hidden), LOW),
            shape((count, width)),
        ],
        [last, given, handed, gate_act, up_act, gate_weight, up_weight, down_weight],
        "feed_back",
        12,
        [smem()] + [None] * 4 + [anywhere()] * 3,
        [
            pltpu.VMEM(gate_weight.shape, LOW),
            pltpu.VMEM(up_weight.shape, LOW),
            pltpu.VMEM(down_weight.shape, LOW),
            pltpu.SemaphoreType.DMA((3,)),
        ],
    )


def leave_kernel(conv_ref, tail_ref, outgate_ref, side_ref, weight_ref, low_ref, sums_ref):
    rows, conv_cols = conv_ref.shape
    conv = conv_ref[...]
    conv = jnp.concatenate([conv[: rows - 8], conv[rows - 8 :] + tail_ref[...]], 0)
    low = jnp.concatenate([conv.astype(LOW), outgate_ref[...], side_ref[...]], 1)
    low_ref[...] = low
    sums_ref[...] = low_dot(low, weight_ref[...], NT)


def leave(conv, tail, outgate, side, weight):
    count, width = conv.shape[0], weight.shape[0]
    return call(
        leave_kernel,
        [shape((count, weight.shape[1]), LOW), shape((count, width))],
        [conv, tail, outgate, side, weight],
        "leave",
        7,
    )


def row_norm_back(values, gain, grad):
    inverse = lax.rsqrt(jnp.mean(values * values, -1, keepdims=True) + EPSILON)
    unit = values * inverse
    scaled = grad * gain
    back = inverse * (scaled - unit * jnp.mean(unit * scaled, -1, keepdims=True))
    return back, jnp.sum(unit * grad, 0)


def ring(value, axis, steps):
    count = lax.axis_size(axis)
    return lax.ppermute(value, axis, [(at, (at + steps) % count) for at in range(count)])


def all_seq(value):
    return [value] + [ring(value, "seq", step) for step in range(1, lax.axis_size("seq"))]


def handed_on(value, axis, steps):
    count = lax.axis_size(axis)
    first, last = max(0, -steps), min(count, count - steps)
    return lax.ppermute(value, axis, [(at, at + steps) for at in range(first, last)])


def gather_tp(values):
    return lax.all_gather(values, "tp", axis=0, tiled=True)


def scatter_tp(values):
    return lax.psum_scatter(values, "tp", scatter_dimension=0, tiled=True)


def crossed(value, bit):
    return lax.ppermute(value, "seq", [(at, at ^ bit) for at in range(lax.axis_size("seq"))])


def butterfly(value, axis):
    count = lax.axis_size(axis)
    step = 1
    while step < count:
        value = value + lax.ppermute(value, axis, [(at, at ^ step) for at in range(count)])
        step *= 2
    return value


class CoreSums:
    def __init__(self, left, right, axis):
        count = lax.axis_size("seq")
        index = lax.axis_index("seq")
        self.left, self.right, self.axis = left, right, axis
        self.chunk = (left, right)[axis].shape[1] // count
        self.core, chip, chips = index % 2, index // 2, count // 2
        self.order = [(chip + step) % chips for step in range(1, chips)] + [chip]

    def product(self, chip, core):
        place = (chip * 2 + core) * self.chunk
        left, right = self.left, self.right
        if self.axis:
            right = lax.dynamic_slice_in_dim(right, place, self.chunk, 1)
        else:
            left = lax.dynamic_slice_in_dim(left, place, self.chunk, 1)
        return tock([low_dot(tick(left), right, TN)])[0]

    def send(self):
        self.received = [crossed(self.product(at, 1 - self.core), 1) for at in self.order]
        return self

    def sums(self, *others):
        sums = []
        for at, part in zip(self.order, self.received):
            if len(sums) == len(self.order) - 1 and others:
                self.left = after(self.left, *others)
            sums.append(tock([self.product(at, self.core) + part])[0])
        return sums


def chip_moves(parts):
    return [ring(part, "seq", 2 * step) for step, part in enumerate(parts[:-1], 1)]


def total(parts, moved):
    return sum(moved, parts[-1])


def after(value, *others):
    return lax.optimization_barrier((value, *others))[0]


def after_all(parts, *others):
    return [None if part is None else after(part, *others) for part in parts]


def local(
    inputs, cotangent, doc_start, norm_in, query_weight, key_weight, value_weight, outgate_weight,
    decay_weight, beta_weight, conv_query, conv_key, conv_value, decay_log, decay_bias, head_norm,
    out_weight, norm_feed, gate_weight, up_weight, down_weight,
):
    Clock.latest = None
    query_weight, key_weight, value_weight = query_weight[0], key_weight[0], value_weight[0]
    outgate_weight, decay_weight, beta_weight = outgate_weight[0], decay_weight[0], beta_weight[0]
    gate_weight, up_weight, down_weight, out_weight = (
        gate_weight[0], up_weight[0], down_weight[0], out_weight[0],
    )
    taps = jnp.concatenate([conv_query[0], conv_key[0], conv_value[0]], 1)
    rate, bias = jnp.exp(decay_log[0]), decay_bias[0]
    heads = bias.shape[0]
    key_size = query_weight.shape[1] // heads
    value_size = value_weight.shape[1] // heads
    sizes = (heads, key_size, value_size)
    key_cols, value_cols = heads * key_size, heads * value_size
    micros, own_rows, width = inputs.shape
    rows = cotangent.shape[1]
    seq_size, seq_index = lax.axis_size("seq"), lax.axis_index("seq")
    tp_index = lax.axis_index("tp")
    section = lax.axis_index("section")
    at_start, at_end = seq_index == 0, seq_index == seq_size - 1
    order = (seq_index - jnp.arange(seq_size, dtype=jnp.int32)) % seq_size
    tp_size = lax.axis_size("tp")
    sources = (tp_index - jnp.arange(tp_size, dtype=jnp.int32)) % tp_size
    targets = (tp_index + jnp.arange(tp_size, dtype=jnp.int32)) % tp_size
    last_section = section.astype(jnp.int32).reshape(1)
    groups = 2
    group = micros // groups

    def own(values):
        return lax.dynamic_slice_in_dim(values, tp_index * own_rows, own_rows, 0)

    def whole_out_weight(whole, piece, member, members):
        for step in range(0, seq_size, 2):
            moved = ring(piece, "seq", step) if step else piece
            for at, values in (
                ((seq_index - step) % seq_size, moved),
                (((seq_index ^ 1) - step) % seq_size, crossed(moved, 1)),
            ):
                whole = narrow_into(
                    whole, values, at.astype(jnp.int32).reshape(1), width, member, members, tp_size
                )
                tock([whole])
        return whole

    spare = jnp.zeros((width, 128 - 2 * heads), LOW)
    in_weight = jnp.concatenate(
        [query_weight, key_weight, value_weight, outgate_weight, decay_weight, beta_weight, spare], 1
    )
    conv_cols = 2 * key_cols + value_cols
    offsets = jnp.arange(rows, dtype=jnp.int32)

    def micro_of(step, member):
        return jnp.clip(step - section, 0, groups - 1) * group + member

    def reset_flags(micro):
        starts = micro * (rows * seq_size) + seq_index * rows + offsets
        flags = lax.dynamic_index_in_dim(doc_start, micro, 0, keepdims=False) == starts
        return jnp.broadcast_to(flags.astype(F32)[:, None], (rows, 128))

    def enter_mixer(residual, step, member, border_carry):
        micro = micro_of(step, member)
        hidden, projected = enter(residual, norm_in, in_weight)
        moved = ring(projected[rows - 8 :, :conv_cols], "seq", 1)
        border = jnp.where(at_start, border_carry, moved)
        resets = reset_flags(micro)
        carried, local_out, maps, inverse = mixer_local(
            sizes, projected, resets, border, taps, rate, bias
        )
        saved[step, member] = dict(
            hidden=hidden, border=border, projected=projected, resets=resets, carried=carried,
            maps=all_seq(maps), inverse=inverse,
        )
        return moved, local_out

    def gate(step, member, local_out, state):
        kept = saved[step, member]
        kept["gated"], kept["output"], kept["entry_state"], state = mixer_gate(
            sizes, order, kept["maps"], state, kept["carried"], local_out, kept["projected"], head_norm
        )
        return state

    def rows_outer(name):
        return jnp.concatenate(
            [
                jnp.where(section == 0, saved[0, member][name], saved[2, member][name])
                for member in range(group)
            ],
            0,
        )

    def rows_inner(name):
        return jnp.concatenate([saved[1, member][name] for member in range(group)], 0)

    def rows_of(name):
        return jnp.concatenate([rows_outer(name), rows_inner(name)], 0)

    def rounded(values):
        zero = jnp.zeros((1,), jnp.int32)
        return tock([narrow_into(None, values, zero, width, 0, 1, tp_size)])[0]

    def enter_mixer(residual, step, member, border_carry):
        micro = micro_of(step, member)
        hidden, projected = enter(residual, norm_in, in_weight)
        moved = ring(projected[rows - 8 :, :conv_cols], "seq", 1)
        border = jnp.where(at_start, border_carry, moved)
        resets = reset_flags(micro)
        carried, local_out, maps, inverse = mixer_local(
            sizes, projected, resets, border, taps, rate, bias
        )
        saved[step, member] = dict(
            hidden=hidden, border=border, projected=projected, resets=resets, carried=carried,
            maps=all_seq(maps), inverse=inverse,
        )
        return moved, local_out

    def gate(step, member, local_out, state):
        kept = saved[step, member]
        kept["gated"], kept["output"], kept["entry_state"], state = mixer_gate(
            sizes, order, kept["maps"], state, kept["carried"], local_out, kept["projected"], head_norm
        )
        return state

    def rows_of(name):
        outer = [
            jnp.where(section == 0, saved[0, member][name], saved[2, member][name])
            for member in range(group)
        ]
        return jnp.concatenate(outer + [saved[1, member][name] for member in range(group)], 0)

    saved = {}
    section_rows = {}
    part = width // seq_size
    entering = [inputs[member].astype(F32) * (section == 0) for member in range(group)]
    residuals = [gather_tp(values) for values in entering]
    out_piece = widen(lax.dynamic_slice_in_dim(out_weight, seq_index * part, part, 1))
    out_pieces = [
        gather_tp(after(values, *entering)) for values in jnp.split(out_piece, 2, 0)
    ]
    out_full = None
    border_carry = jnp.zeros((8, conv_cols), F32)
    state = jnp.zeros((heads, key_size, value_size), F32)
    nothing = jnp.zeros((rows, width), F32)
    members = list(reversed(range(group)))
    early, late = members[0], members[-1]
    tops, feed_grads, late_sums = {}, {}, {}

    def feed(back_step, member, received, handed):
        step = groups - back_step
        kept = saved[step, member]
        given = lax.dynamic_index_in_dim(cotangent, micro_of(step, member), 0, keepdims=False)
        if step == 0:
            given = jnp.where(section == 0, given, jnp.zeros_like(given))
        kept["top_low"], kept["gate_low"], kept["up_low"], sums = feed_back(
            last_section, given, handed, kept["gate_act"], kept["up_act"],
            gate_weight, up_weight, down_weight,
        )
        tops[member] = jnp.where(section == 0, received, own(given).astype(F32))
        if step:
            feed_grads[member] = scatter_tp(sums)
        else:
            summed = scatter_tp(jnp.where(section == 0, sums, late_sums[member]))
            section_rows[groups, member] = saved[groups, member]["mixed"] + summed
            feed_grads[member] = jnp.where(section == 0, summed, 0.0)

    for step in range(groups + 1):
        all_gated = []
        for member in range(group):
            border_carry, local_out = enter_mixer(residuals[member], step, member, border_carry)
            state = gate(step, member, local_out, state)
            saved[step, member]["entering"] = entering[member]
            all_gated.append(lax.all_gather(saved[step, member]["gated"], "tp", axis=0))
        if out_full is None:
            for member, piece in enumerate(out_pieces):
                out_full = whole_out_weight(out_full, after(piece, state), member, 2)
        all_sums = []
        for member in range(group):
            kept = saved[step, member]
            mixed, kept["hidden_feed"], kept["gate_act"], kept["up_act"], kept["inner"], sums = join_heads(
                residuals[member], all_gated[member], out_full, norm_feed,
                gate_weight, up_weight, down_weight,
            )
            kept["mixed"] = own(mixed)
            if step < groups:
                all_sums.append(scatter_tp(sums))
            else:
                late_sums[member] = sums
                feed(0, member, jnp.zeros((own_rows, width), F32), nothing)
        if step == groups:
            break
        ready = None
        entering, residuals = [], []
        for member in range(group):
            summed = all_sums[member] if ready is None else after(all_sums[member], ready)
            out_rows = saved[step, member]["mixed"] + summed
            section_rows[step, member] = out_rows
            handed = handed_on(out_rows, "section", 1)
            micro = micro_of(step + 1, member)
            given = lax.dynamic_index_in_dim(inputs, micro, 0, keepdims=False).astype(F32)
            ready = jnp.where(section == 0, given, handed)
            entering.append(ready)
            residuals.append(gather_tp(ready))

    tail_carry = jnp.zeros((8, conv_cols), F32)
    state_grad = jnp.zeros((heads, key_size, value_size), F32)
    in_grads = {}
    norm_in_grad = jnp.zeros((width,), F32)
    norm_feed_grad = jnp.zeros((width,), F32)
    gain_grad = jnp.zeros((value_size,), F32)
    taps_grad = jnp.zeros(taps.shape, F32)
    side_sums = jnp.zeros((8, 128), F32)
    received, handed = [None] * group, [None] * group
    for back_step in range(groups + 1):
        step = groups - back_step
        final = back_step == groups
        if back_step:
            for member in members:
                feed(back_step, member, received[member], handed[member])
        if final:
            feed_all, top_all = rows_of("hidden_feed"), rows_of("top_low")
            gate_sums = CoreSums(feed_all, rows_of("gate_low"), 0).send()
            gate_parts = gate_sums.sums()
            gate_moved = chip_moves(gate_parts)
        all_sums = {}

        def depart(member, tail):
            kept = saved[step, member]
            kept["projected_low"], sums = leave(
                kept["conv_grad"], tail, kept["outgate_low"], kept["side_low"], in_weight
            )
            all_sums[member] = scatter_tp(sums)
            return sums

        def mix(member):
            kept = saved[step, member]
            feed_part, kept["mixed_grad"], *pieces = mix_back(
                targets, feed_grads[member], kept["mixed"], tops[member], norm_feed, out_full
            )
            return feed_part[0], [ring(piece, "tp", at) if at else piece for at, piece in enumerate(pieces)]

        for member in members:
            kept = saved[step, member]
            feed_part, pieces = mix(member)
            norm_feed_grad = norm_feed_grad + feed_part
            if final and member == early:
                up_sums = CoreSums(feed_all, rows_of("up_low"), 0).send()
            elif final:
                inner_mixed = gather_tp(rows_inner("mixed_grad"))
                outer_mixed = gather_tp(rows_outer("mixed_grad"))
            output_grad, kept["outgate_low"], gain_part, entry_grad = mixer_gate_back(
                sizes, sources, pieces, kept["output"], kept["projected"], head_norm, kept["carried"]
            )
            gain_grad = gain_grad + gain_part[0]
            all_entries = all_seq(entry_grad)
            if final and member == early:
                up_sums.left = after(up_sums.left, *gate_moved)
                up_parts = up_sums.sums()
            elif final:
                down_sums = CoreSums(after(rows_of("inner"), *up_moved), top_all, 1).send()
                down_parts = down_sums.sums()
                inner_mixed = rounded(inner_mixed)
            kept["conv_grad"], border_grad, taps_part, kept["side_low"], sums_part, state_grad = mixer_local_back(
                sizes, order, kept["maps"], all_entries, state_grad, kept["projected"],
                kept["resets"], kept["border"], taps, rate, bias, kept["inverse"],
                kept["entry_state"], output_grad,
            )
            moved = ring(border_grad, "seq", -1)
            tail = jnp.where(at_end, tail_carry, moved)
            tail_carry = moved
            if final and member == early:
                up_moved = chip_moves(after_all(up_parts, tail))
            elif final:
                down_moved = chip_moves(after_all(down_parts, tail))
                tail = after(tail, all_sums[early])
            taps_grad = taps_grad + taps_part
            side_sums = side_sums + sums_part
            last = depart(member, tail)
        ready = None
        received, handed = [None] * group, [None] * group
        if final:
            in_sums = CoreSums(rows_of("hidden"), rows_of("projected_low"), 0).send()
            in_parts = in_sums.sums(*down_moved)
            in_moved = chip_moves(in_parts)
            outer_mixed = rounded(after(outer_mixed, *in_moved))
            ready = outer_mixed
        for member in members:
            kept = saved[step, member]
            summed = all_sums[member]
            if ready is not None and (not final or member == late):
                summed = after(summed, ready)
            entering_back, in_part = row_norm_back(kept["entering"], norm_in[0], summed)
            norm_in_grad = norm_in_grad + in_part
            own_grad = kept["mixed_grad"] + entering_back
            in_grads[step, member] = own_grad
            if not final:
                ready = handed_on(own_grad, "section", -1)
                received[member] = ready
                handed[member] = gather_tp(ready)
    def of_section(values):
        return [
            jnp.where(section == 0, values[at, member], values[at + 1, member])
            for at in range(groups)
            for member in range(group)
        ]

    def by_device(values):
        split = values.astype(LOW).reshape(-1, tp_size, own_rows, value_cols)
        return jnp.moveaxis(split, 0, 1).reshape(-1, value_cols)

    out_sums = CoreSums(
        jnp.concatenate([by_device(rows_outer("gated")), by_device(rows_inner("gated"))], 0),
        jnp.concatenate([outer_mixed, inner_mixed], 0),
        1,
    )
    out_parts = out_sums.send().sums()
    grad_out = total(out_parts, chip_moves(out_parts))
    grad_gate, grad_up, grad_in, grad_down = [
        total(after_all(parts, out_parts[-1]), moved)
        for parts, moved in (
            (gate_parts, gate_moved), (up_parts, up_moved), (in_parts, in_moved),
            (down_parts, down_moved),
        )
    ]

    shared = butterfly(jnp.concatenate([norm_in_grad, norm_feed_grad, gain_grad]), "tp")
    small = butterfly(
        jnp.concatenate(
            [
                after(shared, out_parts[0]), taps_grad.reshape(-1), side_sums[0, :heads],
                side_sums[1, :heads],
            ]
        ),
        "seq",
    )
    bounds = [0, width, 2 * width, 2 * width + value_size]
    bounds += [bounds[-1] + taps.size, bounds[-1] + taps.size + heads, bounds[-1] + taps.size + 2 * heads]
    norm_in_grad, norm_feed_grad, gain_grad, taps_grad, log_grad, bias_grad = [
        small[low:high] for low, high in zip(bounds[:-1], bounds[1:])
    ]
    taps_grad = taps_grad.reshape(taps.shape)
    bounds = [
        0, key_cols, 2 * key_cols, conv_cols, conv_cols + value_cols, conv_cols + value_cols + heads,
        conv_cols + value_cols + 2 * heads,
    ]
    in_parts = [grad_in[:, low:high] for low, high in zip(bounds[:-1], bounds[1:])]
    return (
        jnp.stack(of_section(section_rows))[None],
        jnp.stack(of_section(in_grads))[None],
        norm_in_grad[None],
        *[member[None] for member in in_parts],
        taps_grad[None, :, :key_cols],
        taps_grad[None, :, key_cols : 2 * key_cols],
        taps_grad[None, :, 2 * key_cols :],
        log_grad[None],
        bias_grad[None],
        gain_grad[None],
        grad_out[None],
        norm_feed_grad[None],
        grad_gate[None],
        grad_up[None],
        grad_down[None],
    )


def solution(mesh):
    by_column, by_row = P("section", None, "tp"), P("section", "tp", None)
    placed = (
        P(None, ("seq", "tp"), None),
        P(None, "seq", None),
        P(None, "seq"),
        P("section", None),
        *[by_column] * 9,
        P("section", "tp"),
        P("section", "tp"),
        P("section", None),
        by_row,
        P("section", None),
        by_column,
        by_column,
        by_row,
    )
    rows_out = P("section", None, ("seq", "tp"), None)
    both = P("section", "seq", "tp")
    return jax.shard_map(
        local,
        mesh=mesh,
        in_specs=placed,
        out_specs=(
            rows_out,
            rows_out,
            P("section", None),
            *[both] * 6,
            *[by_column] * 3,
            P("section", "tp"),
            P("section", "tp"),
            P("section", None),
            P("section", "tp", "seq"),
            P("section", None),
            both,
            both,
            P("section", "tp", "seq"),
        ),
        check_vma=False,
    )
```

```python
from functools import partial

import jax
import jax.numpy as jnp
from jax import lax
from jax.experimental import pallas as pl
from jax.experimental.pallas import tpu as pltpu
from jax.sharding import PartitionSpec as P

EPSILON = 1e-06
F32 = jnp.float32
LOW = jnp.bfloat16
VMEM_BYTES = 48 * 1024 * 1024
NN = ((1,), (0,))
NT = ((1,), (1,))
TN = ((0,), (0,))


def low_dot(a, b, contract=NN):
    return lax.dot_general(a, b, (contract, ((), ())), preferred_element_type=F32)


def halves(x):
    high = x.astype(LOW)
    return high, (x - high.astype(F32)).astype(LOW)


def thirds(x):
    high = x.astype(LOW)
    rest = x - high.astype(F32)
    middle = rest.astype(LOW)
    return high, middle, (rest - middle.astype(F32)).astype(LOW)


def pair_dot(a, b, contract=NN):
    left, right = contract[0][0], contract[1][0]
    return low_dot(
        jnp.concatenate([a[0], a[0], a[1]], left),
        jnp.concatenate([b[0], b[1], b[0]], right),
        contract,
    )


def fine_dot(a, b, contract=NN):
    return pair_dot(halves(a), halves(b), contract)


def sigmoid(x):
    return 1.0 / (1.0 + jnp.exp(-x))


def places(size):
    return (
        lax.broadcasted_iota(jnp.int32, (size, size), 0),
        lax.broadcasted_iota(jnp.int32, (size, size), 1),
    )


def unit_lower_inverses(strict_parts, rows, cols):
    size = strict_parts[0].shape[0]
    near = (rows >> 3) == (cols >> 3)
    eye = jnp.where(rows == cols, 1.0, 0.0)
    inner = [jnp.where(near, part, 0.0) for part in strict_parts]
    split = [halves(part) for part in inner]
    second = [halves(pair_dot(part, part)) for part in split]
    fourth = [halves(pair_dot(part, part)) for part in second]
    inverse = [eye - part for part in inner]
    inverse = [part + pair_dot(halves(part), power) for part, power in zip(inverse, second)]
    inverse = [part + pair_dot(halves(part), power) for part, power in zip(inverse, fourth)]
    level = 3
    while (1 << level) < size:
        joined = ((rows >> (level + 1)) == (cols >> (level + 1))) & ((rows >> level) != (cols >> level))
        split = [halves(part) for part in inverse]
        middle = [
            halves(pair_dot(halves(jnp.where(joined, strict, 0.0)), part))
            for strict, part in zip(strict_parts, split)
        ]
        inverse = [
            part - pair_dot(pair, between) for part, pair, between in zip(inverse, split, middle)
        ]
        level += 1
    return inverse


def taps_back(padded, steps):
    rolled = padded if steps == 0 else pltpu.roll(padded, steps, 0)
    return rolled[8:]


def conv_sum(padded, taps):
    count = taps.shape[0]
    total = taps[0:1] * taps_back(padded, count - 1)
    for member in range(1, count):
        total = total + taps[member : member + 1] * taps_back(padded, count - 1 - member)
    return total


def conv_transposed(grad, taps):
    count = taps.shape[0]
    padded = jnp.concatenate([jnp.zeros((8, grad.shape[1]), F32), grad], 0)
    size = padded.shape[0]
    total = taps[count - 1 : count] * padded
    for member in range(count - 1):
        total = total + taps[member : member + 1] * pltpu.roll(padded, size - (count - 1 - member), 0)
    return total


def conv_taps_grad(padded, grad, count):
    return jnp.concatenate(
        [
            jnp.sum(grad * taps_back(padded, count - 1 - member), 0, keepdims=True)
            for member in range(count)
        ],
        0,
    )


def softplus(x):
    return jnp.maximum(x, 0.0) + jnp.log(1.0 + jnp.exp(-jnp.abs(x)))


class Gates:
    def __init__(self, side, resets, head, heads, rate, bias, rows, cols):
        size = side.shape[0]
        self.rate = rate
        self.shifted = side[:, head : head + 1] + bias
        self.log_decay = -rate * softplus(self.shifted)
        self.beta = sigmoid(side[:, heads + head : heads + head + 1])
        lanes = lax.broadcasted_iota(jnp.int32, (size, 128), 1)
        pair = jnp.where(lanes == 0, self.log_decay, jnp.where(lanes == 1, resets, 0.0))
        lower = jnp.where(rows >= cols, 1.0, 0.0).astype(LOW)
        split = thirds(pair)
        as_columns = low_dot(
            jnp.concatenate([lower] * 3, 1), jnp.concatenate(split, 0)
        )
        as_rows = low_dot(
            jnp.concatenate(split, 0), jnp.concatenate([lower] * 3, 1), ((0,), (1,))
        )
        total, count = as_columns[:, 0:1], as_columns[:, 1:2]
        linked = (jnp.abs(count - as_rows[1:2, :]) < 0.5) & (rows >= cols)
        self.decays = jnp.where(linked, jnp.exp(jnp.minimum(total - as_rows[0:1, :], 0.0)), 0.0)
        last_total, last_count = total[size - 1 : size], count[size - 1 : size]
        self.head_decay = jnp.where(count < 0.5, jnp.exp(total), 0.0)
        self.tail_decay = jnp.where(
            jnp.abs(count - last_count) < 0.5, jnp.exp(jnp.minimum(last_total - total, 0.0)), 0.0
        )


def silu_unit(summed, scale):
    gate = sigmoid(summed)
    act = summed * gate
    inverse = lax.rsqrt(jnp.sum(act * act, 1, keepdims=True) + EPSILON)
    return act, gate, inverse, act * (inverse * scale)


def silu_unit_back(grad, summed, gate, act, inverse, scale):
    unit = act * inverse
    grad = grad * scale
    act_grad = inverse * (grad - unit * jnp.sum(grad * unit, 1, keepdims=True))
    return act_grad * gate * (1.0 + summed * (1.0 - gate))


def head_columns(sizes, head):
    heads, key_size, value_size = sizes
    base = 2 * heads * key_size
    return (
        slice(head * key_size, (head + 1) * key_size),
        slice((heads + head) * key_size, (heads + head + 1) * key_size),
        slice(base + head * value_size, base + (head + 1) * value_size),
    )


def side_columns(sizes):
    heads, key_size, value_size = sizes
    start = 2 * heads * (key_size + value_size)
    return slice(start, start + 128)


def local_kernel(
    sizes, projected_ref, resets_ref, border_ref, taps_ref, rate_ref, bias_ref,
    carried_ref, local_ref, map_ref, inverse_ref,
):
    heads, key_size, value_size = sizes
    size = projected_ref.shape[0]
    rows, cols = places(size)
    side, resets = projected_ref[:, side_columns(sizes)], resets_ref[:, 0:1]
    gates, queries, keys, values, mixing = [], [], [], [], []
    for head in range(heads):
        gate = Gates(side, resets, head, heads, rate_ref[head], bias_ref[head], rows, cols)
        summed = [
            conv_sum(jnp.concatenate([border_ref[:, at], projected_ref[:, at]], 0), taps_ref[:, at])
            for at in head_columns(sizes, head)
        ]
        gates.append(gate)
        queries.append(silu_unit(summed[0], key_size**-0.5)[3])
        keys.append(silu_unit(summed[1], 1.0)[3])
        values.append(summed[2] * sigmoid(summed[2]))
        split = halves(keys[head])
        gram = pair_dot(split, split, NT)
        mixing.append(gate.beta * jnp.where(rows > cols, gate.decays * gram, 0.0))
    inverses = [halves(part) for part in unit_lower_inverses(mixing, rows, cols)]
    krows, kcols = places(key_size)
    for head in range(heads):
        gate, query, key, value, inverse = (
            gates[head], queries[head], keys[head], values[head], inverses[head],
        )
        inverse_ref[head, 0] = inverse[0]
        inverse_ref[head, 1] = inverse[1]
        both = halves(
            pair_dot(
                inverse,
                halves(jnp.concatenate([(gate.beta * gate.head_decay) * key, gate.beta * value], 1)),
            )
        )
        scores = fine_dot(query, key, NT) * gate.decays
        read = pair_dot(halves(scores), both)
        carried_ref[:, head * key_size : (head + 1) * key_size] = (
            gate.head_decay * query - read[:, :key_size]
        )
        local_ref[:, head * value_size : (head + 1) * value_size] = read[:, key_size:]
        written = pair_dot(halves(key * gate.tail_decay), both, TN)
        kept = jnp.where(krows == kcols, gate.head_decay[size - 1 : size], 0.0)
        map_ref[head, :, :key_size] = kept - written[:, :key_size]
        map_ref[head, :, key_size:] = written[:, key_size:]


def pick(refs, index, head):
    value = refs[0][head]
    for at in range(1, len(refs)):
        value = jnp.where(index == at, refs[at][head], value)
    return value


def gate_kernel(sizes, count, order_ref, *refs):
    heads, key_size, value_size = sizes
    maps = refs[:count]
    (
        state_ref, carried_ref, local_ref, outgate_ref, gain_ref, gated_ref, output_ref, entry_ref, end_ref,
    ) = refs[count:]
    states = [state_ref[head] for head in range(heads)]
    entries = list(states)
    for at in range(count):
        index = order_ref[at]
        for head in range(heads):
            if at:
                entries[head] = jnp.where(index == 0, states[head], entries[head])
            step = pick(maps, index, head)
            states[head] = fine_dot(step[:, :key_size], states[head]) + step[:, key_size:]
    for head in range(heads):
        at = slice(head * value_size, (head + 1) * value_size)
        entry_ref[head] = entries[head]
        end_ref[head] = states[head]
        output = local_ref[:, at] + fine_dot(
            carried_ref[:, head * key_size : (head + 1) * key_size], entries[head]
        )
        output_ref[:, at] = output
        normed = output * lax.rsqrt(jnp.mean(output * output, 1, keepdims=True) + EPSILON)
        gate = outgate_ref[:, at]
        gated_ref[:, at] = (normed * gain_ref[...] * (gate * sigmoid(gate))).astype(LOW).astype(F32)


def gate_back_kernel(sizes, count, order_ref, *refs):
    heads, key_size, value_size = sizes
    pieces = refs[:count]
    (
        output_ref, outgate_ref, gain_ref, carried_ref,
        output_grad_ref, outgate_grad_ref, gain_grad_ref, entry_ref, grads,
    ) = refs[count:]
    part = pieces[0].shape[0]
    for at, piece in enumerate(pieces):
        grads[pl.ds(pl.multiple_of(order_ref[at] * part, part), part), :] = piece[...]
    gain = gain_ref[...]
    total = jnp.zeros_like(gain)
    for head in range(heads):
        at = slice(head * value_size, (head + 1) * value_size)
        grad, output, gate = grads[:, at], output_ref[:, at], outgate_ref[:, at]
        inverse = lax.rsqrt(jnp.mean(output * output, 1, keepdims=True) + EPSILON)
        unit = output * inverse
        opened = sigmoid(gate)
        swished = gate * opened
        outgate_grad_ref[:, at] = (
            grad * unit * gain * (opened * (1.0 + gate * (1.0 - opened)))
        ).astype(LOW)
        total = total + jnp.sum(grad * unit * swished, 0, keepdims=True)
        unit_grad = grad * gain * swished
        output_grad = inverse * (unit_grad - unit * jnp.mean(unit_grad * unit, 1, keepdims=True))
        output_grad_ref[:, at] = output_grad
        entry_ref[head] = fine_dot(
            carried_ref[:, head * key_size : (head + 1) * key_size], output_grad, TN
        )
    gain_grad_ref[...] = total


def mix_back_kernel(count, target_ref, grad_ref, mixed_ref, top_ref, gain_ref, weight_ref, sum_ref, *refs):
    values, grad = mixed_ref[...], grad_ref[...]
    inverse = lax.rsqrt(jnp.mean(values * values, 1, keepdims=True) + EPSILON)
    unit = values * inverse
    scaled = grad * gain_ref[...]
    mixed_grad = top_ref[...] + inverse * (scaled - unit * jnp.mean(unit * scaled, 1, keepdims=True))
    refs[0][...] = mixed_grad
    sum_ref[...] = jnp.sum(unit * grad, 0, keepdims=True)
    low = mixed_grad.astype(LOW)
    part = weight_ref.shape[0] // count
    for at in range(count):
        place = pl.multiple_of(target_ref[at] * part, part)
        refs[1 + at][...] = low_dot(low, weight_ref[pl.ds(place, part), :], NT)


def local_back_kernel(sizes, count, order_ref, *refs):
    heads, key_size, value_size = sizes
    maps, entries = refs[:count], refs[count : 2 * count]
    (
        state_grad_ref, projected_ref, resets_ref, border_ref, taps_ref, rate_ref, bias_ref,
        inverse_ref, entry_state_ref, output_grad_ref,
        conv_grad_ref, border_grad_ref, taps_grad_ref, side_grad_ref, sums_ref, start_grad_ref,
    ) = refs[2 * count :]
    size = projected_ref.shape[0]
    scale = key_size**-0.5
    state_grads = [state_grad_ref[head] for head in range(heads)]
    end_grads = list(state_grads)
    for at in reversed(range(count)):
        index = order_ref[at]
        for head in range(heads):
            if at < count - 1:
                end_grads[head] = jnp.where(index == 0, state_grads[head], end_grads[head])
            step = pick(maps, index, head)[:, :key_size]
            state_grads[head] = fine_dot(step, state_grads[head], TN) + pick(entries, index, head)
    rows, cols = places(size)
    strict = rows > cols
    lower = jnp.where(rows >= cols, 1.0, 0.0).astype(LOW)
    lanes = lax.broadcasted_iota(jnp.int32, (size, 128), 1)
    at_row = lax.broadcasted_iota(jnp.int32, (size, 1), 0)
    sum_lanes = lax.broadcasted_iota(jnp.int32, (8, 128), 1)
    sum_rows = lax.broadcasted_iota(jnp.int32, (8, 128), 0)
    side, resets = projected_ref[:, side_columns(sizes)], resets_ref[:, 0:1]
    side_grad = jnp.zeros((size, 128), F32)
    sums = jnp.zeros((8, 128), F32)
    for head in range(heads):
        start_grad_ref[head] = state_grads[head]
        gate = Gates(side, resets, head, heads, rate_ref[head], bias_ref[head], rows, cols)
        columns = head_columns(sizes, head)
        padded = [jnp.concatenate([border_ref[:, at], projected_ref[:, at]], 0) for at in columns]
        summed = [conv_sum(part, taps_ref[:, at]) for part, at in zip(padded, columns)]
        act_q, gate_q, inverse_q, query = silu_unit(summed[0], scale)
        act_k, gate_k, inverse_k, key = silu_unit(summed[1], 1.0)
        gate_v = sigmoid(summed[2])
        value = summed[2] * gate_v
        beta, decays, head_decay, tail_decay = gate.beta, gate.decays, gate.head_decay, gate.tail_decay
        end_grad, state = end_grads[head], entry_state_ref[head]
        inverse = (inverse_ref[head, 0], inverse_ref[head, 1])
        output_grad = halves(output_grad_ref[:, head * value_size : (head + 1) * value_size])
        query_s, key_s, state_s, end_s = halves(query), halves(key), halves(state), halves(end_grad)

        gram = pair_dot(key_s, key_s, NT)
        pure = pair_dot(query_s, key_s, NT)
        residue = value - head_decay * pair_dot(key_s, state_s)
        update = halves(pair_dot(inverse, halves(beta * residue)))
        update_grad = pair_dot(halves(pure * decays), output_grad, TN) + pair_dot(
            halves(key * tail_decay), end_s
        )
        target_grad = pair_dot(inverse, halves(update_grad), TN)
        target_s = halves(target_grad)
        weighted = jnp.where(strict, -pair_dot(target_s, update, NT), 0.0) * decays
        pure_grad = pair_dot(output_grad, update, NT) * decays
        reached = pair_dot(output_grad, state_s, NT)
        erased = pair_dot(target_s, state_s, NT)
        kept = pair_dot(update, end_s, NT)
        gram_grad = weighted * beta
        pure_s, gram_s = halves(pure_grad), halves(gram_grad)
        query_grad = head_decay * reached + pair_dot(pure_s, key_s)
        key_grad = (
            pair_dot(pure_s, query_s, TN)
            + tail_decay * kept
            - (beta * head_decay) * erased
            + pair_dot(gram_s, key_s)
            + pair_dot(gram_s, key_s, TN)
        )
        value_grad = beta * target_grad
        beta_grad = jnp.sum(target_grad * residue, 1, keepdims=True) + jnp.sum(
            weighted * gram, 1, keepdims=True
        )
        spread = pure_grad * pure + gram_grad * gram
        head_decay_grad = jnp.sum(query * reached, 1, keepdims=True) - beta * jnp.sum(
            key * erased, 1, keepdims=True
        )
        tail_part = tail_decay * jnp.sum(key * kept, 1, keepdims=True)
        spread_s = jnp.concatenate(thirds(spread), 0)
        column_sums = low_dot(spread_s, jnp.ones((3 * size, 128), LOW), TN)[:, 0:1]
        total_grad = (
            head_decay * head_decay_grad - tail_part + jnp.sum(spread, 1, keepdims=True) - column_sums
        )
        last_grad = jnp.sum(tail_part, 0, keepdims=True) + head_decay[size - 1 : size] * jnp.sum(
            jnp.sum(end_grad * state, 1, keepdims=True), 0, keepdims=True
        )
        total_grad = total_grad + jnp.where(at_row == size - 1, last_grad, 0.0)
        total_s = jnp.concatenate(thirds(jnp.where(lanes == 0, total_grad, 0.0)), 0)
        log_grad = low_dot(jnp.concatenate([lower] * 3, 0), total_s, TN)[:, 0:1]
        decay_grad = log_grad * (-gate.rate) * sigmoid(gate.shifted)
        beta_in_grad = beta_grad * beta * (1.0 - beta)
        side_grad = jnp.where(
            lanes == head, decay_grad, jnp.where(lanes == heads + head, beta_in_grad, side_grad)
        )
        log_sum = jnp.sum(log_grad * gate.log_decay, 0, keepdims=True)
        bias_sum = jnp.sum(decay_grad, 0, keepdims=True)
        sums = jnp.where(
            (sum_lanes == head) & (sum_rows == 0),
            log_sum,
            jnp.where((sum_lanes == head) & (sum_rows == 1), bias_sum, sums),
        )
        grads = (
            silu_unit_back(query_grad, summed[0], gate_q, act_q, inverse_q, scale),
            silu_unit_back(key_grad, summed[1], gate_k, act_k, inverse_k, 1.0),
            value_grad * gate_v * (1.0 + summed[2] * (1.0 - gate_v)),
        )
        for grad, part, at in zip(grads, padded, columns):
            spread_out = conv_transposed(grad, taps_ref[:, at])
            border_grad_ref[:, at] = spread_out[:8]
            conv_grad_ref[:, at] = spread_out[8:]
            taps_grad_ref[:, at] = conv_taps_grad(part, grad, taps_ref.shape[0])
    side_grad_ref[...] = side_grad.astype(LOW)
    sums_ref[...] = sums


class Clock:
    latest = None


def tick(value):
    if Clock.latest is None:
        return value
    return lax.optimization_barrier((value, Clock.latest))[0]


def tock(results):
    Clock.latest = min(results, key=lambda array: array.size)
    return results


def smem():
    return pl.BlockSpec(memory_space=pltpu.SMEM)


def anywhere():
    return pl.BlockSpec(memory_space=pl.ANY)


def call(kernel, out_shape, operands, name, micros, in_specs=None, scratch=(), vmem=VMEM_BYTES):
    whole = lambda array: pl.BlockSpec(array.shape, lambda i: (0,) * len(array.shape))
    vectors = [at for at in range(len(operands)) if in_specs is None or in_specs[at] is None]
    least = min(vectors, key=lambda at: operands[at].size)
    operands = list(operands)
    operands[least] = tick(operands[least])
    specs = [whole(array) for array in operands] if in_specs is None else in_specs
    specs = [whole(array) if spec is None else spec for spec, array in zip(specs, operands)]
    results = pl.pallas_call(
        kernel,
        grid=(1,),
        in_specs=specs,
        out_specs=[whole(array) for array in out_shape],
        out_shape=out_shape,
        scratch_shapes=list(scratch),
        compiler_params=pltpu.CompilerParams(vmem_limit_bytes=vmem),
        cost_estimate=pl.CostEstimate(
            flops=int(micros * 1e+07), bytes_accessed=int(micros * 30000), transcendentals=0
        ),
        name=name,
    )(*operands)
    return tock(results)


def shape(dims, dtype=F32):
    return jax.ShapeDtypeStruct(tuple(dims), dtype)


def columns_spec(rows, width, at):
    return pl.BlockSpec((rows, width), lambda i: (0, at))


def mixer_local(sizes, projected, resets, border, taps, rate, bias):
    heads, key_size, value_size = sizes
    rows = projected.shape[0]
    return call(
        partial(local_kernel, sizes),
        [
            shape((rows, heads * key_size)),
            shape((rows, heads * value_size)),
            shape((heads, key_size, key_size + value_size)),
            shape((heads, 2, rows, rows), LOW),
        ],
        [projected, resets, border, taps, rate, bias],
        "mixer_local",
        12,
        [None, None, None, None, smem(), smem()],
    )


def mixer_gate(sizes, order, maps, state, carried, local, projected, gain):
    heads, key_size, value_size = sizes
    rows = projected.shape[0]
    count = len(maps)
    value_cols = heads * value_size
    outgate = columns_spec(rows, value_cols, (2 * heads * key_size + value_cols) // value_cols)
    return call(
        partial(gate_kernel, sizes, count),
        [
            shape((rows, value_cols)),
            shape((rows, value_cols)),
            shape((heads, key_size, value_size)),
            shape((heads, key_size, value_size)),
        ],
        [order, *maps, state, carried, local, projected, gain],
        "mixer_gate",
        5,
        [smem()] + [None] * (count + 3) + [outgate, None],
    )


def mix_back(target, grad, mixed, top, gain, weight):
    rows, width = grad.shape
    count = target.shape[0]
    return call(
        partial(mix_back_kernel, count),
        [shape((1, width)), shape((rows, width))] + [shape((rows, weight.shape[0] // count))] * count,
        [target, grad, mixed, top, gain, weight],
        "mix_back",
        5,
        [smem()] + [None] * 5,
    )


def mixer_gate_back(sizes, order, pieces, output, projected, gain, carried):
    heads, key_size, value_size = sizes
    rows = projected.shape[0]
    count = len(pieces)
    value_cols = heads * value_size
    outgate = columns_spec(rows, value_cols, (2 * heads * key_size + value_cols) // value_cols)
    return call(
        partial(gate_back_kernel, sizes, count),
        [
            shape((rows, value_cols)),
            shape((rows, value_cols), LOW),
            shape((1, value_size)),
            shape((heads, key_size, value_size)),
        ],
        [order, *pieces, output, projected, gain, carried],
        "mixer_gate_back",
        4,
        [smem()] + [None] * (count + 1) + [outgate, None, None],
        [pltpu.VMEM((rows, value_cols), F32)],
    )


def mixer_local_back(
    sizes, order, maps, entries, state_grad, projected, resets, border, taps, rate, bias, inverse,
    entry_state, output_grad,
):
    heads, key_size, value_size = sizes
    rows = projected.shape[0]
    count = len(maps)
    conv_cols = taps.shape[1]
    return call(
        partial(local_back_kernel, sizes, count),
        [
            shape((rows, conv_cols)),
            shape((8, conv_cols)),
            shape(taps.shape),
            shape((rows, 128), LOW),
            shape((8, 128)),
            shape((heads, key_size, value_size)),
        ],
        [
            order, *maps, *entries, state_grad, projected, resets, border, taps, rate, bias, inverse,
            entry_state, output_grad,
        ],
        "mixer_local_back",
        12,
        [smem()] + [None] * (2 * count + 5) + [smem(), smem(), None, None, None],
    )


def recast_kernel(index_ref, source_ref, *refs):
    refs[-1][...] = source_ref[...].astype(refs[-1].dtype)


def widen(values):
    rows, cols = values.shape
    tile = min(rows, 256)
    spec = pl.BlockSpec((tile, cols), lambda i, index: (i, 0))
    return pl.pallas_call(
        recast_kernel,
        grid_spec=pltpu.PrefetchScalarGridSpec(
            num_scalar_prefetch=1, grid=(rows // tile,), in_specs=[spec], out_specs=spec
        ),
        out_shape=shape((rows, cols)),
        name="widen",
    )(jnp.zeros((1,), jnp.int32), values)


def narrow_into(whole, values, index, total, member, members, pieces):
    rows, cols = values.shape
    tile = rows // pieces
    source = pl.BlockSpec((tile, cols), lambda i, index: (i, 0))
    placed = pl.BlockSpec((tile, cols), lambda i, index: (i * members + member, index[0]))
    more = [] if whole is None else [whole]
    return pl.pallas_call(
        recast_kernel,
        grid_spec=pltpu.PrefetchScalarGridSpec(
            num_scalar_prefetch=1,
            grid=(pieces,),
            in_specs=[source] + [anywhere()] * len(more),
            out_specs=placed,
        ),
        out_shape=shape((rows * members, total), LOW),
        input_output_aliases={2: 0} if more else {},
        name="narrow_into",
    )(tick(index), values, *more)


def choose_kernel(first_ref, own_ref, other_ref, low_ref):
    low_ref[...] = jnp.where(first_ref[0] == 1, own_ref[...], other_ref[...]).astype(LOW)


def choose(first, paired, single, member, members, pieces):
    rows, cols = single.shape
    tile = rows // pieces
    return pl.pallas_call(
        choose_kernel,
        grid=(pieces,),
        in_specs=[
            smem(),
            pl.BlockSpec((tile, cols), lambda i: (i, 0)),
            pl.BlockSpec((tile, cols), lambda i: (i * members + member, 0)),
        ],
        out_specs=pl.BlockSpec((tile, cols), lambda i: (i, 0)),
        out_shape=shape((rows, cols), LOW),
        name="choose",
    )(tick(first), single, paired)


def enter_kernel(rows_ref, gain_ref, weight_ref, hidden_ref, projected_ref):
    values = rows_ref[...]
    inverse = lax.rsqrt(jnp.mean(values * values, 1, keepdims=True) + EPSILON)
    hidden = (values * inverse * gain_ref[...]).astype(LOW)
    hidden_ref[...] = hidden
    projected_ref[...] = low_dot(hidden, weight_ref[...])


def enter(rows, gain, weight):
    count, width = rows.shape
    return call(
        enter_kernel,
        [shape((count, width), LOW), shape((count, weight.shape[1]))],
        [rows, gain, weight],
        "enter",
        6,
    )


def join_kernel(
    rows_ref, gated_ref, weight_ref, gain_ref, gate_hbm, up_hbm, down_hbm,
    mixed_ref, hidden_ref, gate_ref, up_ref, inner_ref, sums_ref,
    gate_weight, up_weight, down_weight, arrived,
):
    copies = [
        pltpu.make_async_copy(source, target, arrived.at[at])
        for at, (source, target) in enumerate(
            ((gate_hbm, gate_weight), (up_hbm, up_weight), (down_hbm, down_weight))
        )
    ]
    for copy in copies:
        copy.start()
    depth = gated_ref.shape[2]
    mixed = rows_ref[...]
    for part in range(gated_ref.shape[0]):
        mixed = mixed + low_dot(
            gated_ref[part].astype(LOW), weight_ref[part * depth : (part + 1) * depth, :]
        )
    mixed_ref[...] = mixed
    inverse = lax.rsqrt(jnp.mean(mixed * mixed, 1, keepdims=True) + EPSILON)
    hidden = (mixed * inverse * gain_ref[...]).astype(LOW)
    hidden_ref[...] = hidden
    copies[0].wait()
    gate = low_dot(hidden, gate_weight[...])
    gate_ref[...] = gate
    copies[1].wait()
    up = low_dot(hidden, up_weight[...])
    up_ref[...] = up
    inner = (gate * sigmoid(gate) * up).astype(LOW)
    inner_ref[...] = inner
    copies[2].wait()
    sums_ref[...] = low_dot(inner, down_weight[...])


def join_heads(rows, gated, weight, gain, gate_weight, up_weight, down_weight):
    count, width = rows.shape
    hidden = gate_weight.shape[1]
    return call(
        join_kernel,
        [
            shape((count, width)),
            shape((count, width), LOW),
            shape((count, hidden)),
            shape((count, hidden)),
            shape((count, hidden), LOW),
            shape((count, width)),
        ],
        [rows, gated, weight, gain, gate_weight, up_weight, down_weight],
        "join_heads",
        12,
        [None] * 4 + [anywhere()] * 3,
        [
            pltpu.VMEM(gate_weight.shape, LOW),
            pltpu.VMEM(up_weight.shape, LOW),
            pltpu.VMEM(down_weight.shape, LOW),
            pltpu.SemaphoreType.DMA((3,)),
        ],
        56 * 1024 * 1024,
    )


def feed_back_kernel(
    last_ref, given_ref, handed_ref, gate_ref, up_ref, gate_hbm, up_hbm, down_hbm,
    top_ref, gate_grad_ref, up_grad_ref, sums_ref, gate_weight, up_weight, down_weight, arrived,
):
    copies = [
        pltpu.make_async_copy(source, target, arrived.at[at])
        for at, (source, target) in enumerate(
            ((down_hbm, down_weight), (gate_hbm, gate_weight), (up_hbm, up_weight))
        )
    ]
    for copy in copies:
        copy.start()
    top = jnp.where(last_ref[0] == 1, given_ref[...].astype(F32), handed_ref[...]).astype(LOW)
    top_ref[...] = top
    copies[0].wait()
    grad = low_dot(top, down_weight[...], NT)
    gate = gate_ref[...]
    opened = sigmoid(gate)
    gate_grad = (grad * up_ref[...] * (opened * (1.0 + gate * (1.0 - opened)))).astype(LOW)
    up_grad = (grad * gate * opened).astype(LOW)
    gate_grad_ref[...] = gate_grad
    up_grad_ref[...] = up_grad
    copies[1].wait()
    sums = low_dot(gate_grad, gate_weight[...], NT)
    copies[2].wait()
    sums_ref[...] = sums + low_dot(up_grad, up_weight[...], NT)


def feed_back(last, given, handed, gate_act, up_act, gate_weight, up_weight, down_weight):
    count, width = given.shape
    hidden = gate_weight.shape[1]
    return call(
        feed_back_kernel,
        [
            shape((count, width), LOW),
            shape((count, hidden), LOW),
            shape((count, hidden), LOW),
            shape((count, width)),
        ],
        [last, given, handed, gate_act, up_act, gate_weight, up_weight, down_weight],
        "feed_back",
        12,
        [smem()] + [None] * 4 + [anywhere()] * 3,
        [
            pltpu.VMEM(gate_weight.shape, LOW),
            pltpu.VMEM(up_weight.shape, LOW),
            pltpu.VMEM(down_weight.shape, LOW),
            pltpu.SemaphoreType.DMA((3,)),
        ],
    )


def leave_kernel(conv_ref, tail_ref, outgate_ref, side_ref, weight_ref, low_ref, sums_ref):
    rows, conv_cols = conv_ref.shape
    conv = conv_ref[...]
    conv = jnp.concatenate([conv[: rows - 8], conv[rows - 8 :] + tail_ref[...]], 0)
    low = jnp.concatenate([conv.astype(LOW), outgate_ref[...], side_ref[...]], 1)
    low_ref[...] = low
    sums_ref[...] = low_dot(low, weight_ref[...], NT)


def leave(conv, tail, outgate, side, weight):
    count, width = conv.shape[0], weight.shape[0]
    return call(
        leave_kernel,
        [shape((count, weight.shape[1]), LOW), shape((count, width))],
        [conv, tail, outgate, side, weight],
        "leave",
        7,
    )


def row_norm_back(values, gain, grad):
    inverse = lax.rsqrt(jnp.mean(values * values, -1, keepdims=True) + EPSILON)
    unit = values * inverse
    scaled = grad * gain
    back = inverse * (scaled - unit * jnp.mean(unit * scaled, -1, keepdims=True))
    return back, jnp.sum(unit * grad, 0)


def ring(value, axis, steps):
    count = lax.axis_size(axis)
    return lax.ppermute(value, axis, [(at, (at + steps) % count) for at in range(count)])


def all_seq(value):
    return [value] + [ring(value, "seq", step) for step in range(1, lax.axis_size("seq"))]


def handed_on(value, axis, steps):
    count = lax.axis_size(axis)
    first, last = max(0, -steps), min(count, count - steps)
    return lax.ppermute(value, axis, [(at, at + steps) for at in range(first, last)])


def gather_tp(values):
    return lax.all_gather(values, "tp", axis=0, tiled=True)


def scatter_tp(values):
    return lax.psum_scatter(values, "tp", scatter_dimension=0, tiled=True)


def crossed(value, bit):
    return lax.ppermute(value, "seq", [(at, at ^ bit) for at in range(lax.axis_size("seq"))])


def butterfly(value, axis):
    count = lax.axis_size(axis)
    step = 1
    while step < count:
        value = value + lax.ppermute(value, axis, [(at, at ^ step) for at in range(count)])
        step *= 2
    return value


class CoreSums:
    def __init__(self, left, right, axis):
        count = lax.axis_size("seq")
        index = lax.axis_index("seq")
        self.left, self.right, self.axis = left, right, axis
        self.chunk = (left, right)[axis].shape[1] // count
        self.core, chip, chips = index % 2, index // 2, count // 2
        self.order = [(chip + step) % chips for step in range(1, chips)] + [chip]

    def product(self, chip, core):
        place = (chip * 2 + core) * self.chunk
        left, right = self.left, self.right
        if self.axis:
            right = lax.dynamic_slice_in_dim(right, place, self.chunk, 1)
        else:
            left = lax.dynamic_slice_in_dim(left, place, self.chunk, 1)
        return tock([low_dot(tick(left), right, TN)])[0]

    def send(self):
        self.received = [crossed(self.product(at, 1 - self.core), 1) for at in self.order]
        return self

    def sums(self, *others):
        sums = []
        for at, part in zip(self.order, self.received):
            if len(sums) == len(self.order) - 1 and others:
                self.left = after(self.left, *others)
            sums.append(tock([self.product(at, self.core) + part])[0])
        return sums


def chip_moves(parts):
    return [ring(part, "seq", 2 * step) for step, part in enumerate(parts[:-1], 1)]


def total(parts, moved):
    return sum(moved, parts[-1])


def after(value, *others):
    return lax.optimization_barrier((value, *others))[0]


def after_all(parts, *others):
    return [None if part is None else after(part, *others) for part in parts]


def local(
    inputs, cotangent, doc_start, norm_in, query_weight, key_weight, value_weight, outgate_weight,
    decay_weight, beta_weight, conv_query, conv_key, conv_value, decay_log, decay_bias, head_norm,
    out_weight, norm_feed, gate_weight, up_weight, down_weight,
):
    Clock.latest = None
    query_weight, key_weight, value_weight = query_weight[0], key_weight[0], value_weight[0]
    outgate_weight, decay_weight, beta_weight = outgate_weight[0], decay_weight[0], beta_weight[0]
    gate_weight, up_weight, down_weight, out_weight = (
        gate_weight[0], up_weight[0], down_weight[0], out_weight[0],
    )
    taps = jnp.concatenate([conv_query[0], conv_key[0], conv_value[0]], 1)
    rate, bias = jnp.exp(decay_log[0]), decay_bias[0]
    heads = bias.shape[0]
    key_size = query_weight.shape[1] // heads
    value_size = value_weight.shape[1] // heads
    sizes = (heads, key_size, value_size)
    key_cols, value_cols = heads * key_size, heads * value_size
    micros, own_rows, width = inputs.shape
    rows = cotangent.shape[1]
    seq_size, seq_index = lax.axis_size("seq"), lax.axis_index("seq")
    tp_index = lax.axis_index("tp")
    section = lax.axis_index("section")
    at_start, at_end = seq_index == 0, seq_index == seq_size - 1
    order = (seq_index - jnp.arange(seq_size, dtype=jnp.int32)) % seq_size
    tp_size = lax.axis_size("tp")
    sources = (tp_index - jnp.arange(tp_size, dtype=jnp.int32)) % tp_size
    targets = (tp_index + jnp.arange(tp_size, dtype=jnp.int32)) % tp_size
    last_section = section.astype(jnp.int32).reshape(1)
    groups = 2
    group = micros // groups

    def own(values):
        return lax.dynamic_slice_in_dim(values, tp_index * own_rows, own_rows, 0)

    def whole_out_weight(whole, piece, member, members):
        for step in range(0, seq_size, 2):
            moved = ring(piece, "seq", step) if step else piece
            for at, values in (
                ((seq_index - step) % seq_size, moved),
                (((seq_index ^ 1) - step) % seq_size, crossed(moved, 1)),
            ):
                whole = narrow_into(
                    whole, values, at.astype(jnp.int32).reshape(1), width, member, members, tp_size
                )
                tock([whole])
        return whole

    spare = jnp.zeros((width, 128 - 2 * heads), LOW)
    in_weight = jnp.concatenate(
        [query_weight, key_weight, value_weight, outgate_weight, decay_weight, beta_weight, spare], 1
    )
    conv_cols = 2 * key_cols + value_cols
    offsets = jnp.arange(rows, dtype=jnp.int32)

    def micro_of(step, member):
        return jnp.clip(step - section, 0, groups - 1) * group + member

    def reset_flags(micro):
        starts = micro * (rows * seq_size) + seq_index * rows + offsets
        flags = lax.dynamic_index_in_dim(doc_start, micro, 0, keepdims=False) == starts
        return jnp.broadcast_to(flags.astype(F32)[:, None], (rows, 128))

    def enter_mixer(residual, step, member, border_carry):
        micro = micro_of(step, member)
        hidden, projected = enter(residual, norm_in, in_weight)
        moved = ring(projected[rows - 8 :, :conv_cols], "seq", 1)
        border = jnp.where(at_start, border_carry, moved)
        resets = reset_flags(micro)
        carried, local_out, maps, inverse = mixer_local(
            sizes, projected, resets, border, taps, rate, bias
        )
        saved[step, member] = dict(
            hidden=hidden, border=border, projected=projected, resets=resets, carried=carried,
            maps=all_seq(maps), inverse=inverse,
        )
        return moved, local_out

    def gate(step, member, local_out, state):
        kept = saved[step, member]
        kept["gated"], kept["output"], kept["entry_state"], state = mixer_gate(
            sizes, order, kept["maps"], state, kept["carried"], local_out, kept["projected"], head_norm
        )
        return state

    def rows_outer(name):
        return jnp.concatenate(
            [
                jnp.where(section == 0, saved[0, member][name], saved[2, member][name])
                for member in range(group)
            ],
            0,
        )

    def rows_inner(name):
        return jnp.concatenate([saved[1, member][name] for member in range(group)], 0)

    def rows_of(name):
        return jnp.concatenate([rows_outer(name), rows_inner(name)], 0)

    def rounded(values):
        zero = jnp.zeros((1,), jnp.int32)
        return tock([narrow_into(None, values, zero, width, 0, 1, tp_size)])[0]

    def enter_mixer(residual, step, member, border_carry):
        micro = micro_of(step, member)
        hidden, projected = enter(residual, norm_in, in_weight)
        moved = ring(projected[rows - 8 :, :conv_cols], "seq", 1)
        border = jnp.where(at_start, border_carry, moved)
        resets = reset_flags(micro)
        carried, local_out, maps, inverse = mixer_local(
            sizes, projected, resets, border, taps, rate, bias
        )
        saved[step, member] = dict(
            hidden=hidden, border=border, projected=projected, resets=resets, carried=carried,
            maps=all_seq(maps), inverse=inverse,
        )
        return moved, local_out

    def gate(step, member, local_out, state):
        kept = saved[step, member]
        kept["gated"], kept["output"], kept["entry_state"], state = mixer_gate(
            sizes, order, kept["maps"], state, kept["carried"], local_out, kept["projected"], head_norm
        )
        return state

    def rows_of(name):
        outer = [
            jnp.where(section == 0, saved[0, member][name], saved[2, member][name])
            for member in range(group)
        ]
        return jnp.concatenate(outer + [saved[1, member][name] for member in range(group)], 0)

    saved = {}
    section_rows = {}
    part = width // seq_size
    entering = [inputs[member].astype(F32) * (section == 0) for member in range(group)]
    residuals = [gather_tp(values) for values in entering]
    out_piece = widen(lax.dynamic_slice_in_dim(out_weight, seq_index * part, part, 1))
    out_pieces = [
        gather_tp(after(values, *entering)) for values in jnp.split(out_piece, 2, 0)
    ]
    out_full = None
    border_carry = jnp.zeros((8, conv_cols), F32)
    state = jnp.zeros((heads, key_size, value_size), F32)
    nothing = jnp.zeros((rows, width), F32)
    members = list(reversed(range(group)))
    early, late = members[0], members[-1]
    tops, feed_grads, late_sums = {}, {}, {}

    def feed(back_step, member, received, handed):
        step = groups - back_step
        kept = saved[step, member]
        given = lax.dynamic_index_in_dim(cotangent, micro_of(step, member), 0, keepdims=False)
        if step == 0:
            given = jnp.where(section == 0, given, jnp.zeros_like(given))
        kept["top_low"], kept["gate_low"], kept["up_low"], sums = feed_back(
            last_section, given, handed, kept["gate_act"], kept["up_act"],
            gate_weight, up_weight, down_weight,
        )
        tops[member] = jnp.where(section == 0, received, own(given).astype(F32))
        if step:
            if not back_step and feed_grads:
                sums = after(sums, *feed_grads.values())
            feed_grads[member] = scatter_tp(sums)
        else:
            summed = scatter_tp(jnp.where(section == 0, sums, late_sums[member]))
            section_rows[groups, member] = saved[groups, member]["mixed"] + summed
            feed_grads[member] = jnp.where(section == 0, summed, 0.0)

    for step in range(groups + 1):
        all_gated = []
        for member in range(group):
            border_carry, local_out = enter_mixer(residuals[member], step, member, border_carry)
            state = gate(step, member, local_out, state)
            saved[step, member]["entering"] = entering[member]
            all_gated.append(lax.all_gather(saved[step, member]["gated"], "tp", axis=0))
        if out_full is None:
            for member, piece in enumerate(out_pieces):
                out_full = whole_out_weight(out_full, after(piece, state), member, 2)
        all_sums = []
        for member in range(group):
            kept = saved[step, member]
            mixed, kept["hidden_feed"], kept["gate_act"], kept["up_act"], kept["inner"], sums = join_heads(
                residuals[member], all_gated[member], out_full, norm_feed,
                gate_weight, up_weight, down_weight,
            )
            kept["mixed"] = own(mixed)
            if step < groups:
                all_sums.append(scatter_tp(sums))
            else:
                late_sums[member] = sums
                feed(0, member, jnp.zeros((own_rows, width), F32), nothing)
        if step == groups:
            break
        ready = None
        entering, residuals = [], []
        for member in range(group):
            summed = all_sums[member] if ready is None else after(all_sums[member], ready)
            out_rows = saved[step, member]["mixed"] + summed
            section_rows[step, member] = out_rows
            handed = handed_on(out_rows, "section", 1)
            micro = micro_of(step + 1, member)
            given = lax.dynamic_index_in_dim(inputs, micro, 0, keepdims=False).astype(F32)
            ready = jnp.where(section == 0, given, handed)
            entering.append(ready)
            residuals.append(gather_tp(ready))

    tail_carry = jnp.zeros((8, conv_cols), F32)
    state_grad = jnp.zeros((heads, key_size, value_size), F32)
    in_grads = {}
    norm_in_grad = jnp.zeros((width,), F32)
    norm_feed_grad = jnp.zeros((width,), F32)
    gain_grad = jnp.zeros((value_size,), F32)
    taps_grad = jnp.zeros(taps.shape, F32)
    side_sums = jnp.zeros((8, 128), F32)
    received, handed = [None] * group, [None] * group
    up_sums = up_parts = up_moved = down_parts = down_moved = inner_mixed = outer_mixed = None
    for back_step in range(groups + 1):
        step = groups - back_step
        final = back_step == groups
        if back_step:
            for member in members:
                feed(back_step, member, received[member], handed[member])
        if final:
            feed_all, top_all = rows_of("hidden_feed"), rows_of("top_low")
            gate_sums = CoreSums(feed_all, rows_of("gate_low"), 0).send()
            gate_parts = gate_sums.sums()
            gate_moved = chip_moves(gate_parts)
        all_sums = {}

        def depart(member, tail):
            kept = saved[step, member]
            kept["projected_low"], sums = leave(
                kept["conv_grad"], tail, kept["outgate_low"], kept["side_low"], in_weight
            )
            all_sums[member] = scatter_tp(sums)
            return sums

        def mix(member):
            kept = saved[step, member]
            feed_part, kept["mixed_grad"], *pieces = mix_back(
                targets, feed_grads[member], kept["mixed"], tops[member], norm_feed, out_full
            )
            return feed_part[0], [ring(piece, "tp", at) if at else piece for at, piece in enumerate(pieces)]

        def begin(member):
            nonlocal norm_feed_grad, gain_grad, up_sums, up_parts, down_parts, inner_mixed, outer_mixed
            kept = saved[step, member]
            feed_part, pieces = mix(member)
            norm_feed_grad = norm_feed_grad + feed_part
            if final and member == early:
                up_sums = CoreSums(feed_all, rows_of("up_low"), 0).send()
            elif final:
                inner_mixed = gather_tp(rows_inner("mixed_grad"))
                outer_mixed = gather_tp(rows_outer("mixed_grad"))
            output_grad, kept["outgate_low"], gain_part, entry_grad = mixer_gate_back(
                sizes, sources, pieces, kept["output"], kept["projected"], head_norm, kept["carried"]
            )
            gain_grad = gain_grad + gain_part[0]
            all_entries = all_seq(entry_grad)
            if final and member == early:
                up_sums.left = after(up_sums.left, *gate_moved)
                up_parts = up_sums.sums()
            elif final:
                down_sums = CoreSums(after(rows_of("inner"), *up_moved), top_all, 1).send()
                down_parts = down_sums.sums()
                inner_mixed = rounded(inner_mixed)
            return output_grad, all_entries

        def finish(member, output_grad, all_entries):
            nonlocal state_grad, tail_carry, up_moved, down_moved, taps_grad, side_sums
            kept = saved[step, member]
            kept["conv_grad"], border_grad, taps_part, kept["side_low"], sums_part, state_grad = mixer_local_back(
                sizes, order, kept["maps"], all_entries, state_grad, kept["projected"],
                kept["resets"], kept["border"], taps, rate, bias, kept["inverse"],
                kept["entry_state"], output_grad,
            )
            moved = ring(border_grad, "seq", -1)
            tail = jnp.where(at_end, tail_carry, moved)
            tail_carry = moved
            if final and member == early:
                up_moved = chip_moves(after_all(up_parts, tail))
            elif final:
                down_moved = chip_moves(after_all(down_parts, tail))
                tail = after(tail, all_sums[early])
            taps_grad = taps_grad + taps_part
            side_sums = side_sums + sums_part
            return tail

        if back_step:
            for member in members:
                last = depart(member, finish(member, *begin(member)))
        else:
            begun = {member: begin(member) for member in range(group)}
            for member in members:
                last = depart(member, finish(member, *begun[member]))
        ready = None
        received, handed = [None] * group, [None] * group
        if final:
            in_sums = CoreSums(rows_of("hidden"), rows_of("projected_low"), 0).send()
            in_parts = in_sums.sums(*down_moved)
            in_moved = chip_moves(in_parts)
            outer_mixed = rounded(after(outer_mixed, *in_moved))
            ready = outer_mixed
        for member in members:
            kept = saved[step, member]
            summed = all_sums[member]
            if ready is not None and (not final or member == late):
                summed = after(summed, ready)
            entering_back, in_part = row_norm_back(kept["entering"], norm_in[0], summed)
            norm_in_grad = norm_in_grad + in_part
            own_grad = kept["mixed_grad"] + entering_back
            in_grads[step, member] = own_grad
            if not final:
                ready = handed_on(own_grad, "section", -1)
                received[member] = ready
                handed[member] = gather_tp(ready)
    def of_section(values):
        return [
            jnp.where(section == 0, values[at, member], values[at + 1, member])
            for at in range(groups)
            for member in range(group)
        ]

    def by_device(values):
        split = values.astype(LOW).reshape(-1, tp_size, own_rows, value_cols)
        return jnp.moveaxis(split, 0, 1).reshape(-1, value_cols)

    out_sums = CoreSums(
        jnp.concatenate([by_device(rows_outer("gated")), by_device(rows_inner("gated"))], 0),
        jnp.concatenate([outer_mixed, inner_mixed], 0),
        1,
    )
    out_parts = out_sums.send().sums()
    grad_out = total(out_parts, chip_moves(out_parts))
    grad_gate, grad_up, grad_in, grad_down = [
        total(after_all(parts, out_parts[-1]), moved)
        for parts, moved in (
            (gate_parts, gate_moved), (up_parts, up_moved), (in_parts, in_moved),
            (down_parts, down_moved),
        )
    ]

    shared = butterfly(jnp.concatenate([norm_in_grad, norm_feed_grad, gain_grad]), "tp")
    small = butterfly(
        jnp.concatenate(
            [
                after(shared, out_parts[0]), taps_grad.reshape(-1), side_sums[0, :heads],
                side_sums[1, :heads],
            ]
        ),
        "seq",
    )
    bounds = [0, width, 2 * width, 2 * width + value_size]
    bounds += [bounds[-1] + taps.size, bounds[-1] + taps.size + heads, bounds[-1] + taps.size + 2 * heads]
    norm_in_grad, norm_feed_grad, gain_grad, taps_grad, log_grad, bias_grad = [
        small[low:high] for low, high in zip(bounds[:-1], bounds[1:])
    ]
    taps_grad = taps_grad.reshape(taps.shape)
    bounds = [
        0, key_cols, 2 * key_cols, conv_cols, conv_cols + value_cols, conv_cols + value_cols + heads,
        conv_cols + value_cols + 2 * heads,
    ]
    in_parts = [grad_in[:, low:high] for low, high in zip(bounds[:-1], bounds[1:])]
    return (
        jnp.stack(of_section(section_rows))[None],
        jnp.stack(of_section(in_grads))[None],
        norm_in_grad[None],
        *[member[None] for member in in_parts],
        taps_grad[None, :, :key_cols],
        taps_grad[None, :, key_cols : 2 * key_cols],
        taps_grad[None, :, 2 * key_cols :],
        log_grad[None],
        bias_grad[None],
        gain_grad[None],
        grad_out[None],
        norm_feed_grad[None],
        grad_gate[None],
        grad_up[None],
        grad_down[None],
    )


def solution(mesh):
    by_column, by_row = P("section", None, "tp"), P("section", "tp", None)
    placed = (
        P(None, ("seq", "tp"), None),
        P(None, "seq", None),
        P(None, "seq"),
        P("section", None),
        *[by_column] * 9,
        P("section", "tp"),
        P("section", "tp"),
        P("section", None),
        by_row,
        P("section", None),
        by_column,
        by_column,
        by_row,
    )
    rows_out = P("section", None, ("seq", "tp"), None)
    both = P("section", "seq", "tp")
    return jax.shard_map(
        local,
        mesh=mesh,
        in_specs=placed,
        out_specs=(
            rows_out,
            rows_out,
            P("section", None),
            *[both] * 6,
            *[by_column] * 3,
            P("section", "tp"),
            P("section", "tp"),
            P("section", None),
            P("section", "tp", "seq"),
            P("section", None),
            both,
            both,
            P("section", "tp", "seq"),
        ),
        check_vma=False,
    )
```
